256 devices in a mesh: dp: 16 (over x_lo, z), ctx: 16 (over y, x_hi, core).
Axes of the slice: x: 4 (x_hi: 2, x_lo: 2; x = x_hi * 2 + x_lo), y: 4, z: 8, core: 2. Of those that a mesh axis runs over, the one named last changes fastest.
Arguments:
- hidden: bfloat16 [16, 2048, 4096], P('dp', 'ctx'), may hold values from -6 to 6
- value_weight: bfloat16 [4096, 512], P(('dp', 'ctx')), may hold values from -0.09375 to 0.09375
- queries: bfloat16 [16, 2048, 4096], P('dp', 'ctx'), may hold values from -4.5 to 4.5
- key_rows: bfloat16 [16, 2048, 512], P('dp', 'ctx'), may hold values from -4.5 to 4.5
- attn_saved: bfloat16 [16, 2048, 4096], P('dp', 'ctx'), may hold values from -3 to 3
- grad_out: bfloat16 [16, 2048, 4096], P('dp', 'ctx'), may hold values from -6 to 6
- doc_lengths: int32 [16, 8], P('dp'), may hold values from 1 to 1024, 2048 in all within a row
- routing: int32 [16, 2048], P('dp'), may hold values from 0 to 2047, as said below
- visible_blocks: int32 [16, 32, 32], P('dp'), may hold values from 0 to 1, as said below
Outputs:
- grad_query: bfloat16 [16, 2048, 4096], P('dp', 'ctx')
- grad_key: bfloat16 [16, 2048, 512], P('dp', 'ctx')
- grad_value_weight: float32 [4096, 512], P(('dp', 'ctx'))
The draws below stay inside these ranges and needn't reach their ends.
Inputs may be any that keep to these rules, and one draw needn't show every extreme that they name: For each pack, routing is a permutation: the token at position i, held by device i // 128 of ctx, goes to owner slot routing[i], held by device routing[i] // 128 of ctx, so every owner device receives 128 tokens. At most 16 tokens of one device go to one owner device, and this bound is reached in every draw. visible_blocks[b, b] = 1 for every block b. `doc_lengths`: each pack's lengths sum to 2048; the longest is 1024.
All inputs are finite; a program needn't handle non-finite values.
Results may differ from the reference program's by a relative error of at most 0.023.
Values may be sent and summed in bfloat16 or wider, within the bound.
A program may use at most 128 MiB of HBM per device.

```python
import math
import jax
import jax.numpy as jnp
import numpy as np
from jax import lax

D = 4096
QH = 32
KVH = 4
HD = 128
VB = 64
TOK_DEV = 128
NDOC = 8
TOKENS = 2048
PACKS = 16
NB = 32
MOST = 1024


def draw_queries(key, part):
    key = jax.random.fold_in(key, 3)
    first_key = jax.random.fold_in(key, 0)
    array_shape = (PACKS, TOKENS, QH * HD)
    values = jnp.clip(jax.random.normal(first_key, array_shape, jnp.float32), -4.5, 4.5)
    return values.astype(jnp.bfloat16)


def draw_key_rows(key, part):
    key = jax.random.fold_in(key, 4)
    first_key = jax.random.fold_in(key, 0)
    array_shape = (PACKS, TOKENS, KVH * HD)
    values = jnp.clip(jax.random.normal(first_key, array_shape, jnp.float32), -4.5, 4.5)
    return values.astype(jnp.bfloat16)


def routing_one(key):
    key_offsets, key_rowperm, key_slots = jax.random.split(key, 3)
    device_count = TOKENS // TOK_DEV
    capacity = 2 * TOK_DEV // device_count
    big_count = device_count // 2 - 1
    offsets = jax.random.permutation(key_offsets, device_count).astype(jnp.int32)
    row_iota = jnp.arange(TOK_DEV, dtype=jnp.int32)
    segment = jnp.where(row_iota < big_count * capacity, row_iota // capacity, big_count + (row_iota - big_count * capacity) // (capacity // 2))
    loaders = jnp.arange(device_count, dtype=jnp.int32)
    owners = (loaders[:, None] + offsets[segment][None, :]) % device_count

    def shuffle(sub_key):
        return jax.random.permutation(sub_key, TOK_DEV).astype(jnp.int32)
    row_perm = jax.vmap(shuffle)(jax.random.split(key_rowperm, device_count))
    slot_perm = jax.vmap(shuffle)(jax.random.split(key_slots, device_count))
    destination = owners * TOK_DEV + slot_perm[owners, row_iota[None, :]]
    result = jnp.zeros((device_count, TOK_DEV), jnp.int32).at[loaders[:, None], row_perm].set(destination)
    return result.reshape(TOKENS)


def draw_routing(key, part):
    key = jax.random.fold_in(key, 5)
    return jax.vmap(routing_one)(jax.random.split(key, PACKS)).astype(jnp.int32)


def draw_visible_blocks(key, part):
    key = jax.random.fold_in(key, 7)
    coins = jax.random.randint(key, (PACKS, NB, NB), 0, 4)
    block_iota = jnp.arange(NB, dtype=jnp.int32)
    diagonal = block_iota[:, None] == block_iota[None, :]
    return jnp.where(diagonal[None] | (coins > 0), 1, 0).astype(jnp.int32)


def with_spikes(drawn, key, source, target, blocks, factor):
    owner, partner = [(jnp.arange(drawn.shape[axis_at]) // (drawn.shape[axis_at] // blocks)).reshape([-1 if axis == axis_at else 1 for axis in range(drawn.ndim)]) for axis_at in (source, target)]
    chosen = jax.random.permutation(key, blocks)[partner]
    strong = (owner == chosen) | (owner == (partner + blocks // 2) % blocks)
    return jnp.where(strong, factor * drawn, drawn)


def level_of(stream_key, shape, pieces, low, high):
    loudness = 1.0
    for position, parts in pieces:
        draws = jax.random.uniform(jax.random.fold_in(jax.random.fold_in(stream_key, 6), position), (parts,), jnp.float32, low / len(pieces), high / len(pieces))
        loudness = loudness * jnp.repeat(jnp.exp(draws), shape[position] // parts).reshape((-1,) + (1,) * (len(shape) - 1 - position))
    return loudness


def length_profile(amount, total, reach, lean):
    weights = [(1 << 20) // math.isqrt(rank ** lean) + 1 for rank in range(2, amount + 1)]
    surplus, counts = total - reach - (amount - 1), [1] * (amount - 1)
    while surplus > 0:
        candidates = [i for i in range(amount - 1) if counts[i] < reach]
        pool, remaining = sum([weights[i] for i in candidates]), surplus
        for i in candidates:
            more = min(reach - counts[i], max(1, remaining * weights[i] // pool), surplus)
            counts[i] = counts[i] + more
            surplus = surplus - more
    return np.array([reach] + counts)


def ragged_sizes(stream_key, number_of, total, bound, skew):
    if number_of == 2:
        one = jax.random.randint(stream_key, (), max(1, total - bound), min(bound, total - 1) + 1)
        return jnp.stack([one, total - one])
    sizes = jnp.asarray(length_profile(number_of, total, bound, skew), jnp.int32)
    pairs = (number_of - 1) // 2
    donor, receiver = sizes[1:1 + 2 * pairs:2], sizes[2:2 + 2 * pairs:2]
    margin = jnp.minimum(donor - 1, bound - receiver)
    passed = jax.random.randint(jax.random.fold_in(stream_key, 1), (pairs,), 0, 1 << 20) % (margin + 1)
    sizes = sizes.at[1:1 + 2 * pairs:2].set(donor - passed).at[2:2 + 2 * pairs:2].set(receiver + passed)
    return sizes[jax.random.permutation(jax.random.fold_in(stream_key, 2), number_of)]


def normal_values(own_key, dims, width, reach, cuts=(), kind=jnp.bfloat16):
    array = jax.random.normal(own_key, dims, jnp.float32) * width
    if len(cuts) > 0:
        array = level_of(own_key, dims, cuts, -0.22, 0.18) * array
    return jnp.clip(array, min=-reach, max=reach).astype(kind)


def gaussian_with(key, dims, width, reach, cuts, heavy, kind=jnp.bfloat16):
    entries = width * jax.random.normal(key, dims, jnp.float32)
    if cuts:
        entries = entries * level_of(key, dims, cuts, -0.22, 0.18)
    return jnp.clip(with_spikes(entries, jax.random.fold_in(key, 3), *heavy), -reach, reach).astype(kind)


def setup_inputs(seed: int = 0) -> dict:
    keys = jax.random.split(jax.random.key(seed), 10)
    hidden = gaussian_with(keys[0], (PACKS, TOKENS, D), 1.0, 6.0, ((0, 16), (1, 16)), (1, 2, 16, 2.0))
    value_weight = normal_values(keys[1], (D, KVH * HD), D ** -0.5, 0.09375, ((0, 256),))
    queries = draw_queries(jax.random.fold_in(keys[9], 71), 0)
    key_rows = draw_key_rows(jax.random.fold_in(keys[9], 71), 0)
    attn_saved = normal_values(keys[4], (PACKS, TOKENS, QH * HD), 0.5, 3.0, ((0, 16), (1, 16)))
    grad_out = normal_values(keys[5], (PACKS, TOKENS, QH * HD), 1.0, 6.0, ((0, 16), (1, 16)))
    doc_lengths = jax.vmap(lambda own: ragged_sizes(own, NDOC, TOKENS, MOST, 2))(jax.random.split(keys[6], PACKS)).reshape((PACKS, NDOC)).astype(jnp.int32)
    routing = draw_routing(jax.random.fold_in(keys[9], 71), 0)
    visible_blocks = draw_visible_blocks(jax.random.fold_in(keys[9], 71), 0)
    return dict(hidden=hidden, value_weight=value_weight, queries=queries, key_rows=key_rows, attn_saved=attn_saved, grad_out=grad_out, doc_lengths=doc_lengths, routing=routing, visible_blocks=visible_blocks)


def document_index(positions, doc_lengths):
    doc_ends = jnp.cumsum(doc_lengths).astype(jnp.int32)
    return lax.optimization_barrier(jnp.sum((positions[:, None] >= doc_ends[None, :]).astype(jnp.int32), axis=1))

def reference(hidden, value_weight, queries, key_rows, attn_saved, grad_out, doc_lengths, routing, visible_blocks):
    score_scale = 1.0 / math.sqrt(HD)
    group_size = QH // KVH

    def one_pack(packed):
        pack_hidden, pack_query, pack_keys, pack_saved, pack_grad, pack_lengths, pack_route, pack_blocks = packed
        value_rows = jnp.dot(pack_hidden, value_weight, preferred_element_type=jnp.float32).astype(jnp.bfloat16)
        token_iota = jnp.arange(TOKENS, dtype=jnp.int32)
        slot_position = jnp.zeros((TOKENS,), jnp.int32).at[pack_route.astype(jnp.int32)].set(token_iota)
        query_docs = document_index(slot_position, pack_lengths)
        key_docs = document_index(token_iota, pack_lengths)
        visible = pack_blocks[slot_position // VB][:, token_iota // VB]
        allowed = (query_docs[:, None] == key_docs[None, :]) & (token_iota[None, :] <= slot_position[:, None]) & (visible == 1)
        owner_query = pack_query[slot_position].astype(jnp.float32).reshape(TOKENS, KVH, group_size, HD)
        owner_grad = pack_grad[slot_position].astype(jnp.float32).reshape(TOKENS, KVH, group_size, HD)
        saved_out = pack_saved.astype(jnp.float32).reshape(TOKENS, KVH, group_size, HD)
        row_delta = lax.optimization_barrier(jnp.sum(owner_grad * saved_out, axis=-1))
        keys_float = pack_keys.astype(jnp.float32).reshape(TOKENS, KVH, HD)
        values_float = value_rows.astype(jnp.float32).reshape(TOKENS, KVH, HD)
        query_parts = []
        key_parts = []
        value_parts = []
        for kv_head in range(KVH):
            head_query = owner_query[:, kv_head]
            head_grad = owner_grad[:, kv_head]
            scores = jnp.einsum('jhd,pd->hjp', head_query, keys_float[:, kv_head]) * score_scale
            masked = jnp.where(allowed[None], scores, -jnp.inf)
            row_top = lax.optimization_barrier(jnp.max(masked, axis=-1, keepdims=True))
            log_total = row_top + jnp.log(lax.optimization_barrier(jnp.sum(jnp.exp(masked - row_top), axis=-1, keepdims=True)))
            weights = jnp.exp(masked - log_total)
            weights_b = lax.optimization_barrier(weights.astype(jnp.bfloat16)).astype(jnp.float32)
            dweights = jnp.einsum('jhd,pd->hjp', head_grad, values_float[:, kv_head])
            dweights = lax.optimization_barrier(dweights.astype(jnp.bfloat16)).astype(jnp.float32)
            dscores = (score_scale * weights * (dweights - row_delta[:, kv_head].T[:, :, None])).astype(jnp.bfloat16)
            dscores_float = lax.optimization_barrier(dscores).astype(jnp.float32)
            query_parts.append(jnp.einsum('hjp,pd->jhd', dscores_float, keys_float[:, kv_head]))
            key_parts.append(jnp.einsum('hjp,jhd->pd', dscores_float, head_query))
            value_parts.append(jnp.einsum('hjp,jhd->pd', weights_b, head_grad))
        grad_query = jnp.stack(query_parts, axis=1).reshape(TOKENS, QH * HD).astype(jnp.bfloat16)
        grad_key = jnp.stack(key_parts, axis=1).reshape(TOKENS, KVH * HD).astype(jnp.bfloat16)
        grad_value = jnp.stack(value_parts, axis=1).reshape(TOKENS, KVH * HD).astype(jnp.bfloat16)
        weight_part = jnp.dot(pack_hidden.T, grad_value, preferred_element_type=jnp.float32)
        return (grad_query, grad_key, weight_part)
    grad_query, grad_key, weight_parts = lax.map(one_pack, (hidden, queries, key_rows, attn_saved, grad_out, doc_lengths, routing, visible_blocks))
    grad_value_weight = lax.optimization_barrier(jnp.sum(weight_parts, axis=0)) / math.sqrt(PACKS * TOKENS)
    return (grad_query, grad_key, grad_value_weight)
```

```python
import math

import jax
import jax.numpy as jnp
from jax import lax
from jax.experimental import pallas as pl
from jax.experimental.pallas import tpu as pltpu
from jax.sharding import PartitionSpec as P

HD = 128
VB = 64
ROWS = 128
CTX = 16
CAP = 16
SLOTS = CTX * CAP
GROUP = 8
KVH = 4
Z = 8
D = 4096
KVW = 512
WIN = 1280
USED = 1152
BACK = 4
CHUNK = 256
BF = jnp.bfloat16
F32 = jnp.float32
NT = (((1,), (1,)), ((), ()))
TN = (((0,), (0,)), ((), ()))
SCALE = 1.0 / math.sqrt(HD)


def remote(source, target, send_sem, recv_sem, dp, ctx):
    return pltpu.make_async_remote_copy(
        src_ref=source,
        dst_ref=target,
        send_sem=send_sem,
        recv_sem=recv_sem,
        device_id=(dp, ctx),
        device_id_type=pl.DeviceIdType.MESH,
    )


def rows_at(start, size):
    return pl.ds(pl.multiple_of(start, size), size)


def iota(shape, axis):
    return lax.broadcasted_iota(jnp.int32, shape, axis)


def nt_dot(first, second):
    return lax.dot_general(first, second, NT, preferred_element_type=F32)


def tn_dot(first, second):
    return lax.dot_general(first, second, TN, preferred_element_type=F32)


class Window:
    def __init__(self, own, window, far_send, far_recv, near_send, near_recv, own_sem, dp, ctx):
        self.own, self.window = own, window
        self.far_send, self.far_recv = far_send, far_recv
        self.near_send, self.near_recv = near_send, near_recv
        self.own_sem, self.dp, self.ctx = own_sem, dp, ctx
        self.chip, self.core = ctx // 2, ctx % 2
        self.other = ctx + 1 - 2 * self.core

    def slot(self, back, core):
        return self.window.at[rows_at((8 - 2 * back + core) * ROWS, ROWS)]

    def far(self, back):
        return remote(
            self.own,
            self.slot(back, self.core),
            self.far_send.at[back],
            self.far_recv.at[back],
            self.dp,
            self.ctx + 2 * back,
        )

    def near(self, back, core):
        source = self.own if back == 0 else self.slot(back, core)
        return remote(
            source,
            self.slot(back, core),
            self.near_send.at[back],
            self.near_recv.at[back],
            self.dp,
            self.other,
        )

    def own_copy(self):
        return pltpu.make_async_copy(self.own, self.slot(0, self.core), self.own_sem)

    def start(self):
        for back in range(1, BACK + 1):

            @pl.when(self.chip + back <= 7)
            def _(back=back):
                self.far(back).start()

        self.near(0, self.core).start()
        self.own_copy().start()

    def hand_on(self):
        for back in range(1, BACK + 1):

            @pl.when(self.chip >= back)
            def _(back=back):
                self.far(back).wait_recv()
                self.near(back, self.core).start()

    def finish(self):
        for back in range(BACK + 1):

            @pl.when(self.chip >= back)
            def _(back=back):
                self.near(back, 1 - self.core).wait_recv()
                self.near(back, self.core).wait_send()

        for back in range(1, BACK + 1):

            @pl.when(self.chip + back <= 7)
            def _(back=back):
                self.far(back).wait_send()

        self.own_copy().wait()


class Exchange:
    def __init__(self, source, arrived, send_sem, recv_sem, own_sem, dp, ctx):
        self.source, self.arrived = source, arrived
        self.send_sem, self.recv_sem = send_sem, recv_sem
        self.own_sem, self.dp, self.ctx = own_sem, dp, ctx

    def copy(self, step):
        partner = (self.ctx + step) % CTX
        return remote(
            self.source.at[rows_at(partner * CAP, CAP)],
            self.arrived.at[rows_at(self.ctx * CAP, CAP)],
            self.send_sem.at[step],
            self.recv_sem.at[step],
            self.dp,
            partner,
        )

    def own_copy(self):
        own = rows_at(self.ctx * CAP, CAP)
        return pltpu.make_async_copy(self.source.at[own], self.arrived.at[own], self.own_sem)

    def start(self):
        @pl.loop(1, CTX)
        def _(step):
            self.copy(step).start()

        self.own_copy().start()

    def finish(self):
        @pl.loop(1, CTX)
        def _(step):
            self.copy(step).wait()

        self.own_copy().wait()


def plane_partner(dp, ctx, step):
    chip = ((dp // Z) * 8 + ctx // 2 + step) % 16
    return (chip // 8) * Z + dp % Z, (chip % 8) * 2 + dp // Z


def gather_kernel(
    weight_ref,
    hidden_ref,
    key_ref,
    saved_ref,
    route_ref,
    key_window,
    value_window,
    saved_slots,
    owner_ref,
    pack_ref,
    whole,
    staged,
    value_own,
    empty,
    plane_send,
    plane_recv,
    up_send,
    up_recv,
    down_send,
    down_recv,
    pair_send,
    pair_recv,
    far_send,
    far_recv,
    near_send,
    near_recv,
    slot_send,
    slot_recv,
    own_sems,
):
    dp, ctx = lax.axis_index("dp"), lax.axis_index("ctx")
    x_lo, z = dp // Z, dp % Z
    chip, core = ctx // 2, ctx % 2
    other = ctx + 1 - 2 * core

    shard = whole.at[rows_at((dp * CTX + ctx) * CAP, CAP)]

    def plane_copy(step):
        to_dp, to_ctx = plane_partner(dp, ctx, step)
        return remote(
            weight_ref, shard, plane_send.at[step], plane_recv.at[ctx], to_dp, to_ctx
        )

    own_shard = pltpu.make_async_copy(weight_ref, shard, own_sems.at[3])

    @pl.when(core == x_lo)
    def _():
        own_shard.start()

    @pl.when(core != x_lo)
    def _():
        plane_copy(0).start()

    @pl.loop(1, 16)
    def _(step):
        plane_copy(step).start()

    keys = Window(
        key_ref,
        key_window,
        far_send.at[0],
        far_recv.at[0],
        near_send.at[0],
        near_recv.at[0],
        own_sems.at[0],
        dp,
        ctx,
    )
    values = Window(
        value_own,
        value_window,
        far_send.at[1],
        far_recv.at[1],
        near_send.at[1],
        near_recv.at[1],
        own_sems.at[1],
        dp,
        ctx,
    )
    keys.start()

    route = route_ref[...]
    owner = lax.shift_right_logical(route, 7)
    before = jnp.where(iota((ROWS, ROWS), 0) < iota((ROWS, ROWS), 1), 1.0, 0.0).astype(BF)
    coming = owner == ctx
    rank = jnp.dot(jnp.where(coming, 1.0, 0.0).astype(BF), before, preferred_element_type=F32)
    rank = jnp.where(coming, rank.astype(jnp.int32), -1)
    place = route - ctx * ROWS
    for pack in range(CTX):
        to_rank = jnp.where(rank[pack : pack + 1] == iota((CAP, ROWS), 0), 1.0, 0.0).astype(BF)
        to_place = jnp.where(place[pack : pack + 1] == iota((ROWS, ROWS), 0), 1.0, 0.0).astype(BF)
        owner_ref[pack * CAP : (pack + 1) * CAP] = nt_dot(to_rank, to_place).astype(BF)
    for part in range(4):
        columns = slice(part * 1024, (part + 1) * 1024)
        staged[:, columns] = jnp.dot(
            owner_ref[...], saved_ref[:, columns], preferred_element_type=F32
        ).astype(BF)
    saved_exchange = Exchange(staged, saved_slots, slot_send, slot_recv, own_sems.at[2], dp, ctx)
    saved_exchange.start()

    own_owner = lax.shift_right_logical(route_ref[pl.ds(ctx, 1)], 7)
    hit = own_owner == iota((CTX, ROWS), 0)
    count = jnp.dot(jnp.where(hit, 1.0, 0.0).astype(BF), before, preferred_element_type=F32)
    own_rank = jnp.sum(jnp.where(hit, count, 0.0), axis=0, keepdims=True).astype(jnp.int32)
    pack_ref[...] = jnp.where(
        own_owner * CAP + own_rank == iota((SLOTS, ROWS), 0), 1.0, 0.0
    ).astype(BF)

    empty[...] = jnp.zeros_like(empty)
    for back in range(1, BACK + 1):

        @pl.when(chip < back)
        def _(back=back):
            hole = pl.ds((8 - 2 * back) * ROWS, 2 * ROWS)
            pltpu.sync_copy(empty, key_window.at[hole])
            pltpu.sync_copy(empty, value_window.at[hole])

    @pl.when(core == x_lo)
    def _():
        own_shard.wait()

    @pl.loop(0, CTX)
    def _(source):
        @pl.when(jnp.logical_or(core != x_lo, source != ctx))
        def _():
            shard_in = whole.at[rows_at(((core * Z + z) * CTX + source) * CAP, CAP)]
            remote(
                weight_ref, shard_in, plane_send.at[0], plane_recv.at[source], dp, other
            ).wait_recv()

    def chunk(at_core, at_z, half):
        start = (at_core * Z + at_z) * CHUNK
        if half is None:
            return whole.at[rows_at(start, CHUNK)]
        return whole.at[rows_at(start + half * (CHUNK // 2), CHUNK // 2)]

    def up(step, half=None):
        block = chunk(core, (z + Z - step) % Z, half)
        return remote(block, block, up_send.at[step], up_recv.at[step], x_lo * Z + (z + 1) % Z, ctx)

    def down(step, half=None):
        block = chunk(core, (z + step) % Z, half)
        return remote(
            block, block, down_send.at[step], down_recv.at[step], x_lo * Z + (z + Z - 1) % Z, ctx
        )

    def up_in(step, half=None):
        block = chunk(core, (z + Z - step - 1) % Z, half)
        return remote(
            block, block, up_send.at[step], up_recv.at[step], x_lo * Z + (z + 1) % Z, ctx
        )

    def down_in(step, half=None):
        block = chunk(core, (z + step + 1) % Z, half)
        return remote(
            block, block, down_send.at[step], down_recv.at[step], x_lo * Z + (z + Z - 1) % Z, ctx
        )

    def pair(index, at_core):
        offset, half = ((0, None), (-1, None), (1, None), (-2, None), (2, None), (-3, None), (3, None), (4, 0), (4, 1))[index]
        block = chunk(at_core, (z + Z + offset) % Z, half)
        return remote(block, block, pair_send.at[index], pair_recv.at[index], dp, other)

    up(0).start()
    down(0).start()
    pair(0, core).start()
    keys.hand_on()
    for step in range(3):
        up_in(step).wait_recv()
        if step < 2:
            up(step + 1).start()
        else:
            up(3, 0).start()
        pair(2 * step + 1, core).start()
        down_in(step).wait_recv()
        if step < 2:
            down(step + 1).start()
        else:
            down(3, 1).start()
        pair(2 * step + 2, core).start()
    up_in(3, 0).wait_recv()
    pair(7, core).start()
    down_in(3, 1).wait_recv()
    pair(8, core).start()
    for index in range(9):
        pair(index, 1 - core).wait_recv()
    value_own[...] = jnp.dot(hidden_ref[...], whole[...], preferred_element_type=F32).astype(BF)
    values.start()
    values.hand_on()

    for step in range(3):
        up(step).wait_send()
        down(step).wait_send()
    up(3, 0).wait_send()
    down(3, 1).wait_send()
    for index in range(9):
        pair(index, core).wait_send()

    @pl.when(core != x_lo)
    def _():
        plane_copy(0).wait_send()

    @pl.loop(1, 16)
    def _(step):
        plane_copy(step).wait_send()

    keys.finish()
    values.finish()
    saved_exchange.finish()


def gather(weight, hidden, keys, saved, route):
    vmem = pl.BlockSpec(memory_space=pltpu.VMEM)
    hbm = pl.BlockSpec(memory_space=pl.ANY)
    dma = pltpu.SemaphoreType.DMA
    return pl.pallas_call(
        gather_kernel,
        out_shape=(
            jax.ShapeDtypeStruct((WIN, KVW), BF),
            jax.ShapeDtypeStruct((WIN, KVW), BF),
            jax.ShapeDtypeStruct((SLOTS, D), BF),
            jax.ShapeDtypeStruct((SLOTS, ROWS), BF),
            jax.ShapeDtypeStruct((SLOTS, ROWS), BF),
        ),
        in_specs=[vmem] * 5,
        out_specs=(hbm, hbm, hbm, vmem, vmem),
        scratch_shapes=[
            pltpu.VMEM((D, KVW), BF),
            pltpu.VMEM((SLOTS, D), BF),
            pltpu.VMEM((ROWS, KVW), BF),
            pltpu.VMEM((2 * ROWS, KVW), BF),
            dma((16,)),
            dma((16,)),
            dma((4,)),
            dma((4,)),
            dma((4,)),
            dma((4,)),
            dma((9,)),
            dma((9,)),
            dma((2, BACK + 1)),
            dma((2, BACK + 1)),
            dma((2, BACK + 1)),
            dma((2, BACK + 1)),
            dma((CTX,)),
            dma((CTX,)),
            dma((4,)),
        ],
        compiler_params=pltpu.CompilerParams(
            has_side_effects=True, vmem_limit_bytes=40 * 1024 * 1024
        ),
        name="gather_inputs",
    )(weight, hidden, keys, saved, route)


def attention_kernel(
    length_ref,
    visible_ref,
    query_ref,
    grad_ref,
    saved_ref,
    key_ref,
    value_ref,
    pack_ref,
    staged_ref,
    terms_ref,
    bias,
    queries,
    grads,
    weights_all,
    dscores_all,
):
    ctx = lax.axis_index("ctx")
    core = ctx % 2

    @pl.when(pl.program_id(0) == 0)
    def _():
        position = ctx * ROWS + iota((1, ROWS), 1)
        start = jnp.zeros((1, ROWS), jnp.int32)
        end = jnp.int32(0)
        for n in range(8):
            length = length_ref[0, n]
            end = end + length
            start = start + jnp.where(position >= end, length, 0)
        left = iota((1, ROWS), 1) < VB
        for block in range(USED // VB):
            column = jnp.maximum(2 * ctx - 16 + block, 0)
            seen = jnp.where(left, visible_ref[2 * ctx, column], visible_ref[2 * ctx + 1, column])
            key_position = ctx * ROWS - 1024 + block * VB + iota((VB, ROWS), 0)
            allowed = (key_position >= start) & (key_position <= position) & (seen == 1)
            bias[block * VB : (block + 1) * VB] = jnp.where(allowed, 0.0, -1e30)

    for head in range(GROUP):
        columns = slice(head * HD, (head + 1) * HD)
        queries[columns] = query_ref[:, columns]
        grads[columns] = grad_ref[:, columns]
    product = tn_dot(pack_ref[...], saved_ref[...]) * grad_ref[...].astype(F32)
    high = product.astype(BF)
    low = (product - high.astype(F32)).astype(BF)
    heads = jnp.where(
        lax.shift_right_logical(iota((GROUP, GROUP * HD), 1), 7) == iota((GROUP, GROUP * HD), 0),
        1.0,
        0.0,
    ).astype(BF)
    delta = nt_dot(heads, high) + nt_dot(heads, low)
    used = pl.ds(pl.multiple_of(core * ROWS, ROWS), USED)
    keys = key_ref[used]
    values = value_ref[used]
    mask = bias[...]
    for head in range(GROUP):
        columns = slice(head * HD, (head + 1) * HD)
        scores = nt_dot(keys, queries[columns]) + mask
        top = jnp.max(scores, axis=0, keepdims=True)
        raised = jnp.exp((scores - top) * SCALE)
        weights = raised * (1.0 / jnp.sum(raised, axis=0, keepdims=True))
        weights_all[:, columns] = weights.astype(BF)
        dweights = nt_dot(values, grads[columns]).astype(BF).astype(F32)
        dscores_all[:, columns] = (
            (weights * SCALE) * (dweights - delta[head : head + 1])
        ).astype(BF)
    unused = pl.ds(pl.multiple_of((1 - core) * USED, ROWS), ROWS)
    terms_ref[unused] = jnp.zeros((ROWS, 2 * HD), BF)
    terms_ref[used, :HD] = jnp.dot(
        dscores_all[...], queries[...], preferred_element_type=F32
    ).astype(BF)
    terms_ref[used, HD:] = jnp.dot(
        weights_all[...], grads[...], preferred_element_type=F32
    ).astype(BF)
    query_grad = tn_dot(keys, dscores_all[...]).astype(BF)
    for head in range(GROUP):
        columns = slice(head * HD, (head + 1) * HD)
        staged_ref[:, columns] = nt_dot(pack_ref[...], query_grad[:, columns]).astype(BF)


def attention(lengths, visible, queries, grads, saved_slots, key_window, value_window, pack):
    smem = pl.BlockSpec(memory_space=pltpu.SMEM)
    width = GROUP * HD

    def by_group(rows, columns):
        return pl.BlockSpec((rows, columns), lambda g: (0, g))

    return pl.pallas_call(
        attention_kernel,
        grid=(KVH,),
        out_shape=(
            jax.ShapeDtypeStruct((SLOTS, D), BF),
            jax.ShapeDtypeStruct((WIN, 2 * KVW), BF),
        ),
        in_specs=[
            smem,
            smem,
            by_group(ROWS, width),
            by_group(ROWS, width),
            by_group(SLOTS, width),
            by_group(WIN, HD),
            by_group(WIN, HD),
            pl.BlockSpec((SLOTS, ROWS), lambda g: (0, 0)),
        ],
        out_specs=(by_group(SLOTS, width), by_group(WIN, 2 * HD)),
        scratch_shapes=[
            pltpu.VMEM((USED, ROWS), F32),
            pltpu.VMEM((GROUP * HD, HD), BF),
            pltpu.VMEM((GROUP * HD, HD), BF),
            pltpu.VMEM((USED, GROUP * HD), BF),
            pltpu.VMEM((USED, GROUP * HD), BF),
        ],
        compiler_params=pltpu.CompilerParams(vmem_limit_bytes=48 * 1024 * 1024),
        name="attention_backward",
    )(lengths, visible, queries, grads, saved_slots, key_window, value_window, pack)


def reduce_kernel(
    terms_ref,
    staged_ref,
    hidden_ref,
    owner_ref,
    query_grad_ref,
    key_grad_ref,
    weight_grad_ref,
    near_in,
    far_out,
    far_in,
    total,
    value_grad,
    query_slots,
    mine,
    theirs,
    from_pair,
    up_in,
    down_in,
    up_out,
    down_out,
    plane_in,
    near_send,
    near_recv,
    far_send,
    far_recv,
    slot_send,
    slot_recv,
    own_sem,
    pair_send,
    pair_recv,
    up_send,
    up_recv,
    down_send,
    down_recv,
    plane_send,
    plane_recv,
):
    dp, ctx = lax.axis_index("dp"), lax.axis_index("ctx")
    x_lo, z = dp // Z, dp % Z
    chip, core = ctx // 2, ctx % 2
    other = ctx + 1 - 2 * core

    def block_of(back, at_core):
        return rows_at((8 - 2 * back + at_core) * ROWS, ROWS)

    def near(back):
        return remote(
            terms_ref.at[block_of(back, 1 - core)],
            near_in.at[back],
            near_send.at[back],
            near_recv.at[back],
            dp,
            other,
        )

    def far(back):
        return remote(
            far_out.at[back],
            far_in.at[back],
            far_send.at[back],
            far_recv.at[back],
            dp,
            ctx - 2 * back,
        )

    for back in (1, 2, 3, 4, 0):

        @pl.when(chip >= back)
        def _(back=back):
            near(back).start()

    for back in range(1, BACK + 1):

        @pl.when(chip >= back)
        def _(back=back):
            near(back).wait_recv()
            far_out[back] = (
                terms_ref[block_of(back, core)].astype(F32) + near_in[back].astype(F32)
            ).astype(BF)
            far(back).start()

    query_exchange = Exchange(staged_ref, query_slots, slot_send, slot_recv, own_sem, dp, ctx)
    query_exchange.start()
    near(0).wait_recv()
    total[...] = terms_ref[block_of(0, core)].astype(F32) + near_in[0].astype(F32)
    for back in range(1, BACK + 1):

        @pl.when(chip + back <= 7)
        def _(back=back):
            far(back).wait_recv()
            total[...] += far_in[back].astype(F32)

    for group in range(KVH):
        columns = slice(group * HD, (group + 1) * HD)
        key_grad_ref[:, columns] = total[:, group * 2 * HD : group * 2 * HD + HD].astype(BF)
        value_grad[:, columns] = total[:, group * 2 * HD + HD : (group + 1) * 2 * HD].astype(BF)

    offsets = (4, 3, -3, 2, -2, 1, -1, 0)

    def partial_at(at_core, offset):
        start = (at_core * Z + (z + Z + offset) % Z) * CHUNK
        return tn_dot(hidden_ref[:, rows_at(start, CHUNK)], value_grad[...])

    def pair(index):
        return remote(
            theirs.at[index],
            from_pair.at[index],
            pair_send.at[index],
            pair_recv.at[index],
            dp,
            other,
        )

    for index, offset in enumerate(offsets):
        theirs[index] = partial_at(1 - core, offset).astype(BF)
        pair(index).start()
    for index, offset in enumerate(offsets):
        mine[index] = partial_at(core, offset).astype(BF)

    half = CHUNK // 2
    above, below = x_lo * Z + (z + 1) % Z, x_lo * Z + (z + Z - 1) % Z

    def up(step):
        source, target = up_out.at[step], up_in.at[step]
        if step == 0:
            source, target = source.at[pl.ds(0, half)], target.at[pl.ds(0, half)]
        return remote(source, target, up_send.at[step], up_recv.at[step], above, ctx)

    def down(step):
        source, target = down_out.at[step], down_in.at[step]
        if step == 0:
            source, target = source.at[pl.ds(half, half)], target.at[pl.ds(half, half)]
        return remote(source, target, down_send.at[step], down_recv.at[step], below, ctx)

    def chip_sum(index):
        return mine[index].astype(F32) + from_pair[index].astype(F32)

    pair(0).wait_recv()
    furthest = chip_sum(0).astype(BF)
    up_out[0, :half] = furthest[:half]
    down_out[0, half:] = furthest[half:]
    up(0).start()
    down(0).start()
    for step in range(1, 4):
        for index, ring, out, arrived, kept in (
            (2 * step - 1, up, up_out, up_in, slice(0, half)),
            (2 * step, down, down_out, down_in, slice(half, CHUNK)),
        ):
            pair(index).wait_recv()
            out[step] = chip_sum(index).astype(BF)
            ring(step - 1).wait_recv()
            if step == 1:
                out[step, kept] = (
                    chip_sum(index)[kept] + arrived[step - 1, kept].astype(F32)
                ).astype(BF)
            else:
                out[step] = (chip_sum(index) + arrived[step - 1].astype(F32)).astype(BF)
            ring(step).start()
    pair(7).wait_recv()
    up(3).wait_recv()
    down(3).wait_recv()
    mine[7] = (chip_sum(7) + up_in[3].astype(F32) + down_in[3].astype(F32)).astype(BF)

    plane = (dp // Z) * 8 + chip

    def plane_copy(step):
        to_ctx = (ctx + step) % CTX
        return remote(
            mine.at[7, rows_at(to_ctx * CAP, CAP)],
            plane_in.at[plane],
            plane_send.at[step],
            plane_recv.at[plane],
            core * Z + z,
            to_ctx,
        )

    own_plane = pltpu.make_async_copy(
        mine.at[7, rows_at(ctx * CAP, CAP)], plane_in.at[plane], own_sem
    )

    query_exchange.finish()

    @pl.when(core == x_lo)
    def _():
        own_plane.start()

    @pl.when(core != x_lo)
    def _():
        plane_copy(0).start()

    @pl.loop(1, CTX)
    def _(step):
        plane_copy(step).start()

    for part in range(4):
        columns = slice(part * 1024, (part + 1) * 1024)
        query_grad_ref[:, columns] = tn_dot(owner_ref[...], query_slots[:, columns]).astype(BF)

    @pl.when(core == x_lo)
    def _():
        own_plane.wait()

    @pl.loop(0, 16)
    def _(source):
        @pl.when(jnp.logical_or(core != x_lo, source != plane))
        def _():
            remote(
                mine.at[7, pl.ds(0, CAP)],
                plane_in.at[source],
                plane_send.at[0],
                plane_recv.at[source],
                dp,
                other,
            ).wait_recv()

    weight_sum = plane_in[0].astype(F32)
    for source in range(1, 16):
        weight_sum = weight_sum + plane_in[source].astype(F32)
    weight_grad_ref[...] = weight_sum * (1.0 / math.sqrt(32768.0))

    @pl.when(core != x_lo)
    def _():
        plane_copy(0).wait_send()

    @pl.loop(1, CTX)
    def _(step):
        plane_copy(step).wait_send()

    for step in range(4):
        up(step).wait_send()
        down(step).wait_send()
    for index in range(8):
        pair(index).wait_send()
    for back in range(BACK + 1):

        @pl.when(chip >= back)
        def _(back=back):
            near(back).wait_send()
            if back > 0:
                far(back).wait_send()


def reduce(terms, staged, hidden, owner):
    vmem = pl.BlockSpec(memory_space=pltpu.VMEM)
    hbm = pl.BlockSpec(memory_space=pl.ANY)
    dma = pltpu.SemaphoreType.DMA
    chunk = (CHUNK, KVW)
    return pl.pallas_call(
        reduce_kernel,
        out_shape=(
            jax.ShapeDtypeStruct((ROWS, D), BF),
            jax.ShapeDtypeStruct((ROWS, KVW), BF),
            jax.ShapeDtypeStruct((CAP, KVW), F32),
        ),
        in_specs=[vmem, hbm, vmem, vmem],
        out_specs=(vmem, vmem, vmem),
        scratch_shapes=[
            pltpu.VMEM((BACK + 1, ROWS, 2 * KVW), BF),
            pltpu.VMEM((BACK + 1, ROWS, 2 * KVW), BF),
            pltpu.VMEM((BACK + 1, ROWS, 2 * KVW), BF),
            pltpu.VMEM((ROWS, 2 * KVW), F32),
            pltpu.VMEM((ROWS, KVW), BF),
            pltpu.VMEM((SLOTS, D), BF),
            pltpu.VMEM((8,) + chunk, BF),
            pltpu.VMEM((8,) + chunk, BF),
            pltpu.VMEM((8,) + chunk, BF),
            pltpu.VMEM((4,) + chunk, BF),
            pltpu.VMEM((4,) + chunk, BF),
            pltpu.VMEM((4,) + chunk, BF),
            pltpu.VMEM((4,) + chunk, BF),
            pltpu.VMEM((16, CAP, KVW), BF),
            dma((BACK + 1,)),
            dma((BACK + 1,)),
            dma((BACK + 1,)),
            dma((BACK + 1,)),
            dma((CTX,)),
            dma((CTX,)),
            dma,
            dma((8,)),
            dma((8,)),
            dma((4,)),
            dma((4,)),
            dma((4,)),
            dma((4,)),
            dma((16,)),
            dma((16,)),
        ],
        compiler_params=pltpu.CompilerParams(
            has_side_effects=True, vmem_limit_bytes=48 * 1024 * 1024
        ),
        name="reduce_gradients",
    )(terms, staged, hidden, owner)


def local(
    hidden,
    value_weight,
    queries,
    key_rows,
    attn_saved,
    grad_out,
    doc_lengths,
    routing,
    visible_blocks,
):
    key_window, value_window, saved_slots, owner, pack = gather(
        value_weight, hidden[0], key_rows[0], attn_saved[0], routing.reshape(CTX, ROWS)
    )
    staged, terms = attention(
        doc_lengths,
        visible_blocks[0],
        queries[0],
        grad_out[0],
        saved_slots,
        key_window,
        value_window,
        pack,
    )
    grad_query, grad_key, grad_weight = reduce(terms, staged, hidden[0], owner)
    return (grad_query[None], grad_key[None], grad_weight)


def solution(mesh):
    return jax.shard_map(
        local,
        mesh=mesh,
        in_specs=(
            P("dp", "ctx", None),
            P(("dp", "ctx"), None),
            P("dp", "ctx", None),
            P("dp", "ctx", None),
            P("dp", "ctx", None),
            P("dp", "ctx", None),
            P("dp", None),
            P("dp", None),
            P("dp", None, None),
        ),
        out_specs=(P("dp", "ctx", None), P("dp", "ctx", None), P(("dp", "ctx"), None)),
        check_vma=False,
    )
```

```python
import math

import jax
import jax.numpy as jnp
from jax import lax
from jax.experimental import pallas as pl
from jax.experimental.pallas import tpu as pltpu
from jax.sharding import PartitionSpec as P

QH = 32
HD = 128
VB = 64
ROWS = 128
CTX = 16
CAP = 16
SLOTS = CTX * CAP
GROUP = 8
KVH = 4
Z = 8
D = 4096
KVW = 512
WIN = 1280
USED = 1152
BACK = 4
CHUNK = 256
BF = jnp.bfloat16
F32 = jnp.float32
NT = (((1,), (1,)), ((), ()))
TN = (((0,), (0,)), ((), ()))
SCALE = 1.0 / math.sqrt(HD)


def remote(source, target, send_sem, recv_sem, dp, ctx):
    return pltpu.make_async_remote_copy(
        src_ref=source,
        dst_ref=target,
        send_sem=send_sem,
        recv_sem=recv_sem,
        device_id=(dp, ctx),
        device_id_type=pl.DeviceIdType.MESH,
    )


def rows_at(start, size):
    return pl.ds(pl.multiple_of(start, size), size)


def iota(shape, axis):
    return lax.broadcasted_iota(jnp.int32, shape, axis)


def nt_dot(first, second):
    return lax.dot_general(first, second, NT, preferred_element_type=F32)


def tn_dot(first, second):
    return lax.dot_general(first, second, TN, preferred_element_type=F32)


class Window:
    def __init__(self, own, window, far_send, far_recv, near_send, near_recv, own_sem, dp, ctx):
        self.own, self.window = own, window
        self.far_send, self.far_recv = far_send, far_recv
        self.near_send, self.near_recv = near_send, near_recv
        self.own_sem, self.dp, self.ctx = own_sem, dp, ctx
        self.chip, self.core = ctx // 2, ctx % 2
        self.other = ctx + 1 - 2 * self.core

    def slot(self, back, core):
        return self.window.at[rows_at((8 - 2 * back + core) * ROWS, ROWS)]

    def far(self, back):
        return remote(
            self.own,
            self.slot(back, self.core),
            self.far_send.at[back],
            self.far_recv.at[back],
            self.dp,
            self.ctx + 2 * back,
        )

    def near(self, back, core):
        source = self.own if back == 0 else self.slot(back, core)
        return remote(
            source,
            self.slot(back, core),
            self.near_send.at[back],
            self.near_recv.at[back],
            self.dp,
            self.other,
        )

    def own_copy(self):
        return pltpu.make_async_copy(self.own, self.slot(0, self.core), self.own_sem)

    def start(self):
        for back in range(1, BACK + 1):

            @pl.when(self.chip + back <= 7)
            def _(back=back):
                self.far(back).start()

        self.near(0, self.core).start()
        self.own_copy().start()

    def hand_on(self):
        for back in range(1, BACK + 1):

            @pl.when(self.chip >= back)
            def _(back=back):
                self.far(back).wait_recv()
                self.near(back, self.core).start()

    def arrive(self):
        for back in range(BACK + 1):

            @pl.when(self.chip >= back)
            def _(back=back):
                self.near(back, 1 - self.core).wait_recv()

        self.own_copy().wait()

    def finish(self):
        for back in range(BACK + 1):

            @pl.when(self.chip >= back)
            def _(back=back):
                self.near(back, self.core).wait_send()

        for back in range(1, BACK + 1):

            @pl.when(self.chip + back <= 7)
            def _(back=back):
                self.far(back).wait_send()


class Terms:
    def __init__(self, terms, near_in, far_out, far_in, total, sems, dp, ctx, columns):
        self.terms, self.near_in = terms, near_in
        self.far_out, self.far_in, self.total = far_out, far_in, total
        self.sems, self.dp, self.ctx, self.columns = sems, dp, ctx, columns
        self.chip, self.core = ctx // 2, ctx % 2
        self.other = ctx + 1 - 2 * self.core

    def block(self, back, core):
        return rows_at((8 - 2 * back + core) * ROWS, ROWS)

    def near(self, back):
        return remote(
            self.terms.at[self.block(back, 1 - self.core), self.columns],
            self.near_in.at[back, :, self.columns],
            self.sems[0].at[back],
            self.sems[1].at[back],
            self.dp,
            self.other,
        )

    def far(self, back):
        return remote(
            self.far_out.at[back, :, self.columns],
            self.far_in.at[back, :, self.columns],
            self.sems[2].at[back],
            self.sems[3].at[back],
            self.dp,
            self.ctx - 2 * back,
        )

    def start(self):
        for back in (4, 3, 2, 1, 0):

            @pl.when(self.chip >= back)
            def _(back=back):
                self.near(back).start()

    def pair_sum(self, back):
        own = self.terms[self.block(back, self.core), self.columns]
        return own.astype(F32) + self.near_in[back, :, self.columns].astype(F32)

    def send(self):
        for back in (4, 3, 2, 1):

            @pl.when(self.chip >= back)
            def _(back=back):
                self.near(back).wait_recv()
                self.far_out[back, :, self.columns] = self.pair_sum(back).astype(BF)
                self.far(back).start()

        self.near(0).wait_recv()
        self.total[:, self.columns] = self.pair_sum(0)

    def add(self):
        for back in range(1, BACK + 1):

            @pl.when(self.chip + back <= 7)
            def _(back=back):
                self.far(back).wait_recv()
                self.total[:, self.columns] += self.far_in[back, :, self.columns].astype(F32)

    def finish(self):
        for back in range(BACK + 1):

            @pl.when(self.chip >= back)
            def _(back=back):
                self.near(back).wait_send()
                if back > 0:
                    self.far(back).wait_send()


class Exchange:
    def __init__(self, source, arrived, send_sem, recv_sem, own_sem, dp, ctx, columns):
        self.source, self.arrived = source, arrived
        self.send_sem, self.recv_sem = send_sem, recv_sem
        self.own_sem, self.dp, self.ctx, self.columns = own_sem, dp, ctx, columns

    def copy(self, step):
        partner = (self.ctx + step) % CTX
        return remote(
            self.source.at[rows_at(partner * CAP, CAP), self.columns],
            self.arrived.at[rows_at(self.ctx * CAP, CAP), self.columns],
            self.send_sem.at[step],
            self.recv_sem.at[step],
            self.dp,
            partner,
        )

    def own_copy(self):
        own = rows_at(self.ctx * CAP, CAP)
        return pltpu.make_async_copy(
            self.source.at[own, self.columns], self.arrived.at[own, self.columns], self.own_sem
        )

    def start(self):
        @pl.loop(1, CTX)
        def _(step):
            self.copy(step).start()

        self.own_copy().start()

    def finish(self):
        @pl.loop(1, CTX)
        def _(step):
            self.copy(step).wait()

        self.own_copy().wait()


def plane_partner(dp, ctx, step):
    chip = ((dp // Z) * 8 + ctx // 2 + step) % 16
    return (chip // 8) * Z + dp % Z, (chip % 8) * 2 + dp // Z


def one_hot(rows, shape):
    return jnp.where(rows == iota(shape, 0), 1.0, 0.0).astype(BF)


def kernel(
    length_ref,
    visible_ref,
    weight_ref,
    hidden_hbm,
    key_ref,
    saved_hbm,
    route_ref,
    query_hbm,
    grad_hbm,
    query_grad_ref,
    key_grad_ref,
    weight_grad_ref,
    hidden_ref,
    turned,
    queries,
    grads,
    saved_ref,
    staged,
    saved_slots,
    owner_turned,
    pack_ref,
    pack_turned,
    bias,
    delta,
    whole,
    value_own,
    empty,
    key_window,
    value_window,
    weights_all,
    dscores_all,
    key_terms,
    value_terms,
    staged_grad,
    query_slots,
    near_in,
    far_out,
    far_in,
    totals,
    value_grad,
    mine,
    theirs,
    from_pair,
    up_in,
    down_in,
    up_out,
    down_out,
    plane_in,
    load_sems,
    head_sems,
    own_sems,
    plane_sems,
    ring_sems,
    pair_sems,
    window_sems,
    slot_sems,
    term_sems,
    query_sems,
    pair_back_sems,
    ring_back_sems,
    plane_back_sems,
):
    dp, ctx = lax.axis_index("dp"), lax.axis_index("ctx")
    x_lo, z = dp // Z, dp % Z
    chip, core = ctx // 2, ctx % 2
    other = ctx + 1 - 2 * core
    above, below = x_lo * Z + (z + 1) % Z, x_lo * Z + (z + Z - 1) % Z

    load_saved = pltpu.make_async_copy(saved_hbm, saved_ref, load_sems.at[0])
    load_hidden = pltpu.make_async_copy(hidden_hbm, hidden_ref, load_sems.at[1])

    def load_query(head):
        columns = pl.ds(pl.multiple_of(head * HD, HD), HD)
        return pltpu.make_async_copy(
            query_hbm.at[:, columns], queries.at[rows_at(head * HD, HD)], head_sems.at[0, head]
        )

    def load_grad(head):
        columns = pl.ds(pl.multiple_of(head * HD, HD), HD)
        return pltpu.make_async_copy(
            grad_hbm.at[:, columns], grads.at[rows_at(head * HD, HD)], head_sems.at[1, head]
        )

    load_saved.start()
    load_hidden.start()

    barrier = pltpu.get_barrier_semaphore()

    def greet(to_dp, to_ctx):
        pl.semaphore_signal(
            barrier, inc=1, device_id=(to_dp, to_ctx), device_id_type=pl.DeviceIdType.MESH
        )

    greet(above, ctx)
    greet(below, ctx)

    @pl.loop(1, CTX)
    def _(step):
        greet(dp, (ctx + step) % CTX)
        greet(*plane_partner(dp, ctx, step))
        greet(core * Z + z, (ctx + step) % CTX)

    @pl.when(core != x_lo)
    def _():
        greet(*plane_partner(dp, ctx, 0))
        greet(core * Z + z, ctx)

    @pl.loop(0, QH)
    def _(head):
        load_query(head).start()
        load_grad(head).start()

    same = jnp.where(iota((ROWS, ROWS), 0) == iota((ROWS, ROWS), 1), 1.0, 0.0).astype(BF)
    before = jnp.where(iota((ROWS, ROWS), 0) < iota((ROWS, ROWS), 1), 1.0, 0.0).astype(BF)
    route = route_ref[...]
    coming = lax.shift_right_logical(route, 7) == ctx
    rank = jnp.dot(jnp.where(coming, 1.0, 0.0).astype(BF), before, preferred_element_type=F32)
    rank = jnp.where(coming, rank.astype(jnp.int32), -1)
    place = route - ctx * ROWS
    parts = []
    for pack in range(CTX):
        to_rank = one_hot(rank[pack : pack + 1], (CAP, ROWS))
        to_place = one_hot(place[pack : pack + 1], (ROWS, ROWS))
        parts.append(nt_dot(to_rank, to_place).astype(BF))
    owner = jnp.concatenate(parts, axis=0)
    owner_turned[...] = nt_dot(same, owner).astype(BF)
    load_saved.wait()
    for part in range(4):
        columns = slice(part * 1024, (part + 1) * 1024)
        staged[:, columns] = jnp.dot(
            owner, saved_ref[:, columns], preferred_element_type=F32
        ).astype(BF)

    pl.semaphore_wait(barrier, 2 + 3 * (CTX - 1) + jnp.where(core != x_lo, 2, 0))

    shard = whole.at[rows_at((dp * CTX + ctx) * CAP, CAP)]

    def plane_copy(step):
        to_dp, to_ctx = plane_partner(dp, ctx, step)
        return remote(
            weight_ref, shard, plane_sems.at[0, step], plane_sems.at[1, ctx], to_dp, to_ctx
        )

    own_shard = pltpu.make_async_copy(weight_ref, shard, own_sems.at[3])

    @pl.when(core == x_lo)
    def _():
        own_shard.start()

    @pl.when(core != x_lo)
    def _():
        plane_copy(0).start()

    @pl.loop(1, 16)
    def _(step):
        plane_copy(step).start()

    def window(own, whole_window, which):
        sems = [window_sems.at[which, kind] for kind in range(4)]
        return Window(own, whole_window, *sems, own_sems.at[which], dp, ctx)

    keys = window(key_ref, key_window, 0)
    values = window(value_own, value_window, 1)
    keys.start()
    saved_exchange = Exchange(
        staged,
        saved_slots,
        slot_sems.at[0],
        slot_sems.at[1],
        own_sems.at[2],
        dp,
        ctx,
        slice(0, D),
    )
    saved_exchange.start()

    own_owner = lax.shift_right_logical(route_ref[pl.ds(ctx, 1)], 7)
    hit = own_owner == iota((CTX, ROWS), 0)
    count = jnp.dot(jnp.where(hit, 1.0, 0.0).astype(BF), before, preferred_element_type=F32)
    own_rank = jnp.sum(jnp.where(hit, count, 0.0), axis=0, keepdims=True).astype(jnp.int32)
    pack_ref[...] = one_hot(own_owner * CAP + own_rank, (SLOTS, ROWS))
    pack_turned[...] = nt_dot(same, pack_ref[...]).astype(BF)

    empty[...] = jnp.zeros_like(empty)
    for back in range(1, BACK + 1):

        @pl.when(chip < back)
        def _(back=back):
            hole = pl.ds((8 - 2 * back) * ROWS, 2 * ROWS)
            pltpu.sync_copy(empty, key_window.at[hole])
            pltpu.sync_copy(empty, value_window.at[hole])

    @pl.when(core == x_lo)
    def _():
        own_shard.wait()

    @pl.loop(0, CTX)
    def _(source):
        @pl.when(jnp.logical_or(core != x_lo, source != ctx))
        def _():
            shard_in = whole.at[rows_at(((core * Z + z) * CTX + source) * CAP, CAP)]
            remote(
                weight_ref, shard_in, plane_sems.at[0, 0], plane_sems.at[1, source], dp, other
            ).wait_recv()

    half = CHUNK // 2

    def piece(at_core, offset, part):
        start = (at_core * Z + (z + Z + offset) % Z) * CHUNK + part * half
        return whole.at[rows_at(start, half)]

    def up(step, part, offset):
        block = piece(core, offset, part)
        return remote(
            block, block, ring_sems.at[0, step, part], ring_sems.at[1, step, part], above, ctx
        )

    def down(step, part, offset):
        block = piece(core, offset, part)
        return remote(
            block, block, ring_sems.at[2, step, part], ring_sems.at[3, step, part], below, ctx
        )

    def pair(at_core, offset, part):
        block = piece(at_core, offset, part)
        index = offset + 3
        return remote(
            block, block, pair_sems.at[0, index, part], pair_sems.at[1, index, part], dp, other
        )

    for part in range(2):
        up(0, part, 0).start()
        down(0, part, 0).start()
        pair(core, 0, part).start()

    position = ctx * ROWS + iota((1, ROWS), 1)
    doc_start = jnp.zeros((1, ROWS), jnp.int32)
    doc_end = jnp.int32(0)
    for n in range(8):
        length = length_ref[0, n]
        doc_end = doc_end + length
        doc_start = doc_start + jnp.where(position >= doc_end, length, 0)
    left = iota((1, ROWS), 1) < VB

    for block in range(USED // VB):
        column = jnp.maximum(2 * ctx - 16 + block, 0)
        seen = jnp.where(left, visible_ref[2 * ctx, column], visible_ref[2 * ctx + 1, column])
        key_position = ctx * ROWS - 1024 + block * VB + iota((VB, ROWS), 0)
        allowed = (key_position >= doc_start) & (key_position <= position) & (seen == 1)
        bias[block * VB : (block + 1) * VB] = jnp.where(allowed, 0.0, -1e30)

    @pl.loop(0, QH)
    def _(head):
        load_query(head).wait()
        load_grad(head).wait()

    used = pl.ds(pl.multiple_of(core * ROWS, ROWS), USED)
    unused = pl.ds(pl.multiple_of((1 - core) * USED, ROWS), ROWS)
    key_terms[unused] = jnp.zeros((ROWS, KVW), BF)
    value_terms[unused] = jnp.zeros((ROWS, KVW), BF)

    def forward(group):
        columns = slice(group * HD, (group + 1) * HD)
        rows = slice(group * GROUP * HD, (group + 1) * GROUP * HD)

        @pl.loop(0, GROUP // 2)
        def _(two):
            for head in range(2):
                at = pl.multiple_of((group * GROUP + two * 2 + head) * HD, HD)
                scores = nt_dot(key_window[used, columns], queries[pl.ds(at, HD)]) + bias[...]
                top = jnp.max(scores, axis=0, keepdims=True)
                raised = jnp.exp((scores - top) * SCALE)
                weights = raised * (1.0 / jnp.sum(raised, axis=0, keepdims=True))
                weights_all[:, pl.ds(at, HD)] = weights.astype(BF)

        value_terms[used, columns] = jnp.dot(
            weights_all[:, rows], grads[rows], preferred_element_type=F32
        ).astype(BF)

    query_parts = []

    def backward(group):
        columns = slice(group * HD, (group + 1) * HD)
        rows = slice(group * GROUP * HD, (group + 1) * GROUP * HD)

        @pl.loop(0, GROUP // 2)
        def _(two):
            for head in range(2):
                index = group * GROUP + two * 2 + head
                at = pl.multiple_of(index * HD, HD)
                to = pl.multiple_of((two * 2 + head) * HD, HD)
                weights = weights_all[:, pl.ds(at, HD)].astype(F32)
                dweights = nt_dot(value_window[used, columns], grads[pl.ds(at, HD)])
                dscores_all[:, pl.ds(to, HD)] = (
                    (weights * SCALE)
                    * (dweights.astype(BF).astype(F32) - delta[pl.ds(index, 1)])
                ).astype(BF)

        key_terms[used, columns] = jnp.dot(
            dscores_all[...], queries[rows], preferred_element_type=F32
        ).astype(BF)
        keys_turned = nt_dot(same, key_window[used, columns]).astype(BF)
        query_grad = jnp.dot(
            keys_turned, dscores_all[...], preferred_element_type=F32
        ).astype(BF)
        for head in range(GROUP):
            at = (group * GROUP + head) * HD
            staged_grad[:, at : at + HD] = nt_dot(
                pack_ref[...], query_grad[:, head * HD : (head + 1) * HD]
            ).astype(BF)
        part = Exchange(
            staged_grad,
            query_slots,
            query_sems.at[0, group],
            query_sems.at[1, group],
            own_sems.at[4 + group],
            dp,
            ctx,
            rows,
        )
        part.start()
        query_parts.append(part)

    keys.hand_on()
    keys.arrive()
    for step in range(3):
        for part in range(2):
            up(step, part, -step - 1).wait_recv()
            if step < 2 or part == 0:
                up(step + 1, part, -step - 1).start()
            pair(core, -step - 1, part).start()
            down(step, part, step + 1).wait_recv()
            if step < 2 or part == 1:
                down(step + 1, part, step + 1).start()
            pair(core, step + 1, part).start()
        forward(step)
    up(3, 0, 4).wait_recv()
    pair(core, 4, 0).start()
    down(3, 1, 4).wait_recv()
    pair(core, 4, 1).start()
    load_hidden.wait()
    for offset in range(-3, 5):
        for part in range(2):
            pair(1 - core, offset, part).wait_recv()
    value_own[...] = jnp.dot(hidden_ref[...], whole[...], preferred_element_type=F32).astype(BF)
    values.start()
    forward(3)

    def term_sum(which, terms, columns):
        gradient = min(which, 1)
        return Terms(
            terms,
            near_in.at[gradient],
            far_out.at[gradient],
            far_in.at[gradient],
            totals.at[gradient],
            [term_sems.at[which, kind] for kind in range(4)],
            dp,
            ctx,
            columns,
        )

    value_sum = term_sum(0, value_terms, slice(0, KVW))
    key_sums = [
        term_sum(1 + part, key_terms, slice(part * 256, (part + 1) * 256)) for part in range(2)
    ]
    value_sum.start()
    values.hand_on()
    value_sum.send()
    diagonal = jnp.where(iota((CHUNK, CHUNK), 0) == iota((CHUNK, CHUNK), 1), 1.0, 0.0).astype(BF)
    for block in range(D // CHUNK):
        rows = slice(block * CHUNK, (block + 1) * CHUNK)
        turned[rows] = nt_dot(diagonal, hidden_ref[:, rows]).astype(BF)

    saved_exchange.finish()
    ones = jnp.ones((8, HD), BF)

    @pl.loop(0, QH // 4)
    def _(four):
        for head in range(4):
            index = four * 4 + head
            at = pl.ds(pl.multiple_of(index * HD, HD), HD)
            saved = jnp.dot(pack_turned[...], saved_slots[:, at], preferred_element_type=F32)
            product = saved * grads[at].astype(F32)
            high = product.astype(BF)
            low = (product - high.astype(F32)).astype(BF)
            delta[pl.ds(index, 1)] = (nt_dot(ones, high) + nt_dot(ones, low))[:1]

    values.arrive()
    backward(0)
    value_sum.add()
    value_grad[...] = totals[0].astype(BF)

    offsets = (4, 3, -3, 2, -2, 1, -1, 0)

    def partial_at(at_core, offset):
        start = (at_core * Z + (z + Z + offset) % Z) * CHUNK
        return jnp.dot(
            turned[rows_at(start, CHUNK)], value_grad[...], preferred_element_type=F32
        ).astype(BF)

    def pair_back(index):
        return remote(
            theirs.at[index],
            from_pair.at[index],
            pair_back_sems.at[0, index],
            pair_back_sems.at[1, index],
            dp,
            other,
        )

    for index, offset in enumerate(offsets):
        theirs[index] = partial_at(1 - core, offset)
        pair_back(index).start()
    for index, offset in enumerate(offsets):
        mine[index] = partial_at(core, offset)

    def spans(part):
        return slice(part * half, (part + 1) * half)

    def up_back(step, part):
        return remote(
            up_out.at[step, spans(part)],
            up_in.at[step, spans(part)],
            ring_back_sems.at[0, step, part],
            ring_back_sems.at[1, step, part],
            above,
            ctx,
        )

    def down_back(step, part):
        return remote(
            down_out.at[step, spans(part)],
            down_in.at[step, spans(part)],
            ring_back_sems.at[2, step, part],
            ring_back_sems.at[3, step, part],
            below,
            ctx,
        )

    def chip_sum(index, part):
        return mine[index, spans(part)].astype(F32) + from_pair[index, spans(part)].astype(F32)

    pair_back(0).wait_recv()
    up_out[0, spans(0)] = chip_sum(0, 0).astype(BF)
    up_back(0, 0).start()
    down_out[0, spans(1)] = chip_sum(0, 1).astype(BF)
    down_back(0, 1).start()

    def ring_back(step):
        pair_back(2 * step - 1).wait_recv()
        pair_back(2 * step).wait_recv()
        if step == 1:
            up_out[1, spans(1)] = chip_sum(1, 1).astype(BF)
            up_back(1, 1).start()
            down_out[1, spans(0)] = chip_sum(2, 0).astype(BF)
            down_back(1, 0).start()
        for index, ring, out, arrived, kept in (
            (2 * step - 1, up_back, up_out, up_in, 0),
            (2 * step, down_back, down_out, down_in, 1),
        ):
            for part in (kept,) if step == 1 else (1 - kept, kept):
                ring(step - 1, part).wait_recv()
                out[step, spans(part)] = (
                    chip_sum(index, part) + arrived[step - 1, spans(part)].astype(F32)
                ).astype(BF)
                ring(step, part).start()

    backward(1)
    key_sums[0].start()
    ring_back(1)
    key_sums[0].send()
    backward(2)
    ring_back(2)
    backward(3)
    key_sums[1].start()
    ring_back(3)
    key_sums[1].send()
    pair_back(7).wait_recv()
    for part in (0, 1):
        up_back(3, part).wait_recv()
        down_back(3, part).wait_recv()
        mine[7, spans(part)] = (
            chip_sum(7, part)
            + up_in[3, spans(part)].astype(F32)
            + down_in[3, spans(part)].astype(F32)
        ).astype(BF)

    plane = x_lo * 8 + chip

    def plane_back(step):
        to_ctx = (ctx + step) % CTX
        return remote(
            mine.at[7, rows_at(to_ctx * CAP, CAP)],
            plane_in.at[plane],
            plane_back_sems.at[0, step],
            plane_back_sems.at[1, plane],
            core * Z + z,
            to_ctx,
        )

    own_plane = pltpu.make_async_copy(
        mine.at[7, rows_at(ctx * CAP, CAP)], plane_in.at[plane], own_sems.at[3]
    )

    @pl.when(core == x_lo)
    def _():
        own_plane.start()

    @pl.when(core != x_lo)
    def _():
        plane_back(0).start()

    @pl.loop(1, CTX)
    def _(step):
        plane_back(step).start()

    for group in range(KVH):
        columns = slice(group * 1024, (group + 1) * 1024)
        query_parts[group].finish()
        query_grad_ref[:, columns] = jnp.dot(
            owner_turned[...], query_slots[:, columns], preferred_element_type=F32
        ).astype(BF)
    for part in key_sums:
        part.add()
    key_grad_ref[...] = totals[1].astype(BF)

    @pl.when(core == x_lo)
    def _():
        own_plane.wait()

    @pl.loop(0, 16)
    def _(source):
        @pl.when(jnp.logical_or(core != x_lo, source != plane))
        def _():
            remote(
                mine.at[7, pl.ds(0, CAP)],
                plane_in.at[source],
                plane_back_sems.at[0, 0],
                plane_back_sems.at[1, source],
                dp,
                other,
            ).wait_recv()

    weight_sum = plane_in[0].astype(F32)
    for source in range(1, 16):
        weight_sum = weight_sum + plane_in[source].astype(F32)
    weight_grad_ref[...] = weight_sum * (1.0 / math.sqrt(32768.0))

    @pl.when(core != x_lo)
    def _():
        plane_copy(0).wait_send()
        plane_back(0).wait_send()

    @pl.loop(1, 16)
    def _(step):
        plane_copy(step).wait_send()
        plane_back(step).wait_send()

    for step in range(3):
        for part in range(2):
            up(step, part, -step).wait_send()
            down(step, part, step).wait_send()
    up(3, 0, -3).wait_send()
    down(3, 1, 3).wait_send()
    for offset in range(-3, 5):
        for part in range(2):
            pair(core, offset, part).wait_send()
    up_back(0, 0).wait_send()
    down_back(0, 1).wait_send()
    for step in range(1, 4):
        for part in range(2):
            up_back(step, part).wait_send()
            down_back(step, part).wait_send()
    for index in range(8):
        pair_back(index).wait_send()
    keys.finish()
    values.finish()
    for part in [value_sum] + key_sums:
        part.finish()


def local(
    hidden,
    value_weight,
    queries,
    key_rows,
    attn_saved,
    grad_out,
    doc_lengths,
    routing,
    visible_blocks,
):
    vmem = pl.BlockSpec(memory_space=pltpu.VMEM)
    smem = pl.BlockSpec(memory_space=pltpu.SMEM)
    hbm = pl.BlockSpec(memory_space=pltpu.HBM)
    dma = pltpu.SemaphoreType.DMA
    chunk = (CHUNK, KVW)
    blocks = (2, BACK + 1, ROWS, KVW)
    grad_query, grad_key, grad_weight = pl.pallas_call(
        kernel,
        out_shape=(
            jax.ShapeDtypeStruct((ROWS, D), BF),
            jax.ShapeDtypeStruct((ROWS, KVW), BF),
            jax.ShapeDtypeStruct((CAP, KVW), F32),
        ),
        in_specs=[smem, smem, hbm, hbm, hbm, hbm, vmem, hbm, hbm],
        out_specs=(vmem, vmem, vmem),
        scratch_shapes=[
            pltpu.VMEM((ROWS, D), BF),
            pltpu.VMEM((D, ROWS), BF),
            pltpu.VMEM((QH * HD, HD), BF),
            pltpu.VMEM((QH * HD, HD), BF),
            pltpu.VMEM((ROWS, D), BF),
            pltpu.VMEM((SLOTS, D), BF),
            pltpu.VMEM((SLOTS, D), BF),
            pltpu.VMEM((ROWS, SLOTS), BF),
            pltpu.VMEM((SLOTS, ROWS), BF),
            pltpu.VMEM((ROWS, SLOTS), BF),
            pltpu.VMEM((USED, ROWS), F32),
            pltpu.VMEM((QH, ROWS), F32),
            pltpu.VMEM((D, KVW), BF),
            pltpu.VMEM((ROWS, KVW), BF),
            pltpu.VMEM((2 * ROWS, KVW), BF),
            pltpu.VMEM((WIN, KVW), BF),
            pltpu.VMEM((WIN, KVW), BF),
            pltpu.VMEM((USED, QH * HD), BF),
            pltpu.VMEM((USED, GROUP * HD), BF),
            pltpu.VMEM((WIN, KVW), BF),
            pltpu.VMEM((WIN, KVW), BF),
            pltpu.VMEM((SLOTS, D), BF),
            pltpu.VMEM((SLOTS, D), BF),
            pltpu.VMEM(blocks, BF),
            pltpu.VMEM(blocks, BF),
            pltpu.VMEM(blocks, BF),
            pltpu.VMEM((2, ROWS, KVW), F32),
            pltpu.VMEM((ROWS, KVW), BF),
            pltpu.VMEM((8,) + chunk, BF),
            pltpu.VMEM((8,) + chunk, BF),
            pltpu.VMEM((8,) + chunk, BF),
            pltpu.VMEM((4,) + chunk, BF),
            pltpu.VMEM((4,) + chunk, BF),
            pltpu.VMEM((4,) + chunk, BF),
            pltpu.VMEM((4,) + chunk, BF),
            pltpu.VMEM((16, CAP, KVW), BF),
            dma((2,)),
            dma((2, QH)),
            dma((8,)),
            dma((2, 16)),
            dma((4, 4, 2)),
            dma((2, 8, 2)),
            dma((2, 4, BACK + 1)),
            dma((2, CTX)),
            dma((3, 4, BACK + 1)),
            dma((2, KVH, CTX)),
            dma((2, 8)),
            dma((4, 4, 2)),
            dma((2, 16)),
        ],
        compiler_params=pltpu.CompilerParams(
            has_side_effects=True, vmem_limit_bytes=60 * 1024 * 1024, collective_id=0
        ),
        name="attention_backward",
    )(
        doc_lengths,
        visible_blocks[0],
        value_weight,
        hidden[0],
        key_rows[0],
        attn_saved[0],
        routing.reshape(CTX, ROWS),
        queries[0],
        grad_out[0],
    )
    return (grad_query[None], grad_key[None], grad_weight)


def solution(mesh):
    return jax.shard_map(
        local,
        mesh=mesh,
        in_specs=(
            P("dp", "ctx", None),
            P(("dp", "ctx"), None),
            P("dp", "ctx", None),
            P("dp", "ctx", None),
            P("dp", "ctx", None),
            P("dp", "ctx", None),
            P("dp", None),
            P("dp", None),
            P("dp", None, None),
        ),
        out_specs=(P("dp", "ctx", None), P("dp", "ctx", None), P(("dp", "ctx"), None)),
        check_vma=False,
    )
```

```python
import math

import jax
import jax.numpy as jnp
from jax import lax
from jax.experimental import pallas as pl
from jax.experimental.pallas import tpu as pltpu
from jax.sharding import PartitionSpec as P

QH = 32
HD = 128
VB = 64
ROWS = 128
CTX = 16
CAP = 16
SLOTS = CTX * CAP
GROUP = 8
KVH = 4
Z = 8
D = 4096
KVW = 512
WIN = 1280
USED = 1152
BACK = 4
CHUNK = 256
BF = jnp.bfloat16
F32 = jnp.float32
NT = (((1,), (1,)), ((), ()))
TN = (((0,), (0,)), ((), ()))
SCALE = 1.0 / math.sqrt(HD)


def remote(source, target, send_sem, recv_sem, dp, ctx):
    return pltpu.make_async_remote_copy(
        src_ref=source,
        dst_ref=target,
        send_sem=send_sem,
        recv_sem=recv_sem,
        device_id=(dp, ctx),
        device_id_type=pl.DeviceIdType.MESH,
    )


def rows_at(start, size):
    return pl.ds(pl.multiple_of(start, size), size)


def iota(shape, axis):
    return lax.broadcasted_iota(jnp.int32, shape, axis)


def nt_dot(first, second):
    return lax.dot_general(first, second, NT, preferred_element_type=F32)


def tn_dot(first, second):
    return lax.dot_general(first, second, TN, preferred_element_type=F32)


class Window:
    def __init__(self, own, window, far_send, far_recv, near_send, near_recv, own_sem, dp, ctx):
        self.own, self.window = own, window
        self.far_send, self.far_recv = far_send, far_recv
        self.near_send, self.near_recv = near_send, near_recv
        self.own_sem, self.dp, self.ctx = own_sem, dp, ctx
        self.chip, self.core = ctx // 2, ctx % 2
        self.other = ctx + 1 - 2 * self.core

    def slot(self, back, core):
        return self.window.at[rows_at((8 - 2 * back + core) * ROWS, ROWS)]

    def far(self, back):
        return remote(
            self.own,
            self.slot(back, self.core),
            self.far_send.at[back],
            self.far_recv.at[back],
            self.dp,
            self.ctx + 2 * back,
        )

    def near(self, back, core):
        source = self.own if back == 0 else self.slot(back, core)
        return remote(
            source,
            self.slot(back, core),
            self.near_send.at[back],
            self.near_recv.at[back],
            self.dp,
            self.other,
        )

    def own_copy(self):
        return pltpu.make_async_copy(self.own, self.slot(0, self.core), self.own_sem)

    def start(self):
        for back in range(1, BACK + 1):

            @pl.when(self.chip + back <= 7)
            def _(back=back):
                self.far(back).start()

        self.near(0, self.core).start()
        self.own_copy().start()

    def hand_on(self):
        for back in range(1, BACK + 1):

            @pl.when(self.chip >= back)
            def _(back=back):
                self.far(back).wait_recv()
                self.near(back, self.core).start()

    def arrive(self):
        for back in range(BACK + 1):

            @pl.when(self.chip >= back)
            def _(back=back):
                self.near(back, 1 - self.core).wait_recv()

        self.own_copy().wait()

    def finish(self):
        for back in range(BACK + 1):

            @pl.when(self.chip >= back)
            def _(back=back):
                self.near(back, self.core).wait_send()

        for back in range(1, BACK + 1):

            @pl.when(self.chip + back <= 7)
            def _(back=back):
                self.far(back).wait_send()


class Terms:
    def __init__(self, terms, near_in, far_out, far_in, total, sems, dp, ctx, columns):
        self.terms, self.near_in = terms, near_in
        self.far_out, self.far_in, self.total = far_out, far_in, total
        self.sems, self.dp, self.ctx, self.columns = sems, dp, ctx, columns
        self.chip, self.core = ctx // 2, ctx % 2
        self.other = ctx + 1 - 2 * self.core

    def block(self, back, core):
        return rows_at((8 - 2 * back + core) * ROWS, ROWS)

    def near(self, back):
        return remote(
            self.terms.at[self.block(back, 1 - self.core), self.columns],
            self.near_in.at[back, :, self.columns],
            self.sems[0].at[back],
            self.sems[1].at[back],
            self.dp,
            self.other,
        )

    def far(self, back):
        return remote(
            self.far_out.at[back, :, self.columns],
            self.far_in.at[back, :, self.columns],
            self.sems[2].at[back],
            self.sems[3].at[back],
            self.dp,
            self.ctx - 2 * back,
        )

    def start(self):
        for back in (4, 3, 2, 1, 0):

            @pl.when(self.chip >= back)
            def _(back=back):
                self.near(back).start()

    def pair_sum(self, back):
        own = self.terms[self.block(back, self.core), self.columns]
        return own.astype(F32) + self.near_in[back, :, self.columns].astype(F32)

    def send(self):
        for back in (4, 3, 2, 1):

            @pl.when(self.chip >= back)
            def _(back=back):
                self.near(back).wait_recv()
                self.far_out[back, :, self.columns] = self.pair_sum(back).astype(BF)
                self.far(back).start()

        self.near(0).wait_recv()
        self.total[:, self.columns] = self.pair_sum(0)

    def add(self):
        for back in range(1, BACK + 1):

            @pl.when(self.chip + back <= 7)
            def _(back=back):
                self.far(back).wait_recv()
                self.total[:, self.columns] += self.far_in[back, :, self.columns].astype(F32)

    def finish(self):
        for back in range(BACK + 1):

            @pl.when(self.chip >= back)
            def _(back=back):
                self.near(back).wait_send()
                if back > 0:
                    self.far(back).wait_send()


class Exchange:
    def __init__(self, source, arrived, send_sem, recv_sem, own_sem, dp, ctx, columns):
        self.source, self.arrived = source, arrived
        self.send_sem, self.recv_sem = send_sem, recv_sem
        self.own_sem, self.dp, self.ctx, self.columns = own_sem, dp, ctx, columns

    def copy(self, step):
        partner = (self.ctx + step) % CTX
        return remote(
            self.source.at[rows_at(partner * CAP, CAP), self.columns],
            self.arrived.at[rows_at(self.ctx * CAP, CAP), self.columns],
            self.send_sem.at[step],
            self.recv_sem.at[step],
            self.dp,
            partner,
        )

    def own_copy(self):
        own = rows_at(self.ctx * CAP, CAP)
        return pltpu.make_async_copy(
            self.source.at[own, self.columns], self.arrived.at[own, self.columns], self.own_sem
        )

    def start(self):
        @pl.loop(1, CTX)
        def _(step):
            self.copy(step).start()

        self.own_copy().start()

    def finish(self):
        @pl.loop(1, CTX)
        def _(step):
            self.copy(step).wait()

        self.own_copy().wait()


def plane_partner(dp, ctx, step):
    chip = ((dp // Z) * 8 + ctx // 2 + step) % 16
    return (chip // 8) * Z + dp % Z, (chip % 8) * 2 + dp // Z


def one_hot(rows, shape):
    return jnp.where(rows == iota(shape, 0), 1.0, 0.0).astype(BF)


def kernel(
    length_ref,
    visible_ref,
    weight_ref,
    hidden_hbm,
    key_ref,
    saved_hbm,
    route_ref,
    query_hbm,
    grad_hbm,
    query_grad_ref,
    key_grad_ref,
    weight_grad_ref,
    hidden_ref,
    turned,
    queries,
    grads,
    saved_ref,
    staged,
    saved_slots,
    owner_turned,
    pack_ref,
    pack_turned,
    bias,
    delta,
    whole,
    value_own,
    empty,
    key_window,
    value_window,
    weights_all,
    dscores_all,
    key_terms,
    value_terms,
    staged_grad,
    query_slots,
    near_in,
    far_out,
    far_in,
    totals,
    value_grad,
    mine,
    theirs,
    from_pair,
    up_in,
    down_in,
    up_out,
    down_out,
    plane_in,
    load_sems,
    head_sems,
    own_sems,
    plane_sems,
    ring_sems,
    pair_sems,
    window_sems,
    slot_sems,
    term_sems,
    query_sems,
    pair_back_sems,
    ring_back_sems,
    plane_back_sems,
):
    dp, ctx = lax.axis_index("dp"), lax.axis_index("ctx")
    x_lo, z = dp // Z, dp % Z
    chip, core = ctx // 2, ctx % 2
    other = ctx + 1 - 2 * core
    above, below = x_lo * Z + (z + 1) % Z, x_lo * Z + (z + Z - 1) % Z

    load_saved = pltpu.make_async_copy(saved_hbm, saved_ref, load_sems.at[0])
    load_hidden = pltpu.make_async_copy(hidden_hbm, hidden_ref, load_sems.at[1])

    def load_query(head):
        columns = pl.ds(pl.multiple_of(head * HD, HD), HD)
        return pltpu.make_async_copy(
            query_hbm.at[:, columns], queries.at[rows_at(head * HD, HD)], head_sems.at[0, head]
        )

    def load_grad(head):
        columns = pl.ds(pl.multiple_of(head * HD, HD), HD)
        return pltpu.make_async_copy(
            grad_hbm.at[:, columns], grads.at[rows_at(head * HD, HD)], head_sems.at[1, head]
        )

    load_saved.start()
    load_hidden.start()

    barrier = pltpu.get_barrier_semaphore()

    def greet(to_dp, to_ctx):
        pl.semaphore_signal(
            barrier, inc=1, device_id=(to_dp, to_ctx), device_id_type=pl.DeviceIdType.MESH
        )

    greet(above, ctx)
    greet(below, ctx)

    @pl.loop(1, CTX)
    def _(step):
        greet(dp, (ctx + step) % CTX)
        greet(*plane_partner(dp, ctx, step))
        greet(core * Z + z, (ctx + step) % CTX)

    @pl.when(core != x_lo)
    def _():
        greet(*plane_partner(dp, ctx, 0))
        greet(core * Z + z, ctx)

    @pl.loop(0, QH)
    def _(head):
        load_query(head).start()
        load_grad(head).start()

    same = jnp.where(iota((ROWS, ROWS), 0) == iota((ROWS, ROWS), 1), 1.0, 0.0).astype(BF)
    before = jnp.where(iota((ROWS, ROWS), 0) < iota((ROWS, ROWS), 1), 1.0, 0.0).astype(BF)
    route = route_ref[...]
    coming = lax.shift_right_logical(route, 7) == ctx
    rank = jnp.dot(jnp.where(coming, 1.0, 0.0).astype(BF), before, preferred_element_type=F32)
    rank = jnp.where(coming, rank.astype(jnp.int32), -1)
    place = route - ctx * ROWS
    parts = []
    for pack in range(CTX):
        to_rank = one_hot(rank[pack : pack + 1], (CAP, ROWS))
        to_place = one_hot(place[pack : pack + 1], (ROWS, ROWS))
        parts.append(nt_dot(to_rank, to_place).astype(BF))
    owner = jnp.concatenate(parts, axis=0)
    owner_turned[...] = nt_dot(same, owner).astype(BF)
    load_saved.wait()
    for part in range(4):
        columns = slice(part * 1024, (part + 1) * 1024)
        staged[:, columns] = jnp.dot(
            owner, saved_ref[:, columns], preferred_element_type=F32
        ).astype(BF)

    pl.semaphore_wait(barrier, 2 + 3 * (CTX - 1) + jnp.where(core != x_lo, 2, 0))

    shard = whole.at[rows_at((dp * CTX + ctx) * CAP, CAP)]

    def plane_copy(step):
        to_dp, to_ctx = plane_partner(dp, ctx, step)
        return remote(
            weight_ref, shard, plane_sems.at[0, step], plane_sems.at[1, ctx], to_dp, to_ctx
        )

    own_shard = pltpu.make_async_copy(weight_ref, shard, own_sems.at[3])

    @pl.when(core == x_lo)
    def _():
        own_shard.start()

    @pl.when(core != x_lo)
    def _():
        plane_copy(0).start()

    @pl.loop(1, 16)
    def _(step):
        plane_copy(step).start()

    def window(own, whole_window, which):
        sems = [window_sems.at[which, kind] for kind in range(4)]
        return Window(own, whole_window, *sems, own_sems.at[which], dp, ctx)

    keys = window(key_ref, key_window, 0)
    values = window(value_own, value_window, 1)
    keys.start()
    saved_exchange = Exchange(
        staged,
        saved_slots,
        slot_sems.at[0],
        slot_sems.at[1],
        own_sems.at[2],
        dp,
        ctx,
        slice(0, D),
    )

    own_owner = lax.shift_right_logical(route_ref[pl.ds(ctx, 1)], 7)
    hit = own_owner == iota((CTX, ROWS), 0)
    count = jnp.dot(jnp.where(hit, 1.0, 0.0).astype(BF), before, preferred_element_type=F32)
    own_rank = jnp.sum(jnp.where(hit, count, 0.0), axis=0, keepdims=True).astype(jnp.int32)
    pack_ref[...] = one_hot(own_owner * CAP + own_rank, (SLOTS, ROWS))
    pack_turned[...] = nt_dot(same, pack_ref[...]).astype(BF)

    empty[...] = jnp.zeros_like(empty)
    for back in range(1, BACK + 1):

        @pl.when(chip < back)
        def _(back=back):
            hole = pl.ds((8 - 2 * back) * ROWS, 2 * ROWS)
            pltpu.sync_copy(empty, key_window.at[hole])
            pltpu.sync_copy(empty, value_window.at[hole])

    @pl.when(core == x_lo)
    def _():
        own_shard.wait()

    @pl.loop(0, CTX)
    def _(source):
        @pl.when(jnp.logical_or(core != x_lo, source != ctx))
        def _():
            shard_in = whole.at[rows_at(((core * Z + z) * CTX + source) * CAP, CAP)]
            remote(
                weight_ref, shard_in, plane_sems.at[0, 0], plane_sems.at[1, source], dp, other
            ).wait_recv()

    half = CHUNK // 2

    def piece(at_core, offset, part):
        start = (at_core * Z + (z + Z + offset) % Z) * CHUNK + part * half
        return whole.at[rows_at(start, half)]

    def up(step, part, offset):
        block = piece(core, offset, part)
        return remote(
            block, block, ring_sems.at[0, step, part], ring_sems.at[1, step, part], above, ctx
        )

    def down(step, part, offset):
        block = piece(core, offset, part)
        return remote(
            block, block, ring_sems.at[2, step, part], ring_sems.at[3, step, part], below, ctx
        )

    def pair(at_core, offset, part):
        block = piece(at_core, offset, part)
        index = offset + 3
        return remote(
            block, block, pair_sems.at[0, index, part], pair_sems.at[1, index, part], dp, other
        )

    for part in range(2):
        up(0, part, 0).start()
        down(0, part, 0).start()
        pair(core, 0, part).start()

    position = ctx * ROWS + iota((1, ROWS), 1)
    doc_start = jnp.zeros((1, ROWS), jnp.int32)
    doc_end = jnp.int32(0)
    for n in range(8):
        length = length_ref[0, n]
        doc_end = doc_end + length
        doc_start = doc_start + jnp.where(position >= doc_end, length, 0)
    left = iota((1, ROWS), 1) < VB

    for block in range(USED // VB):
        column = jnp.maximum(2 * ctx - 16 + block, 0)
        seen = jnp.where(left, visible_ref[2 * ctx, column], visible_ref[2 * ctx + 1, column])
        key_position = ctx * ROWS - 1024 + block * VB + iota((VB, ROWS), 0)
        allowed = (key_position >= doc_start) & (key_position <= position) & (seen == 1)
        bias[block * VB : (block + 1) * VB] = jnp.where(allowed, 0.0, -1e30)

    @pl.loop(0, QH)
    def _(head):
        load_query(head).wait()
        load_grad(head).wait()

    used = pl.ds(pl.multiple_of(core * ROWS, ROWS), USED)
    unused = pl.ds(pl.multiple_of((1 - core) * USED, ROWS), ROWS)
    key_terms[unused] = jnp.zeros((ROWS, KVW), BF)
    value_terms[unused] = jnp.zeros((ROWS, KVW), BF)

    def forward(group):
        columns = slice(group * HD, (group + 1) * HD)
        rows = slice(group * GROUP * HD, (group + 1) * GROUP * HD)

        @pl.loop(0, GROUP // 2)
        def _(two):
            for head in range(2):
                at = pl.multiple_of((group * GROUP + two * 2 + head) * HD, HD)
                scores = nt_dot(key_window[used, columns], queries[pl.ds(at, HD)]) + bias[...]
                top = jnp.max(scores, axis=0, keepdims=True)
                raised = jnp.exp((scores - top) * SCALE)
                weights = raised * (1.0 / jnp.sum(raised, axis=0, keepdims=True))
                weights_all[:, pl.ds(at, HD)] = weights.astype(BF)

        value_terms[used, columns] = jnp.dot(
            weights_all[:, rows], grads[rows], preferred_element_type=F32
        ).astype(BF)

    query_parts = []

    def backward(group):
        columns = slice(group * HD, (group + 1) * HD)
        rows = slice(group * GROUP * HD, (group + 1) * GROUP * HD)

        @pl.loop(0, GROUP // 2)
        def _(two):
            for head in range(2):
                index = group * GROUP + two * 2 + head
                at = pl.multiple_of(index * HD, HD)
                to = pl.multiple_of((two * 2 + head) * HD, HD)
                weights = weights_all[:, pl.ds(at, HD)].astype(F32)
                dweights = nt_dot(value_window[used, columns], grads[pl.ds(at, HD)])
                dscores_all[:, pl.ds(to, HD)] = (
                    (weights * SCALE)
                    * (dweights.astype(BF).astype(F32) - delta[pl.ds(index, 1)])
                ).astype(BF)

        key_terms[used, columns] = jnp.dot(
            dscores_all[...], queries[rows], preferred_element_type=F32
        ).astype(BF)
        keys_turned = nt_dot(same, key_window[used, columns]).astype(BF)
        query_grad = jnp.dot(
            keys_turned, dscores_all[...], preferred_element_type=F32
        ).astype(BF)
        for head in range(GROUP):
            at = (group * GROUP + head) * HD
            staged_grad[:, at : at + HD] = nt_dot(
                pack_ref[...], query_grad[:, head * HD : (head + 1) * HD]
            ).astype(BF)
        part = Exchange(
            staged_grad,
            query_slots,
            query_sems.at[0, group],
            query_sems.at[1, group],
            own_sems.at[4 + group],
            dp,
            ctx,
            rows,
        )
        part.start()
        query_parts.append(part)

    def ring(step):
        for part in range(2):
            up(step, part, -step - 1).wait_recv()
            if step < 2 or part == 0:
                up(step + 1, part, -step - 1).start()
            pair(core, -step - 1, part).start()
            down(step, part, step + 1).wait_recv()
            if step < 2 or part == 1:
                down(step + 1, part, step + 1).start()
            pair(core, step + 1, part).start()

    keys.hand_on()
    ring(0)
    keys.arrive()
    saved_exchange.start()
    forward(0)
    ring(1)
    forward(1)
    ring(2)
    forward(2)
    forward(3)

    def term_sum(which, terms, columns):
        gradient = min(which, 1)
        return Terms(
            terms,
            near_in.at[gradient],
            far_out.at[gradient],
            far_in.at[gradient],
            totals.at[gradient],
            [term_sems.at[which, kind] for kind in range(4)],
            dp,
            ctx,
            columns,
        )

    value_sum = term_sum(0, value_terms, slice(0, KVW))
    key_sums = [
        term_sum(1 + part, key_terms, slice(part * 256, (part + 1) * 256)) for part in range(2)
    ]
    value_sum.start()
    up(3, 0, 4).wait_recv()
    pair(core, 4, 0).start()
    down(3, 1, 4).wait_recv()
    pair(core, 4, 1).start()
    load_hidden.wait()
    for offset in range(-3, 5):
        for part in range(2):
            pair(1 - core, offset, part).wait_recv()
    value_own[...] = jnp.dot(hidden_ref[...], whole[...], preferred_element_type=F32).astype(BF)
    values.start()
    value_sum.send()
    diagonal = jnp.where(iota((CHUNK, CHUNK), 0) == iota((CHUNK, CHUNK), 1), 1.0, 0.0).astype(BF)
    for block in range(D // CHUNK):
        rows = slice(block * CHUNK, (block + 1) * CHUNK)
        turned[rows] = nt_dot(diagonal, hidden_ref[:, rows]).astype(BF)

    saved_exchange.finish()
    ones = jnp.ones((8, HD), BF)

    @pl.loop(0, QH // 4)
    def _(four):
        for head in range(4):
            index = four * 4 + head
            at = pl.ds(pl.multiple_of(index * HD, HD), HD)
            saved = jnp.dot(pack_turned[...], saved_slots[:, at], preferred_element_type=F32)
            product = saved * grads[at].astype(F32)
            high = product.astype(BF)
            low = (product - high.astype(F32)).astype(BF)
            delta[pl.ds(index, 1)] = (nt_dot(ones, high) + nt_dot(ones, low))[:1]

    values.hand_on()
    value_sum.add()
    value_grad[...] = totals[0].astype(BF)

    offsets = (4, 3, -3, 2, -2, 1, -1, 0)

    def partial_at(at_core, offset):
        start = (at_core * Z + (z + Z + offset) % Z) * CHUNK
        return jnp.dot(
            turned[rows_at(start, CHUNK)], value_grad[...], preferred_element_type=F32
        ).astype(BF)

    def pair_back(index):
        return remote(
            theirs.at[index],
            from_pair.at[index],
            pair_back_sems.at[0, index],
            pair_back_sems.at[1, index],
            dp,
            other,
        )

    for index, offset in enumerate(offsets):
        theirs[index] = partial_at(1 - core, offset)
        pair_back(index).start()
    for index, offset in enumerate(offsets):
        mine[index] = partial_at(core, offset)

    def spans(part):
        return slice(part * half, (part + 1) * half)

    def up_back(step, part):
        return remote(
            up_out.at[step, spans(part)],
            up_in.at[step, spans(part)],
            ring_back_sems.at[0, step, part],
            ring_back_sems.at[1, step, part],
            above,
            ctx,
        )

    def down_back(step, part):
        return remote(
            down_out.at[step, spans(part)],
            down_in.at[step, spans(part)],
            ring_back_sems.at[2, step, part],
            ring_back_sems.at[3, step, part],
            below,
            ctx,
        )

    def chip_sum(index, part):
        return mine[index, spans(part)].astype(F32) + from_pair[index, spans(part)].astype(F32)

    pair_back(0).wait_recv()
    up_out[0, spans(0)] = chip_sum(0, 0).astype(BF)
    up_back(0, 0).start()
    down_out[0, spans(1)] = chip_sum(0, 1).astype(BF)
    down_back(0, 1).start()

    def ring_back(step):
        pair_back(2 * step - 1).wait_recv()
        pair_back(2 * step).wait_recv()
        if step == 1:
            up_out[1, spans(1)] = chip_sum(1, 1).astype(BF)
            up_back(1, 1).start()
            down_out[1, spans(0)] = chip_sum(2, 0).astype(BF)
            down_back(1, 0).start()
        for index, ring, out, arrived, kept in (
            (2 * step - 1, up_back, up_out, up_in, 0),
            (2 * step, down_back, down_out, down_in, 1),
        ):
            for part in (kept,) if step == 1 else (1 - kept, kept):
                ring(step - 1, part).wait_recv()
                out[step, spans(part)] = (
                    chip_sum(index, part) + arrived[step - 1, spans(part)].astype(F32)
                ).astype(BF)
                ring(step, part).start()

    values.arrive()
    backward(0)
    ring_back(1)
    backward(1)
    key_sums[0].start()
    ring_back(2)
    key_sums[0].send()
    backward(2)
    ring_back(3)
    backward(3)
    key_sums[1].start()
    pair_back(7).wait_recv()
    for part in (0, 1):
        up_back(3, part).wait_recv()
        down_back(3, part).wait_recv()
        mine[7, spans(part)] = (
            chip_sum(7, part)
            + up_in[3, spans(part)].astype(F32)
            + down_in[3, spans(part)].astype(F32)
        ).astype(BF)

    plane = x_lo * 8 + chip

    def plane_back(step):
        to_ctx = (ctx + step) % CTX
        return remote(
            mine.at[7, rows_at(to_ctx * CAP, CAP)],
            plane_in.at[plane],
            plane_back_sems.at[0, step],
            plane_back_sems.at[1, plane],
            core * Z + z,
            to_ctx,
        )

    own_plane = pltpu.make_async_copy(
        mine.at[7, rows_at(ctx * CAP, CAP)], plane_in.at[plane], own_sems.at[3]
    )

    @pl.when(core == x_lo)
    def _():
        own_plane.start()

    @pl.when(core != x_lo)
    def _():
        plane_back(0).start()

    @pl.loop(1, CTX)
    def _(step):
        plane_back(step).start()

    key_sums[1].send()
    for group in range(KVH):
        columns = slice(group * 1024, (group + 1) * 1024)
        query_parts[group].finish()
        query_grad_ref[:, columns] = jnp.dot(
            owner_turned[...], query_slots[:, columns], preferred_element_type=F32
        ).astype(BF)
    for part in key_sums:
        part.add()
    key_grad_ref[...] = totals[1].astype(BF)

    @pl.when(core == x_lo)
    def _():
        own_plane.wait()

    @pl.loop(0, 16)
    def _(source):
        @pl.when(jnp.logical_or(core != x_lo, source != plane))
        def _():
            remote(
                mine.at[7, pl.ds(0, CAP)],
                plane_in.at[source],
                plane_back_sems.at[0, 0],
                plane_back_sems.at[1, source],
                dp,
                other,
            ).wait_recv()

    weight_sum = plane_in[0].astype(F32)
    for source in range(1, 16):
        weight_sum = weight_sum + plane_in[source].astype(F32)
    weight_grad_ref[...] = weight_sum * (1.0 / math.sqrt(32768.0))

    @pl.when(core != x_lo)
    def _():
        plane_copy(0).wait_send()
        plane_back(0).wait_send()

    @pl.loop(1, 16)
    def _(step):
        plane_copy(step).wait_send()
        plane_back(step).wait_send()

    for step in range(3):
        for part in range(2):
            up(step, part, -step).wait_send()
            down(step, part, step).wait_send()
    up(3, 0, -3).wait_send()
    down(3, 1, 3).wait_send()
    for offset in range(-3, 5):
        for part in range(2):
            pair(core, offset, part).wait_send()
    up_back(0, 0).wait_send()
    down_back(0, 1).wait_send()
    for step in range(1, 4):
        for part in range(2):
            up_back(step, part).wait_send()
            down_back(step, part).wait_send()
    for index in range(8):
        pair_back(index).wait_send()
    keys.finish()
    values.finish()
    for part in [value_sum] + key_sums:
        part.finish()


def local(
    hidden,
    value_weight,
    queries,
    key_rows,
    attn_saved,
    grad_out,
    doc_lengths,
    routing,
    visible_blocks,
):
    vmem = pl.BlockSpec(memory_space=pltpu.VMEM)
    smem = pl.BlockSpec(memory_space=pltpu.SMEM)
    hbm = pl.BlockSpec(memory_space=pltpu.HBM)
    dma = pltpu.SemaphoreType.DMA
    chunk = (CHUNK, KVW)
    blocks = (2, BACK + 1, ROWS, KVW)
    grad_query, grad_key, grad_weight = pl.pallas_call(
        kernel,
        out_shape=(
            jax.ShapeDtypeStruct((ROWS, D), BF),
            jax.ShapeDtypeStruct((ROWS, KVW), BF),
            jax.ShapeDtypeStruct((CAP, KVW), F32),
        ),
        in_specs=[smem, smem, hbm, hbm, hbm, hbm, vmem, hbm, hbm],
        out_specs=(vmem, vmem, vmem),
        scratch_shapes=[
            pltpu.VMEM((ROWS, D), BF),
            pltpu.VMEM((D, ROWS), BF),
            pltpu.VMEM((QH * HD, HD), BF),
            pltpu.VMEM((QH * HD, HD), BF),
            pltpu.VMEM((ROWS, D), BF),
            pltpu.VMEM((SLOTS, D), BF),
            pltpu.VMEM((SLOTS, D), BF),
            pltpu.VMEM((ROWS, SLOTS), BF),
            pltpu.VMEM((SLOTS, ROWS), BF),
            pltpu.VMEM((ROWS, SLOTS), BF),
            pltpu.VMEM((USED, ROWS), F32),
            pltpu.VMEM((QH, ROWS), F32),
            pltpu.VMEM((D, KVW), BF),
            pltpu.VMEM((ROWS, KVW), BF),
            pltpu.VMEM((2 * ROWS, KVW), BF),
            pltpu.VMEM((WIN, KVW), BF),
            pltpu.VMEM((WIN, KVW), BF),
            pltpu.VMEM((USED, QH * HD), BF),
            pltpu.VMEM((USED, GROUP * HD), BF),
            pltpu.VMEM((WIN, KVW), BF),
            pltpu.VMEM((WIN, KVW), BF),
            pltpu.VMEM((SLOTS, D), BF),
            pltpu.VMEM((SLOTS, D), BF),
            pltpu.VMEM(blocks, BF),
            pltpu.VMEM(blocks, BF),
            pltpu.VMEM(blocks, BF),
            pltpu.VMEM((2, ROWS, KVW), F32),
            pltpu.VMEM((ROWS, KVW), BF),
            pltpu.VMEM((8,) + chunk, BF),
            pltpu.VMEM((8,) + chunk, BF),
            pltpu.VMEM((8,) + chunk, BF),
            pltpu.VMEM((4,) + chunk, BF),
            pltpu.VMEM((4,) + chunk, BF),
            pltpu.VMEM((4,) + chunk, BF),
            pltpu.VMEM((4,) + chunk, BF),
            pltpu.VMEM((16, CAP, KVW), BF),
            dma((2,)),
            dma((2, QH)),
            dma((8,)),
            dma((2, 16)),
            dma((4, 4, 2)),
            dma((2, 8, 2)),
            dma((2, 4, BACK + 1)),
            dma((2, CTX)),
            dma((3, 4, BACK + 1)),
            dma((2, KVH, CTX)),
            dma((2, 8)),
            dma((4, 4, 2)),
            dma((2, 16)),
        ],
        compiler_params=pltpu.CompilerParams(
            has_side_effects=True, vmem_limit_bytes=60 * 1024 * 1024, collective_id=0
        ),
        name="attention_backward",
    )(
        doc_lengths,
        visible_blocks[0],
        value_weight,
        hidden[0],
        key_rows[0],
        attn_saved[0],
        routing.reshape(CTX, ROWS),
        queries[0],
        grad_out[0],
    )
    return (grad_query[None], grad_key[None], grad_weight)


def solution(mesh):
    return jax.shard_map(
        local,
        mesh=mesh,
        in_specs=(
            P("dp", "ctx", None),
            P(("dp", "ctx"), None),
            P("dp", "ctx", None),
            P("dp", "ctx", None),
            P("dp", "ctx", None),
            P("dp", "ctx", None),
            P("dp", None),
            P("dp", None),
            P("dp", None, None),
        ),
        out_specs=(P("dp", "ctx", None), P("dp", "ctx", None), P(("dp", "ctx"), None)),
        check_vma=False,
    )
```

```python
import math

import jax
import jax.numpy as jnp
from jax import lax
from jax.experimental import pallas as pl
from jax.experimental.pallas import tpu as pltpu
from jax.sharding import PartitionSpec as P

QH = 32
HD = 128
VB = 64
ROWS = 128
CTX = 16
CAP = 16
TOKENS = 2048
PAIR = 2 * HD
KVH = 4
Z = 8
D = 4096
KVW = 512
USED = 1152
CHUNK = 256
BF = jnp.bfloat16
F32 = jnp.float32
NT = (((1,), (1,)), ((), ()))
TN = (((0,), (0,)), ((), ()))
SCALE = 1.0 / math.sqrt(HD)


def remote(source, target, send_sem, recv_sem, dp, ctx):
    return pltpu.make_async_remote_copy(
        src_ref=source,
        dst_ref=target,
        send_sem=send_sem,
        recv_sem=recv_sem,
        device_id=(dp, ctx),
        device_id_type=pl.DeviceIdType.MESH,
    )


def rows_at(start, size):
    return pl.ds(pl.multiple_of(start, size), size)


def iota(shape, axis):
    return lax.broadcasted_iota(jnp.int32, shape, axis)


def nt_dot(first, second):
    return lax.dot_general(first, second, NT, preferred_element_type=F32)


def tn_dot(first, second):
    return lax.dot_general(first, second, TN, preferred_element_type=F32)


class Exchange:
    def __init__(self, source, target, sems, own_sem, dp, ctx):
        self.source, self.target = source, target
        self.sems, self.own_sem, self.dp, self.ctx = sems, own_sem, dp, ctx

    def copy(self, step):
        partner = (self.ctx + step) % CTX
        return remote(
            self.source(partner),
            self.target,
            self.sems.at[0, step],
            self.sems.at[1, step],
            self.dp,
            partner,
        )

    def own_copy(self):
        return pltpu.make_async_copy(self.source(self.ctx), self.target, self.own_sem)

    def start(self):
        self.own_copy().start()

        @pl.loop(1, CTX)
        def _(step):
            self.copy(step).start()

    def arrive(self):
        self.own_copy().wait()

        @pl.loop(1, CTX)
        def _(step):
            self.copy(step).wait_recv()

    def finish(self):
        @pl.loop(1, CTX)
        def _(step):
            self.copy(step).wait_send()


def plane_partner(dp, ctx, step):
    chip = ((dp // Z) * 8 + ctx // 2 + step) % 16
    return (chip // 8) * Z + dp % Z, (chip % 8) * 2 + dp // Z


def kernel(
    length_ref,
    visible_ref,
    weight_ref,
    hidden_hbm,
    key_hbm,
    saved_hbm,
    route_ref,
    query_hbm,
    grad_hbm,
    query_grad_ref,
    key_grad_ref,
    weight_grad_ref,
    hidden_ref,
    turned,
    queries,
    grads,
    saved,
    keys,
    keys_turned,
    values,
    to_owner,
    bias,
    delta,
    whole,
    value_own,
    weights_all,
    key_terms,
    value_terms,
    key_rounded,
    value_rounded,
    query_rows,
    query_owned,
    key_in,
    value_in,
    value_grad,
    mine,
    theirs,
    from_pair,
    up_in,
    down_in,
    up_out,
    down_out,
    plane_in,
    load_sem,
    own_sems,
    plane_sems,
    ring_sems,
    pair_sems,
    exchange_sems,
    pair_back_sems,
    ring_back_sems,
    plane_back_sems,
):
    dp, ctx = lax.axis_index("dp"), lax.axis_index("ctx")
    x_lo, z = dp // Z, dp % Z
    chip, core = ctx // 2, ctx % 2
    other = ctx + 1 - 2 * core
    above, below = x_lo * Z + (z + 1) % Z, x_lo * Z + (z + Z - 1) % Z

    load_hidden = pltpu.make_async_copy(hidden_hbm, hidden_ref, load_sem)
    load_hidden.start()

    barrier = pltpu.get_barrier_semaphore()

    def greet(to_dp, to_ctx):
        pl.semaphore_signal(
            barrier, inc=1, device_id=(to_dp, to_ctx), device_id_type=pl.DeviceIdType.MESH
        )

    greet(above, ctx)
    greet(below, ctx)

    @pl.loop(1, CTX)
    def _(step):
        greet(dp, (ctx + step) % CTX)
        greet(*plane_partner(dp, ctx, step))
        greet(core * Z + z, (ctx + step) % CTX)

    @pl.when(core != x_lo)
    def _():
        greet(*plane_partner(dp, ctx, 0))
        greet(core * Z + z, ctx)

    same = jnp.where(iota((ROWS, ROWS), 0) == iota((ROWS, ROWS), 1), 1.0, 0.0).astype(BF)
    diagonal = jnp.where(iota((CHUNK, CHUNK), 0) == iota((CHUNK, CHUNK), 1), 1.0, 0.0).astype(BF)
    left = iota((1, ROWS), 1) < VB

    @pl.loop(0, CTX)
    def _(block):
        to_owner[:, rows_at(block * ROWS, ROWS)] = jnp.where(
            route_ref[pl.ds(block, 1)] == iota((TOKENS, ROWS), 0), 1.0, 0.0
        ).astype(BF)

    key_terms[...] = jnp.zeros_like(key_terms)
    value_terms[...] = jnp.zeros_like(value_terms)
    pl.semaphore_wait(barrier, 2 + 3 * (CTX - 1) + jnp.where(core != x_lo, 2, 0))

    shard = whole.at[rows_at((dp * CTX + ctx) * CAP, CAP)]

    def plane_copy(step):
        to_dp, to_ctx = plane_partner(dp, ctx, step)
        return remote(
            weight_ref, shard, plane_sems.at[0, step], plane_sems.at[1, ctx], to_dp, to_ctx
        )

    own_shard = pltpu.make_async_copy(weight_ref, shard, own_sems.at[3])

    @pl.when(core == x_lo)
    def _():
        own_shard.start()

    @pl.when(core != x_lo)
    def _():
        plane_copy(0).start()

    @pl.loop(1, 16)
    def _(step):
        plane_copy(step).start()

    def wide(index, width):
        return pl.ds(pl.multiple_of(index * width, width), width)

    here = rows_at(ctx * ROWS, ROWS)

    def exchange(which, source, target):
        return Exchange(source, target, exchange_sems.at[which], own_sems.at[4 + which], dp, ctx)

    key_move = exchange(0, lambda to: key_hbm.at[:, wide(to // 4, HD)], keys.at[here])
    query_move = exchange(1, lambda to: query_hbm.at[:, wide(to, PAIR)], queries.at[here])
    grad_move = exchange(2, lambda to: grad_hbm.at[:, wide(to, PAIR)], grads.at[here])
    saved_move = exchange(3, lambda to: saved_hbm.at[:, wide(to, PAIR)], saved.at[here])
    value_move = exchange(4, lambda to: value_own.at[:, wide(to // 4, HD)], values.at[here])
    value_back = exchange(5, lambda to: value_rounded.at[rows_at(to * ROWS, ROWS)], value_in.at[ctx])
    key_back = exchange(6, lambda to: key_rounded.at[rows_at(to * ROWS, ROWS)], key_in.at[ctx])
    query_back = exchange(
        7, lambda to: query_owned.at[rows_at(to * ROWS, ROWS)], query_grad_ref.at[:, wide(ctx, PAIR)]
    )
    key_move.start()
    query_move.start()

    @pl.when(core == x_lo)
    def _():
        own_shard.wait()

    @pl.loop(0, CTX)
    def _(source):
        @pl.when(jnp.logical_or(core != x_lo, source != ctx))
        def _():
            shard_in = whole.at[rows_at(((core * Z + z) * CTX + source) * CAP, CAP)]
            remote(
                weight_ref, shard_in, plane_sems.at[0, 0], plane_sems.at[1, source], dp, other
            ).wait_recv()

    half = CHUNK // 2

    def piece(at_core, offset, part):
        start = (at_core * Z + (z + Z + offset) % Z) * CHUNK + part * half
        return whole.at[rows_at(start, half)]

    def up(step, part, offset):
        block = piece(core, offset, part)
        return remote(
            block, block, ring_sems.at[0, step, part], ring_sems.at[1, step, part], above, ctx
        )

    def down(step, part, offset):
        block = piece(core, offset, part)
        return remote(
            block, block, ring_sems.at[2, step, part], ring_sems.at[3, step, part], below, ctx
        )

    def pair(at_core, offset, part):
        block = piece(at_core, offset, part)
        index = offset + 3
        return remote(
            block, block, pair_sems.at[0, index, part], pair_sems.at[1, index, part], dp, other
        )

    for part in range(2):
        up(0, part, 0).start()
        down(0, part, 0).start()
        pair(core, 0, part).start()

    def ring(step):
        for part in range(2):
            up(step, part, -step - 1).wait_recv()
            if step < 2 or part == 0:
                up(step + 1, part, -step - 1).start()
            pair(core, -step - 1, part).start()
            down(step, part, step + 1).wait_recv()
            if step < 2 or part == 1:
                down(step + 1, part, step + 1).start()
            pair(core, step + 1, part).start()

    quarters = ((0, 512), (4, 1024), (8, USED), (12, USED))

    def first_block(quarter, block):
        return block - 8 if quarter >= 2 else jnp.int32(0)

    def stacked(pairs, block):
        rows = rows_at(block * ROWS, ROWS)
        return jnp.concatenate([pairs[rows, :HD], pairs[rows, HD:]], axis=0)

    def forward(quarter):
        first, size = quarters[quarter]

        @pl.loop(first, first + 4)
        def _(block):
            base = first_block(quarter, block)
            position = block * ROWS + iota((1, ROWS), 1)
            doc_start = jnp.zeros((1, ROWS), jnp.int32)
            doc_end = jnp.int32(0)
            for n in range(8):
                length = length_ref[0, n]
                doc_end = doc_end + length
                doc_start = doc_start + jnp.where(position >= doc_end, length, 0)
            for part in range(size // VB):
                column = 2 * base + part
                seen = jnp.where(
                    left, visible_ref[2 * block, column], visible_ref[2 * block + 1, column]
                )
                key_position = column * VB + iota((VB, ROWS), 0)
                allowed = (
                    (key_position >= doc_start) & (key_position <= position) & (seen == 1)
                )
                bias[part * VB : (part + 1) * VB] = jnp.where(allowed, 0.0, -1e30)
            window = pl.ds(pl.multiple_of(base * ROWS, ROWS), size)
            scores = nt_dot(keys[window], stacked(queries, block))
            scores = scores + jnp.concatenate([bias[:size], bias[:size]], axis=1)
            top = jnp.max(scores, axis=0, keepdims=True)
            raised = jnp.exp((scores - top) * SCALE)
            weights = raised * (1.0 / jnp.sum(raised, axis=0, keepdims=True))
            weights_all[pl.ds(pl.multiple_of(block * USED, ROWS), size)] = weights.astype(BF)

    def value_part(quarter):
        first, size = quarters[quarter]

        @pl.loop(first, first + 4)
        def _(block):
            window = pl.ds(pl.multiple_of(first_block(quarter, block) * ROWS, ROWS), size)
            stored = pl.ds(pl.multiple_of(block * USED, ROWS), size)
            value_terms[window] += jnp.dot(
                weights_all[stored], stacked(grads, block), preferred_element_type=F32
            )

    def backward(quarter):
        first, size = quarters[quarter]

        @pl.loop(first, first + 4)
        def _(block):
            window = pl.ds(pl.multiple_of(first_block(quarter, block) * ROWS, ROWS), size)
            stored = pl.ds(pl.multiple_of(block * USED, ROWS), size)
            rows = rows_at(block * ROWS, ROWS)
            weights = weights_all[stored].astype(F32)
            dweights = nt_dot(values[window], stacked(grads, block))
            row_delta = jnp.concatenate([delta[:1, rows], delta[1:, rows]], axis=1)
            dscores = (
                (weights * SCALE) * (dweights.astype(BF).astype(F32) - row_delta)
            ).astype(BF)
            key_terms[window] += jnp.dot(
                dscores, stacked(queries, block), preferred_element_type=F32
            )
            query_turned = jnp.dot(
                keys_turned[:, window], dscores, preferred_element_type=F32
            ).astype(BF)
            for head in range(2):
                columns = slice(head * HD, (head + 1) * HD)
                query_rows[rows, columns] = nt_dot(same, query_turned[:, columns]).astype(BF)

    def own_rows():
        @pl.loop(0, TOKENS // CHUNK)
        def _(block):
            rows = rows_at(block * CHUNK, CHUNK)
            query_owned[rows] = jnp.dot(
                to_owner[rows], query_rows[...], preferred_element_type=F32
            ).astype(BF)

        query_back.start()

    key_move.arrive()
    keys_turned[...] = nt_dot(same, keys[...]).astype(BF)
    ring(0)
    ring(1)
    grad_move.start()
    query_move.arrive()
    forward(0)
    ring(2)
    load_hidden.wait()
    forward(1)
    forward(2)
    up(3, 0, 4).wait_recv()
    pair(core, 4, 0).start()
    down(3, 1, 4).wait_recv()
    pair(core, 4, 1).start()
    for offset in range(-3, 5):
        for part in range(2):
            pair(1 - core, offset, part).wait_recv()
    value_own[...] = jnp.dot(hidden_ref[...], whole[...], preferred_element_type=F32).astype(BF)
    value_move.start()
    forward(3)
    grad_move.arrive()
    for quarter in range(4):
        value_part(quarter)
    value_rounded[...] = value_terms[...].astype(BF)
    value_back.start()
    saved_move.start()
    for block in range(D // CHUNK):
        rows = slice(block * CHUNK, (block + 1) * CHUNK)
        turned[rows] = nt_dot(diagonal, hidden_ref[:, rows]).astype(BF)

    def four(arrived, group):
        total = arrived[4 * group].astype(F32)
        for part in range(1, 4):
            total = total + arrived[4 * group + part].astype(F32)
        return total.astype(BF)

    value_back.arrive()
    for group in range(KVH):
        value_grad[:, group * HD : (group + 1) * HD] = four(value_in, group)

    offsets = (4, 3, -3, 2, -2, 1, -1, 0)

    def partial_at(at_core, offset):
        start = (at_core * Z + (z + Z + offset) % Z) * CHUNK
        return jnp.dot(
            turned[rows_at(start, CHUNK)], value_grad[...], preferred_element_type=F32
        ).astype(BF)

    def pair_back(index):
        return remote(
            theirs.at[index],
            from_pair.at[index],
            pair_back_sems.at[0, index],
            pair_back_sems.at[1, index],
            dp,
            other,
        )

    for index, offset in enumerate(offsets):
        theirs[index] = partial_at(1 - core, offset)
        pair_back(index).start()
    for index, offset in enumerate(offsets):
        mine[index] = partial_at(core, offset)

    def spans(part):
        return slice(part * half, (part + 1) * half)

    def up_back(step, part):
        return remote(
            up_out.at[step, spans(part)],
            up_in.at[step, spans(part)],
            ring_back_sems.at[0, step, part],
            ring_back_sems.at[1, step, part],
            above,
            ctx,
        )

    def down_back(step, part):
        return remote(
            down_out.at[step, spans(part)],
            down_in.at[step, spans(part)],
            ring_back_sems.at[2, step, part],
            ring_back_sems.at[3, step, part],
            below,
            ctx,
        )

    def chip_sum(index, part):
        return mine[index, spans(part)].astype(F32) + from_pair[index, spans(part)].astype(F32)

    pair_back(0).wait_recv()
    up_out[0, spans(0)] = chip_sum(0, 0).astype(BF)
    up_back(0, 0).start()
    down_out[0, spans(1)] = chip_sum(0, 1).astype(BF)
    down_back(0, 1).start()

    def ring_back(step):
        pair_back(2 * step - 1).wait_recv()
        pair_back(2 * step).wait_recv()
        if step == 1:
            up_out[1, spans(1)] = chip_sum(1, 1).astype(BF)
            up_back(1, 1).start()
            down_out[1, spans(0)] = chip_sum(2, 0).astype(BF)
            down_back(1, 0).start()
        for index, ring, out, arrived, kept in (
            (2 * step - 1, up_back, up_out, up_in, 0),
            (2 * step, down_back, down_out, down_in, 1),
        ):
            for part in (kept,) if step == 1 else (1 - kept, kept):
                ring(step - 1, part).wait_recv()
                out[step, spans(part)] = (
                    chip_sum(index, part) + arrived[step - 1, spans(part)].astype(F32)
                ).astype(BF)
                ring(step, part).start()

    saved_move.arrive()
    saved_turned = nt_dot(diagonal, saved[...]).astype(BF)

    @pl.loop(0, TOKENS // CHUNK)
    def _(block):
        rows = rows_at(block * CHUNK, CHUNK)
        product = jnp.dot(
            saved_turned, to_owner[:, rows], preferred_element_type=F32
        ) * nt_dot(diagonal, grads[rows])
        for head in range(2):
            delta[head : head + 1, rows] = jnp.sum(
                product[head * HD : (head + 1) * HD], axis=0, keepdims=True
            )

    ring_back(1)
    value_move.arrive()
    backward(0)
    backward(1)
    ring_back(2)
    backward(2)
    backward(3)
    key_rounded[...] = key_terms[...].astype(BF)
    key_back.start()
    ring_back(3)
    own_rows()
    pair_back(7).wait_recv()
    for part in (0, 1):
        up_back(3, part).wait_recv()
        down_back(3, part).wait_recv()
        mine[7, spans(part)] = (
            chip_sum(7, part)
            + up_in[3, spans(part)].astype(F32)
            + down_in[3, spans(part)].astype(F32)
        ).astype(BF)

    plane = x_lo * 8 + chip

    def plane_back(step):
        to_ctx = (ctx + step) % CTX
        return remote(
            mine.at[7, rows_at(to_ctx * CAP, CAP)],
            plane_in.at[plane],
            plane_back_sems.at[0, step],
            plane_back_sems.at[1, plane],
            core * Z + z,
            to_ctx,
        )

    own_plane = pltpu.make_async_copy(
        mine.at[7, rows_at(ctx * CAP, CAP)], plane_in.at[plane], own_sems.at[3]
    )

    @pl.when(core == x_lo)
    def _():
        own_plane.start()

    @pl.when(core != x_lo)
    def _():
        plane_back(0).start()

    @pl.loop(1, CTX)
    def _(step):
        plane_back(step).start()

    key_back.arrive()
    for group in range(KVH):
        key_grad_ref[:, group * HD : (group + 1) * HD] = four(key_in, group)

    @pl.when(core == x_lo)
    def _():
        own_plane.wait()

    @pl.loop(0, 16)
    def _(source):
        @pl.when(jnp.logical_or(core != x_lo, source != plane))
        def _():
            remote(
                mine.at[7, pl.ds(0, CAP)],
                plane_in.at[source],
                plane_back_sems.at[0, 0],
                plane_back_sems.at[1, source],
                dp,
                other,
            ).wait_recv()

    weight_sum = plane_in[0].astype(F32)
    for source in range(1, 16):
        weight_sum = weight_sum + plane_in[source].astype(F32)
    weight_grad_ref[...] = weight_sum * (1.0 / math.sqrt(32768.0))

    @pl.when(core != x_lo)
    def _():
        plane_copy(0).wait_send()
        plane_back(0).wait_send()

    @pl.loop(1, 16)
    def _(step):
        plane_copy(step).wait_send()
        plane_back(step).wait_send()

    for step in range(3):
        for part in range(2):
            up(step, part, -step).wait_send()
            down(step, part, step).wait_send()
    up(3, 0, -3).wait_send()
    down(3, 1, 3).wait_send()
    for offset in range(-3, 5):
        for part in range(2):
            pair(core, offset, part).wait_send()
    up_back(0, 0).wait_send()
    down_back(0, 1).wait_send()
    for step in range(1, 4):
        for part in range(2):
            up_back(step, part).wait_send()
            down_back(step, part).wait_send()
    for index in range(8):
        pair_back(index).wait_send()
    query_back.arrive()
    for part in (
        key_move,
        query_move,
        grad_move,
        saved_move,
        value_move,
        value_back,
        key_back,
        query_back,
    ):
        part.finish()


def local(
    hidden,
    value_weight,
    queries,
    key_rows,
    attn_saved,
    grad_out,
    doc_lengths,
    routing,
    visible_blocks,
):
    vmem = pl.BlockSpec(memory_space=pltpu.VMEM)
    smem = pl.BlockSpec(memory_space=pltpu.SMEM)
    hbm = pl.BlockSpec(memory_space=pltpu.HBM)
    dma = pltpu.SemaphoreType.DMA
    chunk = (CHUNK, KVW)
    grad_query, grad_key, grad_weight = pl.pallas_call(
        kernel,
        out_shape=(
            jax.ShapeDtypeStruct((ROWS, D), BF),
            jax.ShapeDtypeStruct((ROWS, KVW), BF),
            jax.ShapeDtypeStruct((CAP, KVW), F32),
        ),
        in_specs=[smem, smem, hbm, hbm, hbm, hbm, vmem, hbm, hbm],
        out_specs=(vmem, vmem, vmem),
        scratch_shapes=[
            pltpu.VMEM((ROWS, D), BF),
            pltpu.VMEM((D, ROWS), BF),
            pltpu.VMEM((TOKENS, PAIR), BF),
            pltpu.VMEM((TOKENS, PAIR), BF),
            pltpu.VMEM((TOKENS, PAIR), BF),
            pltpu.VMEM((TOKENS, HD), BF),
            pltpu.VMEM((HD, TOKENS), BF),
            pltpu.VMEM((TOKENS, HD), BF),
            pltpu.VMEM((TOKENS, TOKENS), BF),
            pltpu.VMEM((USED, ROWS), F32),
            pltpu.VMEM((2, TOKENS), F32),
            pltpu.VMEM((D, KVW), BF),
            pltpu.VMEM((ROWS, KVW), BF),
            pltpu.VMEM((CTX * USED, PAIR), BF),
            pltpu.VMEM((TOKENS, HD), F32),
            pltpu.VMEM((TOKENS, HD), F32),
            pltpu.VMEM((TOKENS, HD), BF),
            pltpu.VMEM((TOKENS, HD), BF),
            pltpu.VMEM((TOKENS, PAIR), BF),
            pltpu.VMEM((TOKENS, PAIR), BF),
            pltpu.VMEM((CTX, ROWS, HD), BF),
            pltpu.VMEM((CTX, ROWS, HD), BF),
            pltpu.VMEM((ROWS, KVW), BF),
            pltpu.VMEM((8,) + chunk, BF),
            pltpu.VMEM((8,) + chunk, BF),
            pltpu.VMEM((8,) + chunk, BF),
            pltpu.VMEM((4,) + chunk, BF),
            pltpu.VMEM((4,) + chunk, BF),
            pltpu.VMEM((4,) + chunk, BF),
            pltpu.VMEM((4,) + chunk, BF),
            pltpu.VMEM((16, CAP, KVW), BF),
            dma,
            dma((12,)),
            dma((2, 16)),
            dma((4, 4, 2)),
            dma((2, 8, 2)),
            dma((8, 2, CTX)),
            dma((2, 8)),
            dma((4, 4, 2)),
            dma((2, 16)),
        ],
        compiler_params=pltpu.CompilerParams(
            has_side_effects=True, vmem_limit_bytes=60 * 1024 * 1024, collective_id=0
        ),
        name="attention_backward",
    )(
        doc_lengths,
        visible_blocks[0],
        value_weight,
        hidden[0],
        key_rows[0],
        attn_saved[0],
        routing.reshape(CTX, ROWS),
        queries[0],
        grad_out[0],
    )
    return (grad_query[None], grad_key[None], grad_weight)


def solution(mesh):
    return jax.shard_map(
        local,
        mesh=mesh,
        in_specs=(
            P("dp", "ctx", None),
            P(("dp", "ctx"), None),
            P("dp", "ctx", None),
            P("dp", "ctx", None),
            P("dp", "ctx", None),
            P("dp", "ctx", None),
            P("dp", None),
            P("dp", None),
            P("dp", None, None),
        ),
        out_specs=(P("dp", "ctx", None), P("dp", "ctx", None), P(("dp", "ctx"), None)),
        check_vma=False,
    )
```

```python
import math

import jax
import jax.numpy as jnp
from jax import lax
from jax.experimental import pallas as pl
from jax.experimental.pallas import tpu as pltpu
from jax.sharding import PartitionSpec as P

QH = 32
HD = 128
VB = 64
ROWS = 128
CTX = 16
CAP = 16
TOKENS = 2048
PAIR = 2 * HD
KVH = 4
Z = 8
D = 4096
KVW = 512
USED = 1152
CHUNK = 256
BF = jnp.bfloat16
F32 = jnp.float32
NT = (((1,), (1,)), ((), ()))
TN = (((0,), (0,)), ((), ()))
SCALE = 1.0 / math.sqrt(HD)


def remote(source, target, send_sem, recv_sem, dp, ctx):
    return pltpu.make_async_remote_copy(
        src_ref=source,
        dst_ref=target,
        send_sem=send_sem,
        recv_sem=recv_sem,
        device_id=(dp, ctx),
        device_id_type=pl.DeviceIdType.MESH,
    )


def rows_at(start, size):
    return pl.ds(pl.multiple_of(start, size), size)


def iota(shape, axis):
    return lax.broadcasted_iota(jnp.int32, shape, axis)


def nt_dot(first, second):
    return lax.dot_general(first, second, NT, preferred_element_type=F32)


def tn_dot(first, second):
    return lax.dot_general(first, second, TN, preferred_element_type=F32)


class Exchange:
    def __init__(self, source, target, sems, own_sem, dp, ctx):
        self.source, self.target = source, target
        self.sems, self.own_sem, self.dp, self.ctx = sems, own_sem, dp, ctx

    def copy(self, step):
        partner = (self.ctx + step) % CTX
        return remote(
            self.source(partner),
            self.target,
            self.sems.at[0, step],
            self.sems.at[1, step],
            self.dp,
            partner,
        )

    def own_copy(self):
        return pltpu.make_async_copy(self.source(self.ctx), self.target, self.own_sem)

    def start(self):
        self.own_copy().start()

        @pl.loop(1, CTX)
        def _(step):
            self.copy(step).start()

    def arrive(self):
        self.own_copy().wait()

        @pl.loop(1, CTX)
        def _(step):
            self.copy(step).wait_recv()

    def finish(self):
        @pl.loop(1, CTX)
        def _(step):
            self.copy(step).wait_send()


def plane_partner(dp, ctx, step):
    chip = ((dp // Z) * 8 + ctx // 2 + step) % 16
    return (chip // 8) * Z + dp % Z, (chip % 8) * 2 + dp // Z


def kernel(
    length_ref,
    visible_ref,
    weight_ref,
    hidden_hbm,
    key_hbm,
    saved_hbm,
    route_ref,
    query_hbm,
    grad_hbm,
    query_grad_ref,
    key_grad_ref,
    weight_grad_ref,
    hidden_ref,
    turned,
    queries,
    grads,
    saved,
    keys,
    keys_turned,
    values,
    to_owner,
    bias,
    delta,
    whole,
    value_own,
    weights_all,
    key_terms,
    value_terms,
    key_rounded,
    value_rounded,
    query_rows,
    query_owned,
    key_in,
    value_in,
    value_grad,
    mine,
    theirs,
    from_pair,
    up_in,
    down_in,
    up_out,
    down_out,
    plane_in,
    load_sem,
    own_sems,
    plane_sems,
    ring_sems,
    pair_sems,
    exchange_sems,
    pair_back_sems,
    ring_back_sems,
    plane_back_sems,
):
    dp, ctx = lax.axis_index("dp"), lax.axis_index("ctx")
    x_lo, z = dp // Z, dp % Z
    chip, core = ctx // 2, ctx % 2
    other = ctx + 1 - 2 * core
    above, below = x_lo * Z + (z + 1) % Z, x_lo * Z + (z + Z - 1) % Z

    load_hidden = pltpu.make_async_copy(hidden_hbm, hidden_ref, load_sem)
    load_hidden.start()

    barrier = pltpu.get_barrier_semaphore()

    def greet(to_dp, to_ctx):
        pl.semaphore_signal(
            barrier, inc=1, device_id=(to_dp, to_ctx), device_id_type=pl.DeviceIdType.MESH
        )

    greet(above, ctx)
    greet(below, ctx)

    @pl.loop(1, CTX)
    def _(step):
        greet(dp, (ctx + step) % CTX)
        greet(*plane_partner(dp, ctx, step))
        greet(core * Z + z, (ctx + step) % CTX)

    @pl.when(core != x_lo)
    def _():
        greet(*plane_partner(dp, ctx, 0))
        greet(core * Z + z, ctx)

    same = jnp.where(iota((ROWS, ROWS), 0) == iota((ROWS, ROWS), 1), 1.0, 0.0).astype(BF)
    diagonal = jnp.where(iota((CHUNK, CHUNK), 0) == iota((CHUNK, CHUNK), 1), 1.0, 0.0).astype(BF)
    left = iota((1, ROWS), 1) < VB

    @pl.loop(0, CTX)
    def _(block):
        to_owner[:, rows_at(block * ROWS, ROWS)] = jnp.where(
            route_ref[pl.ds(block, 1)] == iota((TOKENS, ROWS), 0), 1.0, 0.0
        ).astype(BF)

    key_terms[...] = jnp.zeros_like(key_terms)
    value_terms[...] = jnp.zeros_like(value_terms)
    pl.semaphore_wait(barrier, 2 + 3 * (CTX - 1) + jnp.where(core != x_lo, 2, 0))

    shard = whole.at[rows_at((dp * CTX + ctx) * CAP, CAP)]

    def plane_copy(step):
        to_dp, to_ctx = plane_partner(dp, ctx, step)
        return remote(
            weight_ref, shard, plane_sems.at[0, step], plane_sems.at[1, ctx], to_dp, to_ctx
        )

    own_shard = pltpu.make_async_copy(weight_ref, shard, own_sems.at[3])

    @pl.when(core == x_lo)
    def _():
        own_shard.start()

    @pl.when(core != x_lo)
    def _():
        plane_copy(0).start()

    @pl.loop(1, 16)
    def _(step):
        plane_copy(step).start()

    def wide(index, width):
        return pl.ds(pl.multiple_of(index * width, width), width)

    here = rows_at(ctx * ROWS, ROWS)

    def exchange(which, source, target):
        return Exchange(source, target, exchange_sems.at[which], own_sems.at[4 + which], dp, ctx)

    key_move = exchange(0, lambda to: key_hbm.at[:, wide(to // 4, HD)], keys.at[here])
    query_move = exchange(1, lambda to: query_hbm.at[:, wide(to, PAIR)], queries.at[here])
    grad_move = exchange(2, lambda to: grad_hbm.at[:, wide(to, PAIR)], grads.at[here])
    saved_move = exchange(3, lambda to: saved_hbm.at[:, wide(to, PAIR)], saved.at[here])
    value_move = exchange(4, lambda to: value_own.at[:, wide(to // 4, HD)], values.at[here])
    value_back = exchange(5, lambda to: value_rounded.at[rows_at(to * ROWS, ROWS)], value_in.at[ctx])
    key_back = exchange(6, lambda to: key_rounded.at[rows_at(to * ROWS, ROWS)], key_in.at[ctx])
    query_back = exchange(
        7, lambda to: query_owned.at[rows_at(to * ROWS, ROWS)], query_grad_ref.at[:, wide(ctx, PAIR)]
    )
    key_move.start()
    query_move.start()

    @pl.when(core == x_lo)
    def _():
        own_shard.wait()

    @pl.loop(0, CTX)
    def _(source):
        @pl.when(jnp.logical_or(core != x_lo, source != ctx))
        def _():
            shard_in = whole.at[rows_at(((core * Z + z) * CTX + source) * CAP, CAP)]
            remote(
                weight_ref, shard_in, plane_sems.at[0, 0], plane_sems.at[1, source], dp, other
            ).wait_recv()

    half = CHUNK // 2

    def piece(at_core, offset, part):
        start = (at_core * Z + (z + Z + offset) % Z) * CHUNK + part * half
        return whole.at[rows_at(start, half)]

    def up(step, part, offset):
        block = piece(core, offset, part)
        return remote(
            block, block, ring_sems.at[0, step, part], ring_sems.at[1, step, part], above, ctx
        )

    def down(step, part, offset):
        block = piece(core, offset, part)
        return remote(
            block, block, ring_sems.at[2, step, part], ring_sems.at[3, step, part], below, ctx
        )

    def pair(at_core, offset, part):
        block = piece(at_core, offset, part)
        index = offset + 3
        return remote(
            block, block, pair_sems.at[0, index, part], pair_sems.at[1, index, part], dp, other
        )

    for part in range(2):
        up(0, part, 0).start()
        down(0, part, 0).start()
        pair(core, 0, part).start()

    def ring(step):
        for part in range(2):
            up(step, part, -step - 1).wait_recv()
            if step < 2 or part == 0:
                up(step + 1, part, -step - 1).start()
            pair(core, -step - 1, part).start()
            down(step, part, step + 1).wait_recv()
            if step < 2 or part == 1:
                down(step + 1, part, step + 1).start()
            pair(core, step + 1, part).start()

    quarters = ((0, 512), (4, 1024), (8, USED), (12, USED))

    def first_block(quarter, block):
        return block - 8 if quarter >= 2 else jnp.int32(0)

    def stacked(pairs, block):
        rows = rows_at(block * ROWS, ROWS)
        return jnp.concatenate([pairs[rows, :HD], pairs[rows, HD:]], axis=0)

    def forward(quarter):
        first, size = quarters[quarter]

        @pl.loop(first, first + 4)
        def _(block):
            base = first_block(quarter, block)
            position = block * ROWS + iota((1, ROWS), 1)
            doc_start = jnp.zeros((1, ROWS), jnp.int32)
            doc_end = jnp.int32(0)
            for n in range(8):
                length = length_ref[0, n]
                doc_end = doc_end + length
                doc_start = doc_start + jnp.where(position >= doc_end, length, 0)
            for part in range(size // VB):
                column = 2 * base + part
                seen = jnp.where(
                    left, visible_ref[2 * block, column], visible_ref[2 * block + 1, column]
                )
                key_position = column * VB + iota((VB, ROWS), 0)
                allowed = (
                    (key_position >= doc_start) & (key_position <= position) & (seen == 1)
                )
                bias[part * VB : (part + 1) * VB] = jnp.where(allowed, 0.0, -1e30)
            window = pl.ds(pl.multiple_of(base * ROWS, ROWS), size)
            scores = nt_dot(keys[window], stacked(queries, block))
            scores = scores + jnp.concatenate([bias[:size], bias[:size]], axis=1)
            top = jnp.max(scores, axis=0, keepdims=True)
            raised = jnp.exp((scores - top) * SCALE)
            weights = raised * (1.0 / jnp.sum(raised, axis=0, keepdims=True))
            weights_all[pl.ds(pl.multiple_of(block * USED, ROWS), size)] = weights.astype(BF)

    def value_part(quarter):
        first, size = quarters[quarter]

        @pl.loop(first, first + 4)
        def _(block):
            window = pl.ds(pl.multiple_of(first_block(quarter, block) * ROWS, ROWS), size)
            stored = pl.ds(pl.multiple_of(block * USED, ROWS), size)
            value_terms[window] += jnp.dot(
                weights_all[stored], stacked(grads, block), preferred_element_type=F32
            )

    def backward(quarter):
        first, size = quarters[quarter]

        @pl.loop(first, first + 4)
        def _(block):
            window = pl.ds(pl.multiple_of(first_block(quarter, block) * ROWS, ROWS), size)
            stored = pl.ds(pl.multiple_of(block * USED, ROWS), size)
            rows = rows_at(block * ROWS, ROWS)
            weights = weights_all[stored].astype(F32)
            dweights = nt_dot(values[window], stacked(grads, block))
            row_delta = jnp.concatenate([delta[:1, rows], delta[1:, rows]], axis=1)
            dscores = (
                (weights * SCALE) * (dweights.astype(BF).astype(F32) - row_delta)
            ).astype(BF)
            key_terms[window] += jnp.dot(
                dscores, stacked(queries, block), preferred_element_type=F32
            )
            query_turned = jnp.dot(
                keys_turned[:, window], dscores, preferred_element_type=F32
            ).astype(BF)
            for head in range(2):
                columns = slice(head * HD, (head + 1) * HD)
                query_rows[rows, columns] = nt_dot(same, query_turned[:, columns]).astype(BF)

    def own_rows():
        @pl.loop(0, TOKENS // CHUNK)
        def _(block):
            rows = rows_at(block * CHUNK, CHUNK)
            query_owned[rows] = jnp.dot(
                to_owner[rows], query_rows[...], preferred_element_type=F32
            ).astype(BF)

        query_back.start()

    key_move.arrive()
    keys_turned[...] = nt_dot(same, keys[...]).astype(BF)
    ring(0)
    ring(1)
    grad_move.start()
    query_move.arrive()
    forward(0)
    ring(2)
    saved_move.start()
    load_hidden.wait()
    forward(1)
    forward(2)
    up(3, 0, 4).wait_recv()
    pair(core, 4, 0).start()
    down(3, 1, 4).wait_recv()
    pair(core, 4, 1).start()
    for offset in range(-3, 5):
        for part in range(2):
            pair(1 - core, offset, part).wait_recv()
    value_own[...] = jnp.dot(hidden_ref[...], whole[...], preferred_element_type=F32).astype(BF)
    value_move.start()
    forward(3)
    grad_move.arrive()
    for quarter in range(4):
        value_part(quarter)
    value_rounded[...] = value_terms[...].astype(BF)
    value_back.start()
    for block in range(D // CHUNK):
        rows = slice(block * CHUNK, (block + 1) * CHUNK)
        turned[rows] = nt_dot(diagonal, hidden_ref[:, rows]).astype(BF)

    saved_move.arrive()
    saved_turned = nt_dot(diagonal, saved[...]).astype(BF)

    @pl.loop(0, TOKENS // CHUNK)
    def _(block):
        rows = rows_at(block * CHUNK, CHUNK)
        product = jnp.dot(
            saved_turned, to_owner[:, rows], preferred_element_type=F32
        ) * nt_dot(diagonal, grads[rows])
        for head in range(2):
            delta[head : head + 1, rows] = jnp.sum(
                product[head * HD : (head + 1) * HD], axis=0, keepdims=True
            )

    def four(arrived, group):
        total = arrived[4 * group].astype(F32)
        for part in range(1, 4):
            total = total + arrived[4 * group + part].astype(F32)
        return total.astype(BF)

    value_back.arrive()
    for group in range(KVH):
        value_grad[:, group * HD : (group + 1) * HD] = four(value_in, group)

    offsets = (4, 3, -3, 2, -2, 1, -1, 0)

    def partial_at(at_core, offset):
        start = (at_core * Z + (z + Z + offset) % Z) * CHUNK
        return jnp.dot(
            turned[rows_at(start, CHUNK)], value_grad[...], preferred_element_type=F32
        ).astype(BF)

    def pair_back(index):
        return remote(
            theirs.at[index],
            from_pair.at[index],
            pair_back_sems.at[0, index],
            pair_back_sems.at[1, index],
            dp,
            other,
        )

    for index, offset in enumerate(offsets):
        theirs[index] = partial_at(1 - core, offset)
        pair_back(index).start()
    for index, offset in enumerate(offsets):
        mine[index] = partial_at(core, offset)

    def spans(part):
        return slice(part * half, (part + 1) * half)

    def up_back(step, part):
        return remote(
            up_out.at[step, spans(part)],
            up_in.at[step, spans(part)],
            ring_back_sems.at[0, step, part],
            ring_back_sems.at[1, step, part],
            above,
            ctx,
        )

    def down_back(step, part):
        return remote(
            down_out.at[step, spans(part)],
            down_in.at[step, spans(part)],
            ring_back_sems.at[2, step, part],
            ring_back_sems.at[3, step, part],
            below,
            ctx,
        )

    def chip_sum(index, part):
        return mine[index, spans(part)].astype(F32) + from_pair[index, spans(part)].astype(F32)

    pair_back(0).wait_recv()
    up_out[0, spans(0)] = chip_sum(0, 0).astype(BF)
    up_back(0, 0).start()
    down_out[0, spans(1)] = chip_sum(0, 1).astype(BF)
    down_back(0, 1).start()

    def ring_back(step):
        pair_back(2 * step - 1).wait_recv()
        pair_back(2 * step).wait_recv()
        if step == 1:
            up_out[1, spans(1)] = chip_sum(1, 1).astype(BF)
            up_back(1, 1).start()
            down_out[1, spans(0)] = chip_sum(2, 0).astype(BF)
            down_back(1, 0).start()
        for index, ring, out, arrived, kept in (
            (2 * step - 1, up_back, up_out, up_in, 0),
            (2 * step, down_back, down_out, down_in, 1),
        ):
            for part in (kept,) if step == 1 else (1 - kept, kept):
                ring(step - 1, part).wait_recv()
                out[step, spans(part)] = (
                    chip_sum(index, part) + arrived[step - 1, spans(part)].astype(F32)
                ).astype(BF)
                ring(step, part).start()

    value_move.arrive()
    backward(0)
    backward(1)
    ring_back(1)
    backward(2)
    backward(3)
    key_rounded[...] = key_terms[...].astype(BF)
    key_back.start()
    ring_back(2)
    own_rows()
    ring_back(3)
    pair_back(7).wait_recv()
    for part in (0, 1):
        up_back(3, part).wait_recv()
        down_back(3, part).wait_recv()
        mine[7, spans(part)] = (
            chip_sum(7, part)
            + up_in[3, spans(part)].astype(F32)
            + down_in[3, spans(part)].astype(F32)
        ).astype(BF)

    plane = x_lo * 8 + chip

    def plane_back(step):
        to_ctx = (ctx + step) % CTX
        return remote(
            mine.at[7, rows_at(to_ctx * CAP, CAP)],
            plane_in.at[plane],
            plane_back_sems.at[0, step],
            plane_back_sems.at[1, plane],
            core * Z + z,
            to_ctx,
        )

    own_plane = pltpu.make_async_copy(
        mine.at[7, rows_at(ctx * CAP, CAP)], plane_in.at[plane], own_sems.at[3]
    )

    @pl.when(core == x_lo)
    def _():
        own_plane.start()

    @pl.when(core != x_lo)
    def _():
        plane_back(0).start()

    @pl.loop(1, CTX)
    def _(step):
        plane_back(step).start()

    key_back.arrive()
    for group in range(KVH):
        key_grad_ref[:, group * HD : (group + 1) * HD] = four(key_in, group)

    @pl.when(core == x_lo)
    def _():
        own_plane.wait()

    @pl.loop(0, 16)
    def _(source):
        @pl.when(jnp.logical_or(core != x_lo, source != plane))
        def _():
            remote(
                mine.at[7, pl.ds(0, CAP)],
                plane_in.at[source],
                plane_back_sems.at[0, 0],
                plane_back_sems.at[1, source],
                dp,
                other,
            ).wait_recv()

    weight_sum = plane_in[0].astype(F32)
    for source in range(1, 16):
        weight_sum = weight_sum + plane_in[source].astype(F32)
    weight_grad_ref[...] = weight_sum * (1.0 / math.sqrt(32768.0))

    @pl.when(core != x_lo)
    def _():
        plane_copy(0).wait_send()
        plane_back(0).wait_send()

    @pl.loop(1, 16)
    def _(step):
        plane_copy(step).wait_send()
        plane_back(step).wait_send()

    for step in range(3):
        for part in range(2):
            up(step, part, -step).wait_send()
            down(step, part, step).wait_send()
    up(3, 0, -3).wait_send()
    down(3, 1, 3).wait_send()
    for offset in range(-3, 5):
        for part in range(2):
            pair(core, offset, part).wait_send()
    up_back(0, 0).wait_send()
    down_back(0, 1).wait_send()
    for step in range(1, 4):
        for part in range(2):
            up_back(step, part).wait_send()
            down_back(step, part).wait_send()
    for index in range(8):
        pair_back(index).wait_send()
    query_back.arrive()
    for part in (
        key_move,
        query_move,
        grad_move,
        saved_move,
        value_move,
        value_back,
        key_back,
        query_back,
    ):
        part.finish()


def local(
    hidden,
    value_weight,
    queries,
    key_rows,
    attn_saved,
    grad_out,
    doc_lengths,
    routing,
    visible_blocks,
):
    vmem = pl.BlockSpec(memory_space=pltpu.VMEM)
    smem = pl.BlockSpec(memory_space=pltpu.SMEM)
    hbm = pl.BlockSpec(memory_space=pltpu.HBM)
    dma = pltpu.SemaphoreType.DMA
    chunk = (CHUNK, KVW)
    grad_query, grad_key, grad_weight = pl.pallas_call(
        kernel,
        out_shape=(
            jax.ShapeDtypeStruct((ROWS, D), BF),
            jax.ShapeDtypeStruct((ROWS, KVW), BF),
            jax.ShapeDtypeStruct((CAP, KVW), F32),
        ),
        in_specs=[smem, smem, hbm, hbm, hbm, hbm, vmem, hbm, hbm],
        out_specs=(hbm, vmem, vmem),
        scratch_shapes=[
            pltpu.VMEM((ROWS, D), BF),
            pltpu.VMEM((D, ROWS), BF),
            pltpu.VMEM((TOKENS, PAIR), BF),
            pltpu.VMEM((TOKENS, PAIR), BF),
            pltpu.VMEM((TOKENS, PAIR), BF),
            pltpu.VMEM((TOKENS, HD), BF),
            pltpu.VMEM((HD, TOKENS), BF),
            pltpu.VMEM((TOKENS, HD), BF),
            pltpu.VMEM((TOKENS, TOKENS), BF),
            pltpu.VMEM((USED, ROWS), F32),
            pltpu.VMEM((2, TOKENS), F32),
            pltpu.VMEM((D, KVW), BF),
            pltpu.VMEM((ROWS, KVW), BF),
            pltpu.VMEM((CTX * USED, PAIR), BF),
            pltpu.VMEM((TOKENS, HD), F32),
            pltpu.VMEM((TOKENS, HD), F32),
            pltpu.VMEM((TOKENS, HD), BF),
            pltpu.VMEM((TOKENS, HD), BF),
            pltpu.VMEM((TOKENS, PAIR), BF),
            pltpu.VMEM((TOKENS, PAIR), BF),
            pltpu.VMEM((CTX, ROWS, HD), BF),
            pltpu.VMEM((CTX, ROWS, HD), BF),
            pltpu.VMEM((ROWS, KVW), BF),
            pltpu.VMEM((8,) + chunk, BF),
            pltpu.VMEM((8,) + chunk, BF),
            pltpu.VMEM((8,) + chunk, BF),
            pltpu.VMEM((4,) + chunk, BF),
            pltpu.VMEM((4,) + chunk, BF),
            pltpu.VMEM((4,) + chunk, BF),
            pltpu.VMEM((4,) + chunk, BF),
            pltpu.VMEM((16, CAP, KVW), BF),
            dma,
            dma((12,)),
            dma((2, 16)),
            dma((4, 4, 2)),
            dma((2, 8, 2)),
            dma((8, 2, CTX)),
            dma((2, 8)),
            dma((4, 4, 2)),
            dma((2, 16)),
        ],
        compiler_params=pltpu.CompilerParams(
            has_side_effects=True, vmem_limit_bytes=60 * 1024 * 1024, collective_id=0
        ),
        name="attention_backward",
    )(
        doc_lengths,
        visible_blocks[0],
        value_weight,
        hidden[0],
        key_rows[0],
        attn_saved[0],
        routing.reshape(CTX, ROWS),
        queries[0],
        grad_out[0],
    )
    return (grad_query[None], grad_key[None], grad_weight)


def solution(mesh):
    return jax.shard_map(
        local,
        mesh=mesh,
        in_specs=(
            P("dp", "ctx", None),
            P(("dp", "ctx"), None),
            P("dp", "ctx", None),
            P("dp", "ctx", None),
            P("dp", "ctx", None),
            P("dp", "ctx", None),
            P("dp", None),
            P("dp", None),
            P("dp", None, None),
        ),
        out_specs=(P("dp", "ctx", None), P("dp", "ctx", None), P(("dp", "ctx"), None)),
        check_vma=False,
    )
```

```python
import math

import jax
import jax.numpy as jnp
from jax import lax
from jax.experimental import pallas as pl
from jax.experimental.pallas import tpu as pltpu
from jax.sharding import PartitionSpec as P

QH = 32
HD = 128
VB = 64
ROWS = 128
CTX = 16
CAP = 16
TOKENS = 2048
PAIR = 2 * HD
KVH = 4
Z = 8
D = 4096
KVW = 512
USED = 1152
CHUNK = 256
BF = jnp.bfloat16
F32 = jnp.float32
NT = (((1,), (1,)), ((), ()))
TN = (((0,), (0,)), ((), ()))
SCALE = 1.0 / math.sqrt(HD)


def remote(source, target, send_sem, recv_sem, dp, ctx):
    return pltpu.make_async_remote_copy(
        src_ref=source,
        dst_ref=target,
        send_sem=send_sem,
        recv_sem=recv_sem,
        device_id=(dp, ctx),
        device_id_type=pl.DeviceIdType.MESH,
    )


def rows_at(start, size):
    return pl.ds(pl.multiple_of(start, size), size)


def iota(shape, axis):
    return lax.broadcasted_iota(jnp.int32, shape, axis)


def nt_dot(first, second):
    return lax.dot_general(first, second, NT, preferred_element_type=F32)


def tn_dot(first, second):
    return lax.dot_general(first, second, TN, preferred_element_type=F32)


class Exchange:
    def __init__(self, source, target, sems, own_sem, dp, ctx):
        self.source, self.target = source, target
        self.sems, self.own_sem, self.dp, self.ctx = sems, own_sem, dp, ctx

    def copy(self, step):
        partner = (self.ctx + step) % CTX
        return remote(
            self.source(partner),
            self.target,
            self.sems.at[0, step],
            self.sems.at[1, step],
            self.dp,
            partner,
        )

    def own_copy(self):
        return pltpu.make_async_copy(self.source(self.ctx), self.target, self.own_sem)

    def start(self):
        self.own_copy().start()

        @pl.loop(1, CTX)
        def _(step):
            self.copy(step).start()

    def arrive(self):
        self.own_copy().wait()

        @pl.loop(1, CTX)
        def _(step):
            self.copy(step).wait_recv()

    def finish(self):
        @pl.loop(1, CTX)
        def _(step):
            self.copy(step).wait_send()


class Shared:
    def __init__(self, source, target, sems, near_sems, own_sem, dp, ctx):
        self.source, self.target = source, target
        self.sems, self.near_sems, self.own_sem = sems, near_sems, own_sem
        self.dp, self.ctx = dp, ctx
        self.chip, self.core = ctx // 2, ctx % 2

    def block(self, device):
        return self.target.at[rows_at(device * ROWS, ROWS)]

    def far(self, step):
        partner = ((self.chip + step) % 8) * 2 + self.core
        return remote(
            self.source(partner),
            self.block(self.ctx),
            self.sems.at[0, step],
            self.sems.at[1, step],
            self.dp,
            partner,
        )

    def near(self, step, core):
        block = self.block(((self.chip + 8 - step) % 8) * 2 + core)
        return remote(
            block,
            block,
            self.near_sems.at[0, step],
            self.near_sems.at[1, step],
            self.dp,
            self.ctx + 1 - 2 * self.core,
        )

    def own_copy(self):
        return pltpu.make_async_copy(self.source(self.ctx), self.block(self.ctx), self.own_sem)

    def start(self):
        self.own_copy().start()

        @pl.loop(1, 8)
        def _(step):
            self.far(step).start()

    def hand_on(self):
        self.own_copy().wait()
        self.near(0, self.core).start()

        @pl.loop(1, 8)
        def _(step):
            self.far(step).wait_recv()
            self.near(step, self.core).start()

    def arrive(self):
        @pl.loop(0, 8)
        def _(step):
            self.near(step, 1 - self.core).wait_recv()

    def finish(self):
        self.near(0, self.core).wait_send()

        @pl.loop(1, 8)
        def _(step):
            self.far(step).wait_send()
            self.near(step, self.core).wait_send()


def plane_partner(dp, ctx, step):
    chip = ((dp // Z) * 8 + ctx // 2 + step) % 16
    return (chip // 8) * Z + dp % Z, (chip % 8) * 2 + dp // Z


def kernel(
    length_ref,
    visible_ref,
    weight_ref,
    hidden_hbm,
    key_hbm,
    saved_hbm,
    route_ref,
    query_hbm,
    grad_hbm,
    query_grad_ref,
    key_grad_ref,
    weight_grad_ref,
    hidden_ref,
    turned,
    queries,
    grads,
    saved,
    keys,
    keys_turned,
    values,
    to_owner,
    bias,
    delta,
    whole,
    value_own,
    weights_all,
    key_terms,
    value_terms,
    key_rounded,
    value_rounded,
    query_rows,
    query_owned,
    key_in,
    value_in,
    value_grad,
    mine,
    theirs,
    from_pair,
    up_in,
    down_in,
    up_out,
    down_out,
    plane_in,
    load_sem,
    own_sems,
    plane_sems,
    ring_sems,
    pair_sems,
    exchange_sems,
    shared_sems,
    pair_back_sems,
    ring_back_sems,
    plane_back_sems,
):
    dp, ctx = lax.axis_index("dp"), lax.axis_index("ctx")
    x_lo, z = dp // Z, dp % Z
    chip, core = ctx // 2, ctx % 2
    other = ctx + 1 - 2 * core
    above, below = x_lo * Z + (z + 1) % Z, x_lo * Z + (z + Z - 1) % Z

    load_hidden = pltpu.make_async_copy(hidden_hbm, hidden_ref, load_sem)
    load_hidden.start()

    barrier = pltpu.get_barrier_semaphore()

    def greet(to_dp, to_ctx):
        pl.semaphore_signal(
            barrier, inc=1, device_id=(to_dp, to_ctx), device_id_type=pl.DeviceIdType.MESH
        )

    greet(above, ctx)
    greet(below, ctx)

    @pl.loop(1, CTX)
    def _(step):
        greet(dp, (ctx + step) % CTX)
        greet(*plane_partner(dp, ctx, step))
        greet(core * Z + z, (ctx + step) % CTX)

    @pl.when(core != x_lo)
    def _():
        greet(*plane_partner(dp, ctx, 0))
        greet(core * Z + z, ctx)

    same = jnp.where(iota((ROWS, ROWS), 0) == iota((ROWS, ROWS), 1), 1.0, 0.0).astype(BF)
    diagonal = jnp.where(iota((CHUNK, CHUNK), 0) == iota((CHUNK, CHUNK), 1), 1.0, 0.0).astype(BF)
    left = iota((1, ROWS), 1) < VB

    @pl.loop(0, CTX)
    def _(block):
        to_owner[:, rows_at(block * ROWS, ROWS)] = jnp.where(
            route_ref[pl.ds(block, 1)] == iota((TOKENS, ROWS), 0), 1.0, 0.0
        ).astype(BF)

    key_terms[...] = jnp.zeros_like(key_terms)
    value_terms[...] = jnp.zeros_like(value_terms)
    pl.semaphore_wait(barrier, 2 + 3 * (CTX - 1) + jnp.where(core != x_lo, 2, 0))

    shard = whole.at[rows_at((dp * CTX + ctx) * CAP, CAP)]

    def plane_copy(step):
        to_dp, to_ctx = plane_partner(dp, ctx, step)
        return remote(
            weight_ref, shard, plane_sems.at[0, step], plane_sems.at[1, ctx], to_dp, to_ctx
        )

    own_shard = pltpu.make_async_copy(weight_ref, shard, own_sems.at[3])

    @pl.when(core == x_lo)
    def _():
        own_shard.start()

    @pl.when(core != x_lo)
    def _():
        plane_copy(0).start()

    @pl.loop(1, 16)
    def _(step):
        plane_copy(step).start()

    def wide(index, width):
        return pl.ds(pl.multiple_of(index * width, width), width)

    here = rows_at(ctx * ROWS, ROWS)

    def exchange(which, source, target):
        return Exchange(source, target, exchange_sems.at[which], own_sems.at[4 + which], dp, ctx)

    def shared(which, source, target):
        near_sems = shared_sems.at[which // 4]
        return Shared(
            source, target, exchange_sems.at[which], near_sems, own_sems.at[4 + which], dp, ctx
        )

    key_move = shared(0, lambda to: key_hbm.at[:, wide(to // 4, HD)], keys)
    query_move = exchange(1, lambda to: query_hbm.at[:, wide(to, PAIR)], queries.at[here])
    grad_move = exchange(2, lambda to: grad_hbm.at[:, wide(to, PAIR)], grads.at[here])
    saved_move = exchange(3, lambda to: saved_hbm.at[:, wide(to, PAIR)], saved.at[here])
    value_move = shared(4, lambda to: value_own.at[:, wide(to // 4, HD)], values)
    value_back = exchange(5, lambda to: value_rounded.at[rows_at(to * ROWS, ROWS)], value_in.at[ctx])
    key_back = exchange(6, lambda to: key_rounded.at[rows_at(to * ROWS, ROWS)], key_in.at[ctx])
    query_back = exchange(
        7, lambda to: query_owned.at[rows_at(to * ROWS, ROWS)], query_grad_ref.at[:, wide(ctx, PAIR)]
    )
    key_move.start()
    query_move.start()

    @pl.when(core == x_lo)
    def _():
        own_shard.wait()

    @pl.loop(0, CTX)
    def _(source):
        @pl.when(jnp.logical_or(core != x_lo, source != ctx))
        def _():
            shard_in = whole.at[rows_at(((core * Z + z) * CTX + source) * CAP, CAP)]
            remote(
                weight_ref, shard_in, plane_sems.at[0, 0], plane_sems.at[1, source], dp, other
            ).wait_recv()

    half = CHUNK // 2

    def piece(at_core, offset, part):
        start = (at_core * Z + (z + Z + offset) % Z) * CHUNK + part * half
        return whole.at[rows_at(start, half)]

    def up(step, part, offset):
        block = piece(core, offset, part)
        return remote(
            block, block, ring_sems.at[0, step, part], ring_sems.at[1, step, part], above, ctx
        )

    def down(step, part, offset):
        block = piece(core, offset, part)
        return remote(
            block, block, ring_sems.at[2, step, part], ring_sems.at[3, step, part], below, ctx
        )

    def pair(at_core, offset, part):
        block = piece(at_core, offset, part)
        index = offset + 3
        return remote(
            block, block, pair_sems.at[0, index, part], pair_sems.at[1, index, part], dp, other
        )

    for part in range(2):
        up(0, part, 0).start()
        down(0, part, 0).start()
        pair(core, 0, part).start()

    def ring(step):
        for part in range(2):
            up(step, part, -step - 1).wait_recv()
            if step < 2 or part == 0:
                up(step + 1, part, -step - 1).start()
            pair(core, -step - 1, part).start()
            down(step, part, step + 1).wait_recv()
            if step < 2 or part == 1:
                down(step + 1, part, step + 1).start()
            pair(core, step + 1, part).start()

    quarters = ((0, 512), (4, 1024), (8, USED), (12, USED))

    def first_block(quarter, block):
        return block - 8 if quarter >= 2 else jnp.int32(0)

    def stacked(pairs, block):
        rows = rows_at(block * ROWS, ROWS)
        return jnp.concatenate([pairs[rows, :HD], pairs[rows, HD:]], axis=0)

    def forward(quarter, behind=()):
        first, size = quarters[quarter]

        @pl.loop(first, first + 4)
        def _(block):
            base = first_block(quarter, block)
            position = block * ROWS + iota((1, ROWS), 1)
            doc_start = jnp.zeros((1, ROWS), jnp.int32)
            doc_end = jnp.int32(0)
            for n in range(8):
                length = length_ref[0, n]
                doc_end = doc_end + length
                doc_start = doc_start + jnp.where(position >= doc_end, length, 0)
            for part in range(size // VB):
                column = 2 * base + part
                seen = jnp.where(
                    left, visible_ref[2 * block, column], visible_ref[2 * block + 1, column]
                )
                key_position = column * VB + iota((VB, ROWS), 0)
                allowed = (
                    (key_position >= doc_start) & (key_position <= position) & (seen == 1)
                )
                bias[part * VB : (part + 1) * VB] = jnp.where(allowed, 0.0, -1e30)
            window = pl.ds(pl.multiple_of(base * ROWS, ROWS), size)
            scores = nt_dot(keys[window], stacked(queries, block))
            scores = scores + jnp.concatenate([bias[:size], bias[:size]], axis=1)
            top = jnp.max(scores, axis=0, keepdims=True)
            raised = jnp.exp2((scores - top) * (SCALE * math.log2(math.e)))
            weights = raised * (1.0 / jnp.sum(raised, axis=0, keepdims=True))
            weights_all[pl.ds(pl.multiple_of(block * USED, ROWS), size)] = weights.astype(BF)
            for earlier in behind:
                value_block(earlier, block - first + quarters[earlier][0])

    def value_block(quarter, block):
        size = quarters[quarter][1]
        window = pl.ds(pl.multiple_of(first_block(quarter, block) * ROWS, ROWS), size)
        stored = pl.ds(pl.multiple_of(block * USED, ROWS), size)
        value_terms[window] += jnp.dot(
            weights_all[stored], stacked(grads, block), preferred_element_type=F32
        )

    def value_part(quarter):
        first = quarters[quarter][0]

        @pl.loop(first, first + 4)
        def _(block):
            value_block(quarter, block)

    def backward(quarter):
        first, size = quarters[quarter]

        @pl.loop(first, first + 4)
        def _(block):
            window = pl.ds(pl.multiple_of(first_block(quarter, block) * ROWS, ROWS), size)
            stored = pl.ds(pl.multiple_of(block * USED, ROWS), size)
            rows = rows_at(block * ROWS, ROWS)
            weights = weights_all[stored].astype(F32)
            dweights = nt_dot(values[window], stacked(grads, block))
            row_delta = jnp.concatenate([delta[:1, rows], delta[1:, rows]], axis=1)
            dscores = (weights * (dweights - row_delta)).astype(BF)
            key_terms[window] += jnp.dot(
                dscores, stacked(queries, block), preferred_element_type=F32
            )
            query_turned = jnp.dot(
                keys_turned[:, window], dscores, preferred_element_type=F32
            )
            query_turned = (query_turned * SCALE).astype(BF)
            for head in range(2):
                columns = slice(head * HD, (head + 1) * HD)
                query_rows[rows, columns] = nt_dot(same, query_turned[:, columns]).astype(BF)

    def own_rows():
        @pl.loop(0, TOKENS // CHUNK)
        def _(block):
            rows = rows_at(block * CHUNK, CHUNK)
            query_owned[rows] = jnp.dot(
                to_owner[rows], query_rows[...], preferred_element_type=F32
            ).astype(BF)

        query_back.start()

    key_move.hand_on()
    ring(0)
    key_move.arrive()
    keys_turned[...] = nt_dot(same, keys[...]).astype(BF)
    ring(1)
    grad_move.start()
    query_move.arrive()
    forward(0)
    ring(2)
    saved_move.start()
    load_hidden.wait()
    forward(1)
    forward(2)
    up(3, 0, 4).wait_recv()
    pair(core, 4, 0).start()
    down(3, 1, 4).wait_recv()
    pair(core, 4, 1).start()
    for offset in range(-3, 5):
        for part in range(2):
            pair(1 - core, offset, part).wait_recv()
    value_own[...] = jnp.dot(hidden_ref[...], whole[...], preferred_element_type=F32).astype(BF)
    value_move.start()
    grad_move.arrive()
    forward(3, (0, 1, 2))
    value_part(3)
    value_rounded[...] = value_terms[...].astype(BF)
    value_back.start()
    for block in range(D // CHUNK):
        rows = slice(block * CHUNK, (block + 1) * CHUNK)
        turned[rows] = nt_dot(diagonal, hidden_ref[:, rows]).astype(BF)

    saved_move.arrive()
    saved_turned = nt_dot(diagonal, saved[...]).astype(BF)

    @pl.loop(0, TOKENS // CHUNK)
    def _(block):
        rows = rows_at(block * CHUNK, CHUNK)
        product = jnp.dot(
            saved_turned, to_owner[:, rows], preferred_element_type=F32
        ) * nt_dot(diagonal, grads[rows])
        for head in range(2):
            delta[head : head + 1, rows] = jnp.sum(
                product[head * HD : (head + 1) * HD], axis=0, keepdims=True
            )

    value_move.hand_on()

    def four(arrived, group):
        total = arrived[4 * group].astype(F32)
        for part in range(1, 4):
            total = total + arrived[4 * group + part].astype(F32)
        return total.astype(BF)

    value_back.arrive()
    for group in range(KVH):
        value_grad[:, group * HD : (group + 1) * HD] = four(value_in, group)

    offsets = (4, 3, -3, 2, -2, 1, -1, 0)

    def partial_at(at_core, offset):
        start = (at_core * Z + (z + Z + offset) % Z) * CHUNK
        return jnp.dot(
            turned[rows_at(start, CHUNK)], value_grad[...], preferred_element_type=F32
        ).astype(BF)

    def pair_back(index):
        return remote(
            theirs.at[index],
            from_pair.at[index],
            pair_back_sems.at[0, index],
            pair_back_sems.at[1, index],
            dp,
            other,
        )

    for index, offset in enumerate(offsets):
        theirs[index] = partial_at(1 - core, offset)
        pair_back(index).start()
    for index, offset in enumerate(offsets):
        mine[index] = partial_at(core, offset)

    def spans(part):
        return slice(part * half, (part + 1) * half)

    def up_back(step, part):
        return remote(
            up_out.at[step, spans(part)],
            up_in.at[step, spans(part)],
            ring_back_sems.at[0, step, part],
            ring_back_sems.at[1, step, part],
            above,
            ctx,
        )

    def down_back(step, part):
        return remote(
            down_out.at[step, spans(part)],
            down_in.at[step, spans(part)],
            ring_back_sems.at[2, step, part],
            ring_back_sems.at[3, step, part],
            below,
            ctx,
        )

    def chip_sum(index, part):
        return mine[index, spans(part)].astype(F32) + from_pair[index, spans(part)].astype(F32)

    pair_back(0).wait_recv()
    up_out[0, spans(0)] = chip_sum(0, 0).astype(BF)
    up_back(0, 0).start()
    down_out[0, spans(1)] = chip_sum(0, 1).astype(BF)
    down_back(0, 1).start()

    def ring_back(step):
        pair_back(2 * step - 1).wait_recv()
        pair_back(2 * step).wait_recv()
        if step == 1:
            up_out[1, spans(1)] = chip_sum(1, 1).astype(BF)
            up_back(1, 1).start()
            down_out[1, spans(0)] = chip_sum(2, 0).astype(BF)
            down_back(1, 0).start()
        for index, ring, out, arrived, kept in (
            (2 * step - 1, up_back, up_out, up_in, 0),
            (2 * step, down_back, down_out, down_in, 1),
        ):
            for part in (kept,) if step == 1 else (1 - kept, kept):
                ring(step - 1, part).wait_recv()
                out[step, spans(part)] = (
                    chip_sum(index, part) + arrived[step - 1, spans(part)].astype(F32)
                ).astype(BF)
                ring(step, part).start()

    value_move.arrive()
    backward(0)
    backward(1)
    ring_back(1)
    backward(2)
    backward(3)
    key_rounded[...] = (key_terms[...] * SCALE).astype(BF)
    key_back.start()
    ring_back(2)
    own_rows()
    ring_back(3)
    pair_back(7).wait_recv()
    for part in (0, 1):
        up_back(3, part).wait_recv()
        down_back(3, part).wait_recv()
        mine[7, spans(part)] = (
            chip_sum(7, part)
            + up_in[3, spans(part)].astype(F32)
            + down_in[3, spans(part)].astype(F32)
        ).astype(BF)

    plane = x_lo * 8 + chip

    def plane_back(step):
        to_ctx = (ctx + step) % CTX
        return remote(
            mine.at[7, rows_at(to_ctx * CAP, CAP)],
            plane_in.at[plane],
            plane_back_sems.at[0, step],
            plane_back_sems.at[1, plane],
            core * Z + z,
            to_ctx,
        )

    own_plane = pltpu.make_async_copy(
        mine.at[7, rows_at(ctx * CAP, CAP)], plane_in.at[plane], own_sems.at[3]
    )

    @pl.when(core == x_lo)
    def _():
        own_plane.start()

    @pl.when(core != x_lo)
    def _():
        plane_back(0).start()

    @pl.loop(1, CTX)
    def _(step):
        plane_back(step).start()

    key_back.arrive()
    for group in range(KVH):
        key_grad_ref[:, group * HD : (group + 1) * HD] = four(key_in, group)

    @pl.when(core == x_lo)
    def _():
        own_plane.wait()

    @pl.loop(0, 16)
    def _(source):
        @pl.when(jnp.logical_or(core != x_lo, source != plane))
        def _():
            remote(
                mine.at[7, pl.ds(0, CAP)],
                plane_in.at[source],
                plane_back_sems.at[0, 0],
                plane_back_sems.at[1, source],
                dp,
                other,
            ).wait_recv()

    weight_sum = plane_in[0].astype(F32)
    for source in range(1, 16):
        weight_sum = weight_sum + plane_in[source].astype(F32)
    weight_grad_ref[...] = weight_sum * (1.0 / math.sqrt(32768.0))

    @pl.when(core != x_lo)
    def _():
        plane_copy(0).wait_send()
        plane_back(0).wait_send()

    @pl.loop(1, 16)
    def _(step):
        plane_copy(step).wait_send()
        plane_back(step).wait_send()

    for step in range(3):
        for part in range(2):
            up(step, part, -step).wait_send()
            down(step, part, step).wait_send()
    up(3, 0, -3).wait_send()
    down(3, 1, 3).wait_send()
    for offset in range(-3, 5):
        for part in range(2):
            pair(core, offset, part).wait_send()
    up_back(0, 0).wait_send()
    down_back(0, 1).wait_send()
    for step in range(1, 4):
        for part in range(2):
            up_back(step, part).wait_send()
            down_back(step, part).wait_send()
    for index in range(8):
        pair_back(index).wait_send()
    query_back.arrive()
    for part in (
        key_move,
        query_move,
        grad_move,
        saved_move,
        value_move,
        value_back,
        key_back,
        query_back,
    ):
        part.finish()


def local(
    hidden,
    value_weight,
    queries,
    key_rows,
    attn_saved,
    grad_out,
    doc_lengths,
    routing,
    visible_blocks,
):
    vmem = pl.BlockSpec(memory_space=pltpu.VMEM)
    smem = pl.BlockSpec(memory_space=pltpu.SMEM)
    hbm = pl.BlockSpec(memory_space=pltpu.HBM)
    dma = pltpu.SemaphoreType.DMA
    chunk = (CHUNK, KVW)
    grad_query, grad_key, grad_weight = pl.pallas_call(
        kernel,
        out_shape=(
            jax.ShapeDtypeStruct((ROWS, D), BF),
            jax.ShapeDtypeStruct((ROWS, KVW), BF),
            jax.ShapeDtypeStruct((CAP, KVW), F32),
        ),
        in_specs=[smem, smem, hbm, hbm, hbm, hbm, vmem, hbm, hbm],
        out_specs=(hbm, vmem, vmem),
        scratch_shapes=[
            pltpu.VMEM((ROWS, D), BF),
            pltpu.VMEM((D, ROWS), BF),
            pltpu.VMEM((TOKENS, PAIR), BF),
            pltpu.VMEM((TOKENS, PAIR), BF),
            pltpu.VMEM((TOKENS, PAIR), BF),
            pltpu.VMEM((TOKENS, HD), BF),
            pltpu.VMEM((HD, TOKENS), BF),
            pltpu.VMEM((TOKENS, HD), BF),
            pltpu.VMEM((TOKENS, TOKENS), BF),
            pltpu.VMEM((USED, ROWS), F32),
            pltpu.VMEM((2, TOKENS), F32),
            pltpu.VMEM((D, KVW), BF),
            pltpu.VMEM((ROWS, KVW), BF),
            pltpu.VMEM((CTX * USED, PAIR), BF),
            pltpu.VMEM((TOKENS, HD), F32),
            pltpu.VMEM((TOKENS, HD), F32),
            pltpu.VMEM((TOKENS, HD), BF),
            pltpu.VMEM((TOKENS, HD), BF),
            pltpu.VMEM((TOKENS, PAIR), BF),
            pltpu.VMEM((TOKENS, PAIR), BF),
            pltpu.VMEM((CTX, ROWS, HD), BF),
            pltpu.VMEM((CTX, ROWS, HD), BF),
            pltpu.VMEM((ROWS, KVW), BF),
            pltpu.VMEM((8,) + chunk, BF),
            pltpu.VMEM((8,) + chunk, BF),
            pltpu.VMEM((8,) + chunk, BF),
            pltpu.VMEM((4,) + chunk, BF),
            pltpu.VMEM((4,) + chunk, BF),
            pltpu.VMEM((4,) + chunk, BF),
            pltpu.VMEM((4,) + chunk, BF),
            pltpu.VMEM((16, CAP, KVW), BF),
            dma,
            dma((12,)),
            dma((2, 16)),
            dma((4, 4, 2)),
            dma((2, 8, 2)),
            dma((8, 2, CTX)),
            dma((2, 2, 8)),
            dma((2, 8)),
            dma((4, 4, 2)),
            dma((2, 16)),
        ],
        compiler_params=pltpu.CompilerParams(
            has_side_effects=True, vmem_limit_bytes=60 * 1024 * 1024, collective_id=0
        ),
        name="attention_backward",
    )(
        doc_lengths,
        visible_blocks[0],
        value_weight,
        hidden[0],
        key_rows[0],
        attn_saved[0],
        routing.reshape(CTX, ROWS),
        queries[0],
        grad_out[0],
    )
    return (grad_query[None], grad_key[None], grad_weight)


def solution(mesh):
    return jax.shard_map(
        local,
        mesh=mesh,
        in_specs=(
            P("dp", "ctx", None),
            P(("dp", "ctx"), None),
            P("dp", "ctx", None),
            P("dp", "ctx", None),
            P("dp", "ctx", None),
            P("dp", "ctx", None),
            P("dp", None),
            P("dp", None),
            P("dp", None, None),
        ),
        out_specs=(P("dp", "ctx", None), P("dp", "ctx", None), P(("dp", "ctx"), None)),
        check_vma=False,
    )
```

```python
import math

import jax
import jax.numpy as jnp
from jax import lax
from jax.experimental import pallas as pl
from jax.experimental.pallas import tpu as pltpu
from jax.sharding import PartitionSpec as P

QH = 32
HD = 128
VB = 64
ROWS = 128
CTX = 16
CAP = 16
TOKENS = 2048
PAIR = 2 * HD
KVH = 4
Z = 8
D = 4096
KVW = 512
USED = 1152
CHUNK = 256
BF = jnp.bfloat16
F32 = jnp.float32
NT = (((1,), (1,)), ((), ()))
TN = (((0,), (0,)), ((), ()))
SCALE = 1.0 / math.sqrt(HD)


def remote(source, target, send_sem, recv_sem, dp, ctx):
    return pltpu.make_async_remote_copy(
        src_ref=source,
        dst_ref=target,
        send_sem=send_sem,
        recv_sem=recv_sem,
        device_id=(dp, ctx),
        device_id_type=pl.DeviceIdType.MESH,
    )


def rows_at(start, size):
    return pl.ds(pl.multiple_of(start, size), size)


def iota(shape, axis):
    return lax.broadcasted_iota(jnp.int32, shape, axis)


def nt_dot(first, second):
    return lax.dot_general(first, second, NT, preferred_element_type=F32)


def tn_dot(first, second):
    return lax.dot_general(first, second, TN, preferred_element_type=F32)


class Exchange:
    def __init__(self, source, target, sems, own_sem, dp, ctx):
        self.source, self.target = source, target
        self.sems, self.own_sem, self.dp, self.ctx = sems, own_sem, dp, ctx

    def copy(self, step):
        partner = (self.ctx + step) % CTX
        return remote(
            self.source(partner),
            self.target,
            self.sems.at[0, step],
            self.sems.at[1, step],
            self.dp,
            partner,
        )

    def own_copy(self):
        return pltpu.make_async_copy(self.source(self.ctx), self.target, self.own_sem)

    def start(self):
        self.own_copy().start()

        @pl.loop(1, CTX)
        def _(step):
            self.copy(step).start()

    def arrive(self):
        self.own_copy().wait()

        @pl.loop(1, CTX)
        def _(step):
            self.copy(step).wait_recv()

    def finish(self):
        @pl.loop(1, CTX)
        def _(step):
            self.copy(step).wait_send()


class Shared:
    def __init__(self, source, target, sems, near_sems, own_sem, dp, ctx):
        self.source, self.target = source, target
        self.sems, self.near_sems, self.own_sem = sems, near_sems, own_sem
        self.dp, self.ctx = dp, ctx
        self.chip, self.core = ctx // 2, ctx % 2

    def block(self, device):
        return self.target.at[rows_at(device * ROWS, ROWS)]

    def far(self, step):
        partner = ((self.chip + step) % 8) * 2 + self.core
        return remote(
            self.source(partner),
            self.block(self.ctx),
            self.sems.at[0, step],
            self.sems.at[1, step],
            self.dp,
            partner,
        )

    def near(self, step, core):
        block = self.block(((self.chip + 8 - step) % 8) * 2 + core)
        return remote(
            block,
            block,
            self.near_sems.at[0, step],
            self.near_sems.at[1, step],
            self.dp,
            self.ctx + 1 - 2 * self.core,
        )

    def own_copy(self):
        return pltpu.make_async_copy(self.source(self.ctx), self.block(self.ctx), self.own_sem)

    def start(self):
        self.own_copy().start()

        @pl.loop(1, 8)
        def _(step):
            self.far(step).start()

    def hand_on(self):
        self.own_copy().wait()
        self.near(0, self.core).start()

        @pl.loop(1, 8)
        def _(step):
            self.far(step).wait_recv()
            self.near(step, self.core).start()

    def arrive(self):
        @pl.loop(0, 8)
        def _(step):
            self.near(step, 1 - self.core).wait_recv()

    def finish(self):
        self.near(0, self.core).wait_send()

        @pl.loop(1, 8)
        def _(step):
            self.far(step).wait_send()
            self.near(step, self.core).wait_send()


def plane_partner(dp, ctx, step):
    chip = ((dp // Z) * 8 + ctx // 2 + step) % 16
    return (chip // 8) * Z + dp % Z, (chip % 8) * 2 + dp // Z


def kernel(
    length_ref,
    visible_ref,
    weight_ref,
    hidden_hbm,
    key_hbm,
    saved_hbm,
    route_ref,
    query_hbm,
    grad_hbm,
    query_grad_ref,
    key_grad_ref,
    weight_grad_ref,
    hidden_ref,
    turned,
    queries,
    grads,
    saved,
    keys,
    keys_turned,
    values,
    to_owner,
    bias,
    delta,
    whole,
    value_own,
    weights_all,
    key_terms,
    value_terms,
    key_rounded,
    value_rounded,
    query_rows,
    query_owned,
    key_in,
    value_in,
    value_grad,
    mine,
    theirs,
    from_pair,
    up_in,
    down_in,
    up_out,
    down_out,
    plane_in,
    load_sem,
    own_sems,
    plane_sems,
    ring_sems,
    pair_sems,
    exchange_sems,
    shared_sems,
    pair_back_sems,
    ring_back_sems,
    plane_back_sems,
):
    dp, ctx = lax.axis_index("dp"), lax.axis_index("ctx")
    x_lo, z = dp // Z, dp % Z
    chip, core = ctx // 2, ctx % 2
    other = ctx + 1 - 2 * core
    above, below = x_lo * Z + (z + 1) % Z, x_lo * Z + (z + Z - 1) % Z

    load_hidden = pltpu.make_async_copy(hidden_hbm, hidden_ref, load_sem)
    load_hidden.start()

    barrier = pltpu.get_barrier_semaphore()

    def greet(to_dp, to_ctx):
        pl.semaphore_signal(
            barrier, inc=1, device_id=(to_dp, to_ctx), device_id_type=pl.DeviceIdType.MESH
        )

    greet(above, ctx)
    greet(below, ctx)

    @pl.loop(1, CTX)
    def _(step):
        greet(dp, (ctx + step) % CTX)
        greet(*plane_partner(dp, ctx, step))
        greet(core * Z + z, (ctx + step) % CTX)

    @pl.when(core != x_lo)
    def _():
        greet(*plane_partner(dp, ctx, 0))
        greet(core * Z + z, ctx)

    same = jnp.where(iota((ROWS, ROWS), 0) == iota((ROWS, ROWS), 1), 1.0, 0.0).astype(BF)
    diagonal = jnp.where(iota((CHUNK, CHUNK), 0) == iota((CHUNK, CHUNK), 1), 1.0, 0.0).astype(BF)
    left = iota((1, ROWS), 1) < VB

    @pl.loop(0, CTX)
    def _(block):
        to_owner[:, rows_at(block * ROWS, ROWS)] = jnp.where(
            route_ref[pl.ds(block, 1)] == iota((TOKENS, ROWS), 0), 1.0, 0.0
        ).astype(BF)

    key_terms[...] = jnp.zeros_like(key_terms)
    value_terms[...] = jnp.zeros_like(value_terms)
    pl.semaphore_wait(barrier, 2 + 3 * (CTX - 1) + jnp.where(core != x_lo, 2, 0))

    shard = whole.at[rows_at((dp * CTX + ctx) * CAP, CAP)]

    def plane_copy(step):
        to_dp, to_ctx = plane_partner(dp, ctx, step)
        return remote(
            weight_ref, shard, plane_sems.at[0, step], plane_sems.at[1, ctx], to_dp, to_ctx
        )

    own_shard = pltpu.make_async_copy(weight_ref, shard, own_sems.at[3])

    def wide(index, width):
        return pl.ds(pl.multiple_of(index * width, width), width)

    here = rows_at(ctx * ROWS, ROWS)

    def exchange(which, source, target):
        return Exchange(source, target, exchange_sems.at[which], own_sems.at[4 + which], dp, ctx)

    def shared(which, source, target):
        near_sems = shared_sems.at[which // 4]
        return Shared(
            source, target, exchange_sems.at[which], near_sems, own_sems.at[4 + which], dp, ctx
        )

    key_move = shared(0, lambda to: key_hbm.at[:, wide(to // 4, HD)], keys)
    query_move = exchange(1, lambda to: query_hbm.at[:, wide(to, PAIR)], queries.at[here])
    grad_move = exchange(2, lambda to: grad_hbm.at[:, wide(to, PAIR)], grads.at[here])
    saved_move = exchange(3, lambda to: saved_hbm.at[:, wide(to, PAIR)], saved.at[here])
    value_move = shared(4, lambda to: value_own.at[:, wide(to // 4, HD)], values)
    value_back = exchange(5, lambda to: value_rounded.at[rows_at(to * ROWS, ROWS)], value_in.at[ctx])
    key_back = exchange(6, lambda to: key_rounded.at[rows_at(to * ROWS, ROWS)], key_in.at[ctx])
    query_back = exchange(
        7, lambda to: query_owned.at[rows_at(to * ROWS, ROWS)], query_grad_ref.at[:, wide(ctx, PAIR)]
    )
    key_move.start()
    @pl.when(core == x_lo)
    def _():
        own_shard.start()

    @pl.when(core != x_lo)
    def _():
        plane_copy(0).start()

    @pl.loop(1, 16)
    def _(step):
        plane_copy(step).start()

    query_move.start()

    @pl.when(core == x_lo)
    def _():
        own_shard.wait()

    @pl.loop(0, CTX)
    def _(source):
        @pl.when(jnp.logical_or(core != x_lo, source != ctx))
        def _():
            shard_in = whole.at[rows_at(((core * Z + z) * CTX + source) * CAP, CAP)]
            remote(
                weight_ref, shard_in, plane_sems.at[0, 0], plane_sems.at[1, source], dp, other
            ).wait_recv()

    half = CHUNK // 2

    def piece(at_core, offset, part):
        start = (at_core * Z + (z + Z + offset) % Z) * CHUNK + part * half
        return whole.at[rows_at(start, half)]

    def up(step, part, offset):
        block = piece(core, offset, part)
        return remote(
            block, block, ring_sems.at[0, step, part], ring_sems.at[1, step, part], above, ctx
        )

    def down(step, part, offset):
        block = piece(core, offset, part)
        return remote(
            block, block, ring_sems.at[2, step, part], ring_sems.at[3, step, part], below, ctx
        )

    def pair(at_core, offset, part):
        block = piece(at_core, offset, part)
        index = offset + 3
        return remote(
            block, block, pair_sems.at[0, index, part], pair_sems.at[1, index, part], dp, other
        )

    for part in range(2):
        up(0, part, 0).start()
        down(0, part, 0).start()
        pair(core, 0, part).start()

    def ring(step):
        for part in range(2):
            up(step, part, -step - 1).wait_recv()
            if step < 2 or part == 0:
                up(step + 1, part, -step - 1).start()
            pair(core, -step - 1, part).start()
            down(step, part, step + 1).wait_recv()
            if step < 2 or part == 1:
                down(step + 1, part, step + 1).start()
            pair(core, step + 1, part).start()

    quarters = ((0, 512), (4, 1024), (8, USED), (12, USED))

    def first_block(quarter, block):
        return block - 8 if quarter >= 2 else jnp.int32(0)

    def stacked(pairs, block):
        rows = rows_at(block * ROWS, ROWS)
        return jnp.concatenate([pairs[rows, :HD], pairs[rows, HD:]], axis=0)

    def forward(quarter, behind=()):
        first, size = quarters[quarter]

        @pl.loop(first, first + 4)
        def _(block):
            base = first_block(quarter, block)
            position = block * ROWS + iota((1, ROWS), 1)
            doc_start = jnp.zeros((1, ROWS), jnp.int32)
            doc_end = jnp.int32(0)
            for n in range(8):
                length = length_ref[0, n]
                doc_end = doc_end + length
                doc_start = doc_start + jnp.where(position >= doc_end, length, 0)
            for part in range(size // VB):
                column = 2 * base + part
                seen = jnp.where(
                    left, visible_ref[2 * block, column], visible_ref[2 * block + 1, column]
                )
                key_position = column * VB + iota((VB, ROWS), 0)
                allowed = (
                    (key_position >= doc_start) & (key_position <= position) & (seen == 1)
                )
                bias[part * VB : (part + 1) * VB] = jnp.where(allowed, 0.0, -1e30)
            window = pl.ds(pl.multiple_of(base * ROWS, ROWS), size)
            scores = nt_dot(keys[window], stacked(queries, block))
            scores = scores + jnp.concatenate([bias[:size], bias[:size]], axis=1)
            top = jnp.max(scores, axis=0, keepdims=True)
            raised = jnp.exp2((scores - top) * (SCALE * math.log2(math.e)))
            weights = raised * (1.0 / jnp.sum(raised, axis=0, keepdims=True))
            weights_all[pl.ds(pl.multiple_of(block * USED, ROWS), size)] = weights.astype(BF)
            for earlier in behind:
                value_block(earlier, block - first + quarters[earlier][0])

    def value_block(quarter, block):
        size = quarters[quarter][1]
        window = pl.ds(pl.multiple_of(first_block(quarter, block) * ROWS, ROWS), size)
        stored = pl.ds(pl.multiple_of(block * USED, ROWS), size)
        value_terms[window] += jnp.dot(
            weights_all[stored], stacked(grads, block), preferred_element_type=F32
        )

    def value_part(quarter):
        first = quarters[quarter][0]

        @pl.loop(first, first + 4)
        def _(block):
            value_block(quarter, block)

    def backward(quarter):
        first, size = quarters[quarter]

        @pl.loop(first, first + 4)
        def _(block):
            window = pl.ds(pl.multiple_of(first_block(quarter, block) * ROWS, ROWS), size)
            stored = pl.ds(pl.multiple_of(block * USED, ROWS), size)
            rows = rows_at(block * ROWS, ROWS)
            weights = weights_all[stored].astype(F32)
            dweights = nt_dot(values[window], stacked(grads, block))
            row_delta = jnp.concatenate([delta[:1, rows], delta[1:, rows]], axis=1)
            dscores = (weights * (dweights - row_delta)).astype(BF)
            key_terms[window] += jnp.dot(
                dscores, stacked(queries, block), preferred_element_type=F32
            )
            query_turned = jnp.dot(
                keys_turned[:, window], dscores, preferred_element_type=F32
            )
            query_turned = (query_turned * SCALE).astype(BF)
            for head in range(2):
                columns = slice(head * HD, (head + 1) * HD)
                query_rows[rows, columns] = nt_dot(same, query_turned[:, columns]).astype(BF)

    def own_rows():
        @pl.loop(0, TOKENS // CHUNK)
        def _(block):
            rows = rows_at(block * CHUNK, CHUNK)
            query_owned[rows] = jnp.dot(
                to_owner[rows], query_rows[...], preferred_element_type=F32
            ).astype(BF)

        query_back.start()

    key_move.hand_on()
    ring(0)
    key_move.arrive()
    keys_turned[...] = nt_dot(same, keys[...]).astype(BF)
    ring(1)
    grad_move.start()
    query_move.arrive()
    forward(0)
    ring(2)
    saved_move.start()
    load_hidden.wait()
    forward(1)
    forward(2)
    up(3, 0, 4).wait_recv()
    pair(core, 4, 0).start()
    down(3, 1, 4).wait_recv()
    pair(core, 4, 1).start()
    for offset in range(-3, 5):
        for part in range(2):
            pair(1 - core, offset, part).wait_recv()
    value_own[...] = jnp.dot(hidden_ref[...], whole[...], preferred_element_type=F32).astype(BF)
    value_move.start()
    grad_move.arrive()
    forward(3, (0, 1, 2))
    value_part(3)
    value_rounded[...] = value_terms[...].astype(BF)
    value_back.start()
    for block in range(D // CHUNK):
        rows = slice(block * CHUNK, (block + 1) * CHUNK)
        turned[rows] = nt_dot(diagonal, hidden_ref[:, rows]).astype(BF)

    saved_move.arrive()
    saved_turned = nt_dot(diagonal, saved[...]).astype(BF)

    @pl.loop(0, TOKENS // CHUNK)
    def _(block):
        rows = rows_at(block * CHUNK, CHUNK)
        product = jnp.dot(
            saved_turned, to_owner[:, rows], preferred_element_type=F32
        ) * nt_dot(diagonal, grads[rows])
        for head in range(2):
            delta[head : head + 1, rows] = jnp.sum(
                product[head * HD : (head + 1) * HD], axis=0, keepdims=True
            )

    value_move.hand_on()

    def four(arrived, group):
        total = arrived[4 * group].astype(F32)
        for part in range(1, 4):
            total = total + arrived[4 * group + part].astype(F32)
        return total.astype(BF)

    value_back.arrive()
    for group in range(KVH):
        value_grad[:, group * HD : (group + 1) * HD] = four(value_in, group)

    offsets = (4, 3, -3, 2, -2, 1, -1, 0)

    def partial_at(at_core, offset):
        start = (at_core * Z + (z + Z + offset) % Z) * CHUNK
        return jnp.dot(
            turned[rows_at(start, CHUNK)], value_grad[...], preferred_element_type=F32
        ).astype(BF)

    def pair_back(index):
        return remote(
            theirs.at[index],
            from_pair.at[index],
            pair_back_sems.at[0, index],
            pair_back_sems.at[1, index],
            dp,
            other,
        )

    for index, offset in enumerate(offsets):
        theirs[index] = partial_at(1 - core, offset)
        pair_back(index).start()
    for index, offset in enumerate(offsets):
        mine[index] = partial_at(core, offset)

    def spans(part):
        return slice(part * half, (part + 1) * half)

    def up_back(step, part):
        return remote(
            up_out.at[step, spans(part)],
            up_in.at[step, spans(part)],
            ring_back_sems.at[0, step, part],
            ring_back_sems.at[1, step, part],
            above,
            ctx,
        )

    def down_back(step, part):
        return remote(
            down_out.at[step, spans(part)],
            down_in.at[step, spans(part)],
            ring_back_sems.at[2, step, part],
            ring_back_sems.at[3, step, part],
            below,
            ctx,
        )

    def chip_sum(index, part):
        return mine[index, spans(part)].astype(F32) + from_pair[index, spans(part)].astype(F32)

    pair_back(0).wait_recv()
    up_out[0, spans(0)] = chip_sum(0, 0).astype(BF)
    up_back(0, 0).start()
    down_out[0, spans(1)] = chip_sum(0, 1).astype(BF)
    down_back(0, 1).start()

    def ring_back(step):
        pair_back(2 * step - 1).wait_recv()
        pair_back(2 * step).wait_recv()
        if step == 1:
            up_out[1, spans(1)] = chip_sum(1, 1).astype(BF)
            up_back(1, 1).start()
            down_out[1, spans(0)] = chip_sum(2, 0).astype(BF)
            down_back(1, 0).start()
        for index, ring, out, arrived, kept in (
            (2 * step - 1, up_back, up_out, up_in, 0),
            (2 * step, down_back, down_out, down_in, 1),
        ):
            for part in (kept,) if step == 1 else (1 - kept, kept):
                ring(step - 1, part).wait_recv()
                out[step, spans(part)] = (
                    chip_sum(index, part) + arrived[step - 1, spans(part)].astype(F32)
                ).astype(BF)
                ring(step, part).start()

    value_move.arrive()
    backward(0)
    backward(1)
    ring_back(1)
    backward(2)
    backward(3)
    key_rounded[...] = (key_terms[...] * SCALE).astype(BF)
    key_back.start()
    ring_back(2)
    own_rows()
    ring_back(3)
    pair_back(7).wait_recv()
    for part in (0, 1):
        up_back(3, part).wait_recv()
        down_back(3, part).wait_recv()
        mine[7, spans(part)] = (
            chip_sum(7, part)
            + up_in[3, spans(part)].astype(F32)
            + down_in[3, spans(part)].astype(F32)
        ).astype(BF)

    plane = x_lo * 8 + chip

    def plane_back(step):
        to_ctx = (ctx + step) % CTX
        return remote(
            mine.at[7, rows_at(to_ctx * CAP, CAP)],
            plane_in.at[plane],
            plane_back_sems.at[0, step],
            plane_back_sems.at[1, plane],
            core * Z + z,
            to_ctx,
        )

    own_plane = pltpu.make_async_copy(
        mine.at[7, rows_at(ctx * CAP, CAP)], plane_in.at[plane], own_sems.at[3]
    )

    @pl.when(core == x_lo)
    def _():
        own_plane.start()

    @pl.when(core != x_lo)
    def _():
        plane_back(0).start()

    @pl.loop(1, CTX)
    def _(step):
        plane_back(step).start()

    key_back.arrive()
    for group in range(KVH):
        key_grad_ref[:, group * HD : (group + 1) * HD] = four(key_in, group)

    @pl.when(core == x_lo)
    def _():
        own_plane.wait()

    @pl.loop(0, 16)
    def _(source):
        @pl.when(jnp.logical_or(core != x_lo, source != plane))
        def _():
            remote(
                mine.at[7, pl.ds(0, CAP)],
                plane_in.at[source],
                plane_back_sems.at[0, 0],
                plane_back_sems.at[1, source],
                dp,
                other,
            ).wait_recv()

    weight_sum = plane_in[0].astype(F32)
    for source in range(1, 16):
        weight_sum = weight_sum + plane_in[source].astype(F32)
    weight_grad_ref[...] = weight_sum * (1.0 / math.sqrt(32768.0))

    @pl.when(core != x_lo)
    def _():
        plane_copy(0).wait_send()
        plane_back(0).wait_send()

    @pl.loop(1, 16)
    def _(step):
        plane_copy(step).wait_send()
        plane_back(step).wait_send()

    for step in range(3):
        for part in range(2):
            up(step, part, -step).wait_send()
            down(step, part, step).wait_send()
    up(3, 0, -3).wait_send()
    down(3, 1, 3).wait_send()
    for offset in range(-3, 5):
        for part in range(2):
            pair(core, offset, part).wait_send()
    up_back(0, 0).wait_send()
    down_back(0, 1).wait_send()
    for step in range(1, 4):
        for part in range(2):
            up_back(step, part).wait_send()
            down_back(step, part).wait_send()
    for index in range(8):
        pair_back(index).wait_send()
    query_back.arrive()
    for part in (
        key_move,
        query_move,
        grad_move,
        saved_move,
        value_move,
        value_back,
        key_back,
        query_back,
    ):
        part.finish()


def local(
    hidden,
    value_weight,
    queries,
    key_rows,
    attn_saved,
    grad_out,
    doc_lengths,
    routing,
    visible_blocks,
):
    vmem = pl.BlockSpec(memory_space=pltpu.VMEM)
    smem = pl.BlockSpec(memory_space=pltpu.SMEM)
    hbm = pl.BlockSpec(memory_space=pltpu.HBM)
    dma = pltpu.SemaphoreType.DMA
    chunk = (CHUNK, KVW)
    grad_query, grad_key, grad_weight = pl.pallas_call(
        kernel,
        out_shape=(
            jax.ShapeDtypeStruct((ROWS, D), BF),
            jax.ShapeDtypeStruct((ROWS, KVW), BF),
            jax.ShapeDtypeStruct((CAP, KVW), F32),
        ),
        in_specs=[smem, smem, hbm, hbm, hbm, hbm, vmem, hbm, hbm],
        out_specs=(hbm, vmem, vmem),
        scratch_shapes=[
            pltpu.VMEM((ROWS, D), BF),
            pltpu.VMEM((D, ROWS), BF),
            pltpu.VMEM((TOKENS, PAIR), BF),
            pltpu.VMEM((TOKENS, PAIR), BF),
            pltpu.VMEM((TOKENS, PAIR), BF),
            pltpu.VMEM((TOKENS, HD), BF),
            pltpu.VMEM((HD, TOKENS), BF),
            pltpu.VMEM((TOKENS, HD), BF),
            pltpu.VMEM((TOKENS, TOKENS), BF),
            pltpu.VMEM((USED, ROWS), F32),
            pltpu.VMEM((2, TOKENS), F32),
            pltpu.VMEM((D, KVW), BF),
            pltpu.VMEM((ROWS, KVW), BF),
            pltpu.VMEM((CTX * USED, PAIR), BF),
            pltpu.VMEM((TOKENS, HD), F32),
            pltpu.VMEM((TOKENS, HD), F32),
            pltpu.VMEM((TOKENS, HD), BF),
            pltpu.VMEM((TOKENS, HD), BF),
            pltpu.VMEM((TOKENS, PAIR), BF),
            pltpu.VMEM((TOKENS, PAIR), BF),
            pltpu.VMEM((CTX, ROWS, HD), BF),
            pltpu.VMEM((CTX, ROWS, HD), BF),
            pltpu.VMEM((ROWS, KVW), BF),
            pltpu.VMEM((8,) + chunk, BF),
            pltpu.VMEM((8,) + chunk, BF),
            pltpu.VMEM((8,) + chunk, BF),
            pltpu.VMEM((4,) + chunk, BF),
            pltpu.VMEM((4,) + chunk, BF),
            pltpu.VMEM((4,) + chunk, BF),
            pltpu.VMEM((4,) + chunk, BF),
            pltpu.VMEM((16, CAP, KVW), BF),
            dma,
            dma((12,)),
            dma((2, 16)),
            dma((4, 4, 2)),
            dma((2, 8, 2)),
            dma((8, 2, CTX)),
            dma((2, 2, 8)),
            dma((2, 8)),
            dma((4, 4, 2)),
            dma((2, 16)),
        ],
        compiler_params=pltpu.CompilerParams(
            has_side_effects=True, vmem_limit_bytes=60 * 1024 * 1024, collective_id=0
        ),
        name="attention_backward",
    )(
        doc_lengths,
        visible_blocks[0],
        value_weight,
        hidden[0],
        key_rows[0],
        attn_saved[0],
        routing.reshape(CTX, ROWS),
        queries[0],
        grad_out[0],
    )
    return (grad_query[None], grad_key[None], grad_weight)


def solution(mesh):
    return jax.shard_map(
        local,
        mesh=mesh,
        in_specs=(
            P("dp", "ctx", None),
            P(("dp", "ctx"), None),
            P("dp", "ctx", None),
            P("dp", "ctx", None),
            P("dp", "ctx", None),
            P("dp", "ctx", None),
            P("dp", None),
            P("dp", None),
            P("dp", None, None),
        ),
        out_specs=(P("dp", "ctx", None), P("dp", "ctx", None), P(("dp", "ctx"), None)),
        check_vma=False,
    )
```
